32 devices in a mesh: dp: 8 (over z, y), mp: 4 (over x, core).
Axes of the slice: x: 2, y: 2, z: 4, core: 2. Of those that a mesh axis runs over, the one named last changes fastest.
Arguments:
- hidden_in: bfloat16 [32768, 768], P('dp'), may hold values from -6 to 6
- incoming: bfloat16 [32768, 768], P('dp'), may hold values from -6 to 6
- spans: int32 [64, 24, 2], P('dp'), may hold values from 0 to 508, as said below
- owners: int32 [12], replicated, may hold values from 0 to 7, as said below
- vectors: float32 [12, 768], replicated, may hold values from -2 to 2
- vec_one: float32 [12, 768], replicated, may hold values from -144.81548 to 144.81548
- vec_two: float32 [12, 768], replicated, may hold values from 1310.72 to 5242.88
- master_slots: float32 [32, 768, 768], P('dp', None, 'mp'), may hold values from -0.9021098 to 0.9021098
- slot_one: float32 [32, 768, 768], P('dp', None, 'mp'), may hold values from -144.81548 to 144.81548
- slot_two: float32 [32, 768, 768], P('dp', None, 'mp'), may hold values from 1310.72 to 5242.88
Outputs:
- layer_out: bfloat16 [32768, 768], P('dp')
- input_grad: bfloat16 [32768, 768], P('dp')
- new_vectors: float32 [12, 768], replicated
- new_vec_one: float32 [12, 768], replicated
- new_vec_two: float32 [12, 768], replicated
- new_slots: float32 [32, 768, 768], P('dp', None, 'mp')
- new_slot_one: float32 [32, 768, 768], P('dp', None, 'mp')
- new_slot_two: float32 [32, 768, 768], P('dp', None, 'mp')
The draws below stay inside these ranges and needn't reach their ends.
Inputs may be any that keep to these rules, and one draw needn't show every extreme that they name: Each span lies within its sequence: length 1 to 4, start + length <= 512; spans may intersect. `owners`: no index of dp owns more than 4 pieces; one owns exactly 4.
All inputs are finite; a program needn't handle non-finite values.
Results may differ from the reference program's by a relative error of at most 0.02.
Values may be sent and summed in bfloat16 or wider, within the bound.
A program may use at most 384 MiB of HBM per device.

```python
import math
import jax
import jax.numpy as jnp
import numpy as np
from jax import lax

D = 768
HEADS = 12
HDIM = 64
FF = 3072
LEN = 512
NSPAN = 24
SPANMAX = 4
CAP = 4
STEP = 10
NMAT = 12
VROWS = 12
SEQS = 64
TOKENS = 32768
SLOTS = 32
N_DP = 8
N_MP = 4


def split_table(total, parts, most):
    found = []

    def extend(prefix, left):
        if len(prefix) == parts - 1:
            if 1 <= left <= most:
                found.append(prefix + [left])
            return
        for amount in range(1, most + 1):
            extend(prefix + [amount], left - amount)
    extend([], total)
    return np.array(found, dtype=np.int32)


def owner_list(key):
    key = jax.random.fold_in(key, 5)
    k_mid, k_table, k_order, k_pieces = jax.random.split(key, 4)
    middle = jax.random.permutation(k_mid, N_DP - 2)[:CAP - 1].astype(jnp.int32) + 1
    devices = jnp.concatenate([jnp.array([0, N_DP - 1], jnp.int32), middle])
    devices = jax.random.permutation(k_order, devices)
    table = jnp.asarray(split_table(NMAT - CAP, CAP, CAP))
    counts = table[jax.random.randint(k_table, (), 0, table.shape[0])]
    ends = jnp.cumsum(counts)
    rest = jnp.arange(NMAT - CAP, dtype=jnp.int32)
    group = jnp.sum((ends[None, :] <= rest[:, None]).astype(jnp.int32), axis=1)
    ordered = jnp.concatenate([jnp.full((CAP,), devices[0], jnp.int32), devices[1 + group]])
    return jax.random.permutation(k_pieces, ordered).astype(jnp.int32)


def draw_owners(key, part):
    shared = owner_list(key)
    return shared


def draw_master_slots(key, part):
    shared = owner_list(key)
    key = jax.random.fold_in(key, 19)
    index = jnp.arange(NMAT, dtype=jnp.int32)
    earlier = index[None, :] < index[:, None]
    same = shared[:, None] == shared[None, :]
    slot_of = jnp.sum((same & earlier).astype(jnp.int32), axis=1)
    target = shared * CAP + slot_of
    wide = (jnp.arange(N_DP * CAP, dtype=jnp.int32) == target[3]).astype(jnp.float32)
    scale = (1.0 + 4.0 * wide) * D ** (-0.5)
    noise = jnp.clip(jax.random.normal(key, (N_DP * CAP, D, D), jnp.float32), -5.0, 5.0)
    return noise * scale[:, None, None]


def draw_spans(key, part):
    key = jax.random.fold_in(key, 11)
    k_start, k_length = jax.random.split(key)
    starts = jax.random.randint(k_start, (SEQS, NSPAN), 0, LEN - SPANMAX + 1)
    lengths = jax.random.randint(k_length, (SEQS, NSPAN), 1, SPANMAX + 1)
    starts = starts.at[0, 0].set(LEN - SPANMAX).at[0, 1].set(0)
    lengths = lengths.at[0, 0].set(SPANMAX)
    return jnp.stack([starts, lengths], axis=-1).astype(jnp.int32)


def draw_vectors(key, part):
    key = jax.random.fold_in(key, 17)
    ratio = FF // D
    rows = jnp.arange(8 + ratio)
    gains = ((rows == 4 + ratio) | (rows == 6 + ratio)).astype(jnp.float32)[:, None]
    noise = jnp.clip(0.35 * jax.random.normal(key, (8 + ratio, D), jnp.float32), -1.2, 1.2)
    return gains * (1.0 + 0.5 * noise) + (1.0 - gains) * noise


def block_levels(own_key, shape, cuts, low, high):
    def one(axis_at, shards_of):
        steps = jax.random.uniform(jax.random.fold_in(jax.random.fold_in(own_key, 6), axis_at), (shards_of,), jnp.float32, low / len(cuts), high / len(cuts))
        return jnp.repeat(jnp.exp(steps), shape[axis_at] // shards_of).reshape((-1,) + (1,) * (len(shape) - axis_at - 1))

    level = one(*cuts[0])
    for cut in cuts[1:]:
        level = level * one(*cut)
    return level


def centred(own_key, shape, scale, limit, shards=(), held_as=jnp.bfloat16):
    level = block_levels(own_key, shape, shards, -0.22, 0.18) if shards else 1.0
    result = jax.random.normal(own_key, shape, jnp.float32) * scale * level
    return jnp.minimum(jnp.maximum(result, -limit), limit).astype(held_as)


def setup_inputs(seed: int = 0) -> dict:
    seeds = jax.random.split(jax.random.key(seed), 11)
    hidden_in = centred(seeds[0], (TOKENS, D), 1.0, 6.0, ((0, 8),))
    incoming = centred(seeds[1], (TOKENS, D), 1.0, 6.0, ((0, 8),))
    spans = draw_spans(jax.random.fold_in(seeds[10], 71), 0)
    owners = draw_owners(jax.random.fold_in(seeds[10], 71), 0)
    vectors = draw_vectors(jax.random.fold_in(seeds[10], 71), 0)
    vec_one = centred(seeds[5], (VROWS, D), ((0.04 * TOKENS) ** 0.5), 144.81548, (), jnp.float32)
    vec_two = jnp.clip(jnp.exp(jax.random.uniform(seeds[6], (VROWS, D), jnp.float32, math.log(1310.72), math.log(5242.88))), 1310.72, 5242.88)
    master_slots = draw_master_slots(jax.random.fold_in(seeds[10], 71), 0)
    slot_one = centred(seeds[8], (SLOTS, D, D), ((0.04 * TOKENS) ** 0.5), 144.81548, ((0, 8), (2, 4)), jnp.float32)
    slot_two = jnp.clip(jnp.exp(math.log(5242.88) - 1.3862944 * jax.random.uniform(seeds[9], (SLOTS, D, D), jnp.float32) ** block_levels(seeds[9], (SLOTS, D, D), ((0, 8), (2, 4)), -0.2, 0.2)), 1310.72, 5242.88)
    return {"hidden_in": hidden_in, "incoming": incoming, "spans": spans, "owners": owners, "vectors": vectors, "vec_one": vec_one, "vec_two": vec_two, "master_slots": master_slots, "slot_one": slot_one, "slot_two": slot_two}


HI = lax.Precision.HIGHEST
LN_EPS = 1e-12
MATRIX_RATE = 0.03
VECTOR_RATE = 0.25
BETA_ONE = 0.5
BETA_TWO = 0.5
DECAY = 0.01
ADAM_EPS = 1e-08

@jax.custom_vjp
def low(v):
    return lax.optimization_barrier(v.astype(jnp.bfloat16)).astype(jnp.float32)

@jax.custom_vjp
def low_back(v):
    return v

def low_keep(v):
    return (low(v), None)

def low_pass(kept, grad):
    return (grad,)

def back_keep(v):
    return (v, None)

def back_low(kept, grad):
    return (low(grad),)
low.defvjp(low_keep, low_pass)
low_back.defvjp(back_keep, back_low)

def rounded(value):
    return low_back(low(value))

def matmul(left, right):
    return jnp.dot(left, right, precision=HI)

def layer_norm(value, gain, shift):
    center = value - lax.optimization_barrier(jnp.mean(value, axis=-1, keepdims=True))
    scale = lax.rsqrt(lax.optimization_barrier(jnp.mean(center * center, axis=-1, keepdims=True)) + LN_EPS)
    return center * scale * gain + shift

def expand(stack, width, ratio):
    return stack.reshape(ratio, width, N_MP, width // N_MP).transpose(1, 2, 0, 3).reshape(width, ratio * width)

def forward(hidden, pieces, vectors):
    ratio = FF // D
    weights = low(pieces)
    w_query, w_key, w_value = (weights[0], weights[1], weights[2])
    w_out = weights[3].T
    w_up = expand(weights[4:4 + ratio], D, ratio)
    w_down = expand(weights[4 + ratio:4 + 2 * ratio], D, ratio).T
    b_query, b_value, b_out = (vectors[0], vectors[1], vectors[2])
    b_up = vectors[3:3 + ratio].reshape(FF)
    b_down = vectors[3 + ratio]
    gain_one, shift_one = (vectors[4 + ratio], vectors[5 + ratio])
    gain_two, shift_two = (vectors[6 + ratio], vectors[7 + ratio])
    nseq = hidden.shape[0] // LEN
    query = rounded(matmul(hidden, w_query) + b_query)
    keys = rounded(matmul(hidden, w_key))
    values = rounded(matmul(hidden, w_value) + b_value)

    def attend(block):
        q_blk, k_blk, v_blk = block
        scores = low_back(jnp.einsum('qhd,khd->hqk', q_blk, k_blk, precision=HI) * HDIM ** (-0.5))
        probs = jax.nn.softmax(scores, axis=-1)
        return jnp.einsum('hqk,khd->qhd', low(probs), v_blk, precision=HI)
    shape = (nseq, LEN, HEADS, HDIM)
    context = lax.map(jax.checkpoint(attend), (query.reshape(shape), keys.reshape(shape), values.reshape(shape)))
    context = rounded(context.reshape(-1, D))
    attn = low_back(matmul(context, w_out) + b_out)
    first = layer_norm(hidden + attn, gain_one, shift_one)
    upper = low_back(matmul(low(first), w_up) + b_up)
    active = jax.nn.gelu(upper, approximate=False)
    down = low_back(matmul(low(active), w_down) + b_down)
    return layer_norm(first + down, gain_two, shift_two)

def adamw(weight, moment_one, moment_two, grad, step_rate):
    new_one = BETA_ONE * moment_one + (1.0 - BETA_ONE) * grad
    new_two = BETA_TWO * moment_two + (1.0 - BETA_TWO) * grad * grad
    corr_one = 1.0 - BETA_ONE ** STEP
    corr_two = 1.0 - BETA_TWO ** STEP
    direction = new_one / corr_one / (jnp.sqrt(new_two / corr_two) + ADAM_EPS)
    return (weight - step_rate * (direction + DECAY * weight), new_one, new_two)

def reference(hidden_in, incoming, spans, owners, vectors, vec_one, vec_two, master_slots, slot_one, slot_two):
    nmat = owners.shape[0]
    index = jnp.arange(nmat, dtype=jnp.int32)
    earlier = index[None, :] < index[:, None]
    same = owners[:, None] == owners[None, :]
    slot_of = lax.optimization_barrier(jnp.sum((same & earlier).astype(jnp.int32), axis=1))
    target = owners * CAP + slot_of
    pick = (jnp.arange(N_DP * CAP, dtype=jnp.int32)[:, None] == target[None, :]).astype(jnp.float32)
    pieces = jnp.einsum('rp,rij->pij', pick, master_slots, precision=HI)
    hidden = hidden_in.astype(jnp.float32)
    position = jnp.arange(LEN, dtype=jnp.int32)
    starts = spans[:, :, 0][:, :, None]
    ends = starts + spans[:, :, 1][:, :, None]
    covered = jnp.any((position[None, None, :] >= starts) & (position[None, None, :] < ends), axis=1)
    mask = covered.reshape(-1).astype(jnp.float32)
    cotangent = incoming.astype(jnp.float32) * mask[:, None]
    layer, pull = jax.vjp(forward, hidden, pieces, vectors)
    grad_hidden, grad_pieces, grad_vectors = pull(cotangent)
    new_vectors, new_vec_one, new_vec_two = adamw(vectors, vec_one, vec_two, grad_vectors, VECTOR_RATE)
    slot_grad = jnp.einsum('rp,pij->rij', pick, grad_pieces, precision=HI)
    occupied = lax.optimization_barrier(jnp.sum(pick, axis=1))[:, None, None]
    new_slots, new_slot_one, new_slot_two = adamw(master_slots, slot_one, slot_two, slot_grad, MATRIX_RATE)
    return (layer.astype(jnp.bfloat16), grad_hidden.astype(jnp.bfloat16), new_vectors, new_vec_one, new_vec_two, new_slots * occupied, new_slot_one * occupied, new_slot_two * occupied)
```

```python
import functools
import jax
import jax.numpy as jnp
from jax import lax
from jax.sharding import PartitionSpec as P
from jax.experimental import pallas as pl
from jax.experimental.pallas import tpu as pltpu

MESH = pl.DeviceIdType.MESH


def place():
    dp, mp = lax.axis_index("dp"), lax.axis_index("mp")
    return dp // 2, dp % 2, mp // 2, mp % 2


def device(z, y, x, c):
    return (z * 2 + y, x * 2 + c)


def greet(line):
    z, y, x, c = place()
    bar = pltpu.get_barrier_semaphore()
    for who in (device(z, 1 - y, x, c), device(z, y, 1 - x, c), device(z, y, x, 1 - c)):
        pl.semaphore_signal(bar, inc=1, device_id=who, device_id_type=MESH)

    @pl.when(z > 0)
    def _():
        pl.semaphore_signal(bar, inc=1, device_id=device(z - 1, y, x, c), device_id_type=MESH)

    @pl.when(z < line - 1)
    def _():
        pl.semaphore_signal(bar, inc=1, device_id=device(z + 1, y, x, c), device_id_type=MESH)

    peers = 3 + jnp.where(z > 0, 1, 0) + jnp.where(z < line - 1, 1, 0)
    pl.semaphore_wait(bar, peers.astype(jnp.int32))


def rcopy(src, dst, send, recv, who):
    return pltpu.make_async_remote_copy(
        src_ref=src, dst_ref=dst, send_sem=send, recv_sem=recv, device_id=who, device_id_type=MESH
    )


def gather_kernel(line, nmat, cap, owners, slots, out, full, ys, fr, fl, zo, idx, slot_sem,
                  sr, rl, sl, rr, xs, xr, ysd, yr, ds, dr, cs, cr, loc):
    share = slots.shape[1]
    quarter = share // 2
    half = quarter // 2
    nchunk = 2 * nmat
    z, y, x, c = place()
    me = 2 * x + c
    over = 2 * (1 - x) + c
    to_y, to_x, to_c = device(z, 1 - y, x, c), device(z, y, 1 - x, c), device(z, y, x, 1 - c)
    greet(line)
    slot_copy = rcopy(
        slots.at[:, pl.ds(pl.multiple_of((1 - y) * quarter, 16), quarter), :],
        ys.at[pl.ds(y * cap, cap)], slot_sem.at[0], slot_sem.at[1], to_y)
    slot_copy.start()
    for p in range(nmat):
        mine = owners[p]
        place_of = jnp.int32(0)
        for q in range(p):
            place_of += jnp.where(owners[q] == mine, 1, 0).astype(jnp.int32)
        zo[p] = mine // 2
        idx[p] = (mine % 2) * cap + jnp.minimum(place_of, cap - 1)
    ys[pl.ds(y * cap, cap)] = slots[:, pl.ds(pl.multiple_of(y * quarter, 16), quarter), :]
    slot_copy.wait()

    def rows(block, yy, h):
        return pl.ds(pl.multiple_of(block * share + yy * quarter + h * half, 16), half)

    def own(r):
        return ys[idx[r // 2], pl.ds(pl.multiple_of((r % 2) * half, 16), half), :]

    def right(r):
        return rcopy(fr.at[r], fr.at[r], sr.at[r], rl.at[r], device(z + 1, y, x, c))

    def left(r):
        return rcopy(fl.at[r], fl.at[r], sl.at[r], rr.at[r], device(z - 1, y, x, c))

    def x_copy(f):
        at = full.at[f // 2, rows(me, y, f % 2), :]
        return rcopy(at, at, xs.at[f], xr.at[f], to_x)

    def x_came(f):
        at = full.at[f // 2, rows(over, y, f % 2), :]
        return rcopy(at, at, xs.at[f], xr.at[f], to_x)

    def y_copy(f):
        at = full.at[f // 2, rows(me, y, f % 2), :]
        return rcopy(at, at, ysd.at[f], yr.at[f], to_y)

    def y_came(f):
        at = full.at[f // 2, rows(me, 1 - y, f % 2), :]
        return rcopy(at, at, ysd.at[f], yr.at[f], to_y)

    def diag_x(f):
        at = full.at[f // 2, rows(me, 1 - y, f % 2), :]
        return rcopy(at, at, ds.at[f], dr.at[f], to_x)

    def diag_y(f):
        at = full.at[f // 2, rows(over, y, f % 2), :]
        return rcopy(at, at, ds.at[f], dr.at[f], to_y)

    def diag_came(f):
        at = full.at[f // 2, rows(over, 1 - y, f % 2), :]
        return rcopy(at, at, ds.at[f], dr.at[f], to_x)

    def core_copy(p, k):
        block = jnp.where(k == 0, me, over) if not isinstance(k, int) else (me, over)[k]
        at = full.at[p, pl.ds(pl.multiple_of(block * share, 16), share), :]
        return rcopy(at, at, cs.at[p, k], cr.at[p, k], to_c)

    def core_came(p, k):
        block = (2 * x + 1 - c, 2 * (1 - x) + 1 - c)[k]
        at = full.at[p, pl.ds(pl.multiple_of(block * share, 16), share), :]
        return rcopy(at, at, cs.at[p, k], cr.at[p, k], to_c)

    def keep(p):
        return pltpu.make_async_copy(full.at[p], out.at[p], loc.at[p])

    lag0 = 2 * (line - 1)
    lag1 = lag0 + 2
    lag2 = lag1 + 3
    lag3 = lag2 + 1

    def tick(t):
        r = t - 2 * z

        @pl.when((r >= 0) & (r < nchunk))
        def _():
            @pl.when(z == 0)
            def _():
                fr[r] = own(r)

            @pl.when(z > 0)
            def _():
                right(r).wait_recv()
                fr[r] = jnp.where(zo[r // 2] == z, own(r), fr[r])

            @pl.when(z < line - 1)
            def _():
                right(r).start()

        l = t - 2 * (line - 1 - z)

        @pl.when((l >= 0) & (l < nchunk))
        def _():
            @pl.when(z == line - 1)
            def _():
                fl[l] = own(l)

            @pl.when(z < line - 1)
            def _():
                left(l).wait_recv()
                fl[l] = jnp.where(zo[l // 2] == z, own(l), fl[l])

            @pl.when(z > 0)
            def _():
                left(l).start()

        f = t - lag0

        @pl.when((f >= 0) & (f < nchunk))
        def _():
            full[f // 2, rows(me, y, f % 2), :] = jnp.where(zo[f // 2] <= z, fr[f], fl[f])
            x_copy(f).start()
            y_copy(f).start()

        g = t - lag1

        @pl.when((g >= 0) & (g < nchunk))
        def _():
            x_came(g).wait_recv()
            y_came(g).wait_recv()

            @pl.when(g % 2 == 0)
            def _():
                diag_x(g).start()

            @pl.when(g % 2 == 1)
            def _():
                diag_y(g).start()

        e = t - lag2

        @pl.when((e >= 0) & (e < nchunk))
        def _():
            diag_came(e).wait_recv()

            @pl.when(e % 2 == 1)
            def _():
                for k in range(2):
                    core_copy(e // 2, k).start()

        w = t - lag3

        @pl.when((w >= 0) & (w < nchunk) & (w % 2 == 1))
        def _():
            for k in range(2):
                core_came(w // 2, k).wait_recv()
            keep(w // 2).start()

    def body(t, carry):
        tick(t)
        return carry

    lax.fori_loop(0, nchunk + lag3, body, 0)

    def finish(r, carry):
        @pl.when(z < line - 1)
        def _():
            right(r).wait_send()

        @pl.when(z > 0)
        def _():
            left(r).wait_send()

        x_copy(r).wait_send()
        y_copy(r).wait_send()
        diag_came(r).wait_send()
        return carry

    lax.fori_loop(0, nchunk, finish, 0)

    def last(p, carry):
        for k in range(2):
            core_copy(p, k).wait_send()
        keep(p).wait()
        return carry

    lax.fori_loop(0, nmat, last, 0)


def gather_weights(owners, slots, line):
    cap, share, width = slots.shape
    nmat = owners.shape[0]
    quarter, half = share // 2, share // 4
    n = 2 * nmat
    bf16 = jnp.bfloat16
    dma = pltpu.SemaphoreType.DMA
    return pl.pallas_call(
        functools.partial(gather_kernel, line, nmat, cap),
        out_shape=jax.ShapeDtypeStruct((nmat, 4 * share, width), bf16),
        in_specs=[pl.BlockSpec(memory_space=pltpu.SMEM), pl.BlockSpec(memory_space=pltpu.VMEM)],
        out_specs=pl.BlockSpec(memory_space=pl.ANY),
        scratch_shapes=[
            pltpu.VMEM((nmat, 4 * share, width), bf16),
            pltpu.VMEM((2 * cap, quarter, width), bf16),
            pltpu.VMEM((n, half, width), bf16),
            pltpu.VMEM((n, half, width), bf16),
            pltpu.SMEM((nmat,), jnp.int32),
            pltpu.SMEM((nmat,), jnp.int32),
            dma((2,)),
        ] + [dma((n,))] * 10 + [dma((nmat, 2)), dma((nmat, 2)), dma((nmat,))],
        name="gather_weights",
        compiler_params=pltpu.CompilerParams(
            collective_id=1, has_side_effects=True, vmem_limit_bytes=56 * 1024 * 1024),
    )(owners, slots)


def reduce_kernel(line, order, cap, owners, grads, out, cin, hold, yo, yi, fr, fl, to, do, di,
                  who, pick, cs, cr, ysd, yr, sr, rl, sl, rr, dsem):
    nmat = len(order)
    share = grads.shape[1] // 2
    quarter = share // 2
    f32, bf16 = jnp.float32, jnp.bfloat16
    z, y, x, c = place()
    to_y, to_c = device(z, 1 - y, x, c), device(z, y, x, 1 - c)
    greet(line)

    for s in range(2 * cap):
        pick[s] = 0
    for j, p in enumerate(order):
        mine = owners[p]
        place_of = jnp.int32(0)
        for q in range(p):
            place_of += jnp.where(owners[q] == mine, 1, 0).astype(jnp.int32)
        who[j] = mine // 2
        slot = (mine % 2) * cap + jnp.minimum(place_of, cap - 1)
        for s in range(2 * cap):
            pick[s] = jnp.where((mine // 2 == z) & (slot == s), j, pick[s])

    def rows(start, size):
        return pl.ds(pl.multiple_of(start, 16), size)

    def core_copy(j):
        return rcopy(grads.at[j, rows((1 - c) * share, share), :], cin.at[j], cs.at[j], cr.at[j], to_c)

    def y_copy(j):
        return rcopy(yo.at[j], yi.at[j], ysd.at[j], yr.at[j], to_y)

    def right(j):
        return rcopy(to.at[0, j], fr.at[j], sr.at[j], rl.at[j], device(z + 1, y, x, c))

    def left(j):
        return rcopy(to.at[1, j], fl.at[j], sl.at[j], rr.at[j], device(z - 1, y, x, c))

    def stage0(j):
        core_copy(j).start()

    def stage1(j):
        core_copy(j).wait_recv()
        for part in range(2):
            at = y if part == 0 else 1 - y
            total = (grads[j, rows(c * share + at * quarter, quarter), :].astype(f32)
                     + cin[j, rows(at * quarter, quarter), :].astype(f32))
            if part == 0:
                hold[j] = total
            else:
                yo[j] = total.astype(bf16)
        y_copy(j).start()

    def stage2(j):
        y_copy(j).wait_recv()
        hold[j] = hold[j] + yi[j].astype(f32)

    def flow_right(j):
        @pl.when(z == 0)
        def _():
            to[0, j] = hold[j].astype(bf16)

        @pl.when(z > 0)
        def _():
            right(j).wait_recv()
            to[0, j] = (hold[j] + fr[j].astype(f32)).astype(bf16)

        @pl.when(z < line - 1)
        def _():
            right(j).start()

    def flow_left(j):
        @pl.when(z == line - 1)
        def _():
            to[1, j] = hold[j].astype(bf16)

        @pl.when(z < line - 1)
        def _():
            left(j).wait_recv()
            to[1, j] = (hold[j] + fl[j].astype(f32)).astype(bf16)

        @pl.when(z > 0)
        def _():
            left(j).start()

    def total(j):
        value = hold[j]
        value = value + jnp.where(z > 0, fr[j].astype(f32), 0.0)
        return value + jnp.where(z < line - 1, fl[j].astype(f32), 0.0)

    def ranged(j, do_it):
        pl.when((j >= 0) & (j < nmat))(functools.partial(do_it, j))

    def tick(t):
        ranged(t, stage0)
        ranged(t - 1, stage1)
        ranged(t - 3, stage2)
        ranged(t - 4 - 2 * z, flow_right)
        ranged(t - 4 - 2 * (line - 1 - z), flow_left)

    def body(t, carry):
        tick(t)
        return carry

    lax.fori_loop(0, nmat + 4 + 2 * (line - 1), body, 0)

    for s in range(cap):
        do[s] = total(pick[(1 - y) * cap + s]).astype(bf16)
    deliver = rcopy(do, di, dsem.at[0], dsem.at[1], to_y)
    deliver.start()
    for s in range(cap):
        out[s, rows(y * quarter, quarter), :] = total(pick[y * cap + s])
    deliver.wait_recv()
    for s in range(cap):
        out[s, rows((1 - y) * quarter, quarter), :] = di[s].astype(f32)
    deliver.wait_send()

    def finish(j, carry):
        core_copy(j).wait_send()
        y_copy(j).wait_send()

        @pl.when(z < line - 1)
        def _():
            right(j).wait_send()

        @pl.when(z > 0)
        def _():
            left(j).wait_send()

        return carry

    lax.fori_loop(0, nmat, finish, 0)


def reduce_grads(owners, grads, line, order, cap):
    nmat, both, width = grads.shape
    share = both // 2
    quarter = share // 2
    bf16, f32 = jnp.bfloat16, jnp.float32
    dma = pltpu.SemaphoreType.DMA
    return pl.pallas_call(
        functools.partial(reduce_kernel, line, order, cap),
        out_shape=jax.ShapeDtypeStruct((cap, share, width), f32),
        in_specs=[pl.BlockSpec(memory_space=pltpu.SMEM), pl.BlockSpec(memory_space=pltpu.VMEM)],
        out_specs=pl.BlockSpec(memory_space=pltpu.VMEM),
        scratch_shapes=[
            pltpu.VMEM((nmat, share, width), bf16),
            pltpu.VMEM((nmat, quarter, width), f32),
            pltpu.VMEM((nmat, quarter, width), bf16),
            pltpu.VMEM((nmat, quarter, width), bf16),
            pltpu.VMEM((nmat, quarter, width), bf16),
            pltpu.VMEM((nmat, quarter, width), bf16),
            pltpu.VMEM((2, nmat, quarter, width), bf16),
            pltpu.VMEM((cap, quarter, width), bf16),
            pltpu.VMEM((cap, quarter, width), bf16),
            pltpu.SMEM((nmat,), jnp.int32),
            pltpu.SMEM((2 * cap,), jnp.int32),
        ] + [dma((nmat,))] * 8 + [dma((2,))],
        name="reduce_grads",
        compiler_params=pltpu.CompilerParams(
            collective_id=2, has_side_effects=True, vmem_limit_bytes=56 * 1024 * 1024),
    )(owners, grads)
HDIM = 64
LEN = 512
STEP = 10
SPAN_ROWS = 96
LN_EPS = 1e-12
MATRIX_RATE = 0.03
VECTOR_RATE = 0.25
BETA_ONE = 0.5
BETA_TWO = 0.5
DECAY = 0.01
ADAM_EPS = 1e-08
BF16 = jnp.bfloat16
F32 = jnp.float32


def layer_norm(value, gain, shift):
    center = value - jnp.mean(value, axis=-1, keepdims=True)
    inverse = lax.rsqrt(jnp.mean(center * center, axis=-1, keepdims=True) + LN_EPS)
    normed = center * inverse
    return (normed * gain + shift, normed, inverse)


def norm_back(grad, normed, inverse, gain):
    scaled = grad * gain
    first = jnp.mean(scaled, axis=-1, keepdims=True)
    second = jnp.mean(scaled * normed, axis=-1, keepdims=True)
    return inverse * (scaled - first - normed * second)


def gelu_slope(value):
    cdf = 0.5 * (1.0 + lax.erf(value * 2.0 ** (-0.5)))
    pdf = jnp.exp(-0.5 * value * value) * (2.0 * jnp.pi) ** (-0.5)
    return cdf + value * pdf


def adamw(weight, moment_one, moment_two, grad, step_rate):
    new_one = BETA_ONE * moment_one + (1.0 - BETA_ONE) * grad
    new_two = BETA_TWO * moment_two + (1.0 - BETA_TWO) * grad * grad
    corr_one = 1.0 - BETA_ONE**STEP
    corr_two = 1.0 - BETA_TWO**STEP
    direction = new_one / corr_one / (jnp.sqrt(new_two / corr_two) + ADAM_EPS)
    return (weight - step_rate * (direction + DECAY * weight), new_one, new_two)


def dot(eq, a, b):
    return jnp.einsum(eq, a, b, preferred_element_type=F32)


def on_device(line, hidden_in, incoming, spans, owners, vectors, vec_one, vec_two, master_slots, slot_one, slot_two):
    cap, width, share = master_slots.shape
    nmat = owners.shape[0]
    ratio = (nmat - 4) // 2
    scale = HDIM ** (-0.5)
    heads = width // HDIM
    rank_mp = lax.axis_index("mp")
    rx, rc = rank_mp // 2, rank_mp % 2
    tokens = hidden_in.shape[0]
    own = tokens // 4
    nseq = own // LEN
    pieces = gather_weights(owners, jnp.transpose(master_slots, (0, 2, 1)).astype(BF16), line)
    wq, wk, wv, wo = pieces[0], pieces[1], pieces[2], pieces[3]
    b_up = vectors[3:3 + ratio].reshape(4, ratio, share).transpose(1, 0, 2).reshape(ratio, width)
    b_q, b_v, b_o, b_down = vectors[0], vectors[1], vectors[2], vectors[3 + ratio]
    gain_one, shift_one, gain_two, shift_two = (vectors[4 + ratio + i] for i in range(4))

    def split(v):
        return v.reshape(-1, LEN, heads, HDIM)

    def attend(block):
        q_blk, k_blk, v_blk = block
        scores = dot("qhd,khd->hqk", q_blk, k_blk) * scale
        probs = jax.nn.softmax(scores, axis=-1)
        return dot("hqk,khd->qhd", probs.astype(BF16), v_blk).astype(BF16)

    mine = lax.dynamic_slice_in_dim(hidden_in, rank_mp * own, own, 0)
    q = (dot("td,sd->ts", mine, wq) + b_q).astype(BF16)
    k = dot("td,sd->ts", mine, wk).astype(BF16)
    v = (dot("td,sd->ts", mine, wv) + b_v).astype(BF16)
    ctx = lax.map(attend, (split(q), split(k), split(v))).reshape(own, width)
    first, _, _ = layer_norm(mine.astype(F32) + dot("ts,so->to", ctx, wo) + b_o, gain_one, shift_one)
    low = first.astype(BF16)
    second = first + b_down
    for i in range(ratio):
        act = jax.nn.gelu(dot("td,fd->tf", low, pieces[4 + i]) + b_up[i], approximate=False).astype(BF16)
        second = second + dot("tf,fo->to", act, pieces[4 + ratio + i])
    layer = layer_norm(second, gain_two, shift_two)[0].astype(BF16)
    layer = lax.all_gather(layer, "mp", axis=0, tiled=True)

    def ours(v):
        v = v.reshape((2, 2, v.shape[0] // 4) + v.shape[1:])
        v = lax.dynamic_index_in_dim(v, rc, 1, keepdims=False)
        return v.reshape((-1,) + v.shape[2:])
    hid = ours(hidden_in)
    inc = ours(incoming)
    spn = ours(spans)
    position = jnp.arange(LEN, dtype=jnp.int32)
    starts = spn[:, :, 0][:, :, None]
    ends = starts + spn[:, :, 1][:, :, None]
    covered = jnp.any((position >= starts) & (position < ends), axis=1)
    rank = jnp.cumsum(covered.astype(jnp.int32), axis=1) - 1
    pick = ((rank[:, None, :] == jnp.arange(SPAN_ROWS)[None, :, None]) & covered[:, None, :]).astype(BF16)
    hid_s = hid.reshape(-1, LEN, width)
    ns = hid_s.shape[0]
    hm = dot("sit,std->sid", pick, hid_s).astype(BF16).reshape(-1, width)
    gm = dot("sit,std->sid", pick, inc.reshape(-1, LEN, width)).reshape(-1, width)
    q = (dot("td,sd->ts", hm, wq) + b_q).astype(BF16)
    k = dot("td,sd->ts", hid, wk).astype(BF16)
    v = (dot("td,sd->ts", hid, wv) + b_v).astype(BF16)
    q_s, k_s, v_s = q.reshape(ns, SPAN_ROWS, heads, HDIM), split(k), split(v)
    probs = jax.nn.softmax(dot("sqhd,skhd->shqk", q_s, k_s) * scale, axis=-1)
    pr = probs.astype(BF16)
    ctx = dot("shqk,skhd->sqhd", pr, v_s).astype(BF16).reshape(-1, width)
    y1, n1, i1 = layer_norm(hm.astype(F32) + dot("ts,so->to", ctx, wo) + b_o, gain_one, shift_one)
    low = y1.astype(BF16)
    second = y1 + b_down
    acts, ups = [], []
    for i in range(ratio):
        up = dot("td,fd->tf", low, pieces[4 + i]) + b_up[i]
        act = jax.nn.gelu(up, approximate=False).astype(BF16)
        second = second + dot("tf,fo->to", act, pieces[4 + ratio + i])
        ups.append(up)
        acts.append(act)
    _, n2, i2 = layer_norm(second, gain_two, shift_two)
    grad_g2 = jnp.sum(gm * n2, axis=0)
    grad_e2 = jnp.sum(gm, axis=0)
    dh2 = norm_back(gm, n2, i2, gain_two)
    df = dh2.astype(BF16)
    grad_b2 = jnp.sum(df.astype(F32), axis=0)

    def half(v):
        return lax.dynamic_slice_in_dim(v, rx * 2 * share, 2 * share, 1)
    grads = [None] * nmat
    dy1 = dh2
    b_rows = []
    for i in range(ratio):
        du = (dot("to,fo->tf", df, pieces[4 + ratio + i]) * gelu_slope(ups[i])).astype(BF16)
        dy1 = dy1 + dot("tf,fd->td", du, pieces[4 + i])
        b_rows.append(jnp.sum(du.astype(F32), axis=0))
        grads[4 + i] = dot("tf,td->fd", half(du), low)
        grads[4 + ratio + i] = dot("tf,to->fo", half(acts[i]), df)
    grad_b1 = jnp.stack(b_rows).reshape(ratio, 4, share).transpose(1, 0, 2).reshape(ratio, width)
    grad_g1 = jnp.sum(dy1 * n1, axis=0)
    grad_e1 = jnp.sum(dy1, axis=0)
    dh1 = norm_back(dy1, n1, i1, gain_one)
    da = dh1.astype(BF16)
    grad_bo = jnp.sum(da.astype(F32), axis=0)
    grads[3] = dot("ts,to->so", half(ctx), da)
    dctx = dot("to,so->ts", da, wo).astype(BF16).reshape(ns, SPAN_ROWS, heads, HDIM)
    dp = dot("sqhd,skhd->shqk", dctx, v_s)
    ds = (probs * (dp - jnp.sum(probs * dp, axis=-1, keepdims=True))).astype(BF16)
    dq = (dot("shqk,skhd->sqhd", ds, k_s) * scale).astype(BF16).reshape(-1, width)
    dk = (dot("shqk,sqhd->skhd", ds, q_s) * scale).astype(BF16).reshape(-1, width)
    dv = dot("shqk,sqhd->skhd", pr, dctx).astype(BF16).reshape(-1, width)
    grads[0] = dot("ts,td->sd", half(dq), hm)
    grads[1] = dot("ts,td->sd", half(dk), hid)
    grads[2] = dot("ts,td->sd", half(dv), hid)
    grad_bq = jnp.sum(dq.astype(F32), axis=0)
    grad_bv = jnp.sum(dv.astype(F32), axis=0)
    back = (dh1 + dot("ts,sd->td", dq, wq)).astype(BF16).reshape(ns, SPAN_ROWS, width)
    dx = dot("ts,sd->td", dk, wk) + dot("ts,sd->td", dv, wv) + dot("sit,sid->std", pick, back).reshape(-1, width)
    dx = lax.dynamic_slice_in_dim(dx.astype(BF16), rx * own, own, 0)
    grad_in = lax.all_gather(dx, "mp", axis=0, tiled=True)

    vec_grad = jnp.concatenate([
        jnp.stack([grad_bq, grad_bv, grad_bo]), grad_b1,
        jnp.stack([grad_b2, grad_g1, grad_e1, grad_g2, grad_e2])], axis=0)
    vec_total = lax.psum(vec_grad, ("dp", "mp")) * 0.5
    new_vec = adamw(vectors, vec_one, vec_two, vec_total, VECTOR_RATE)

    order = tuple(p for i in range(ratio) for p in (4 + ratio + i, 4 + i)) + (3, 0, 1, 2)
    slot_grad = reduce_grads(owners, jnp.stack([grads[p] for p in order]).astype(BF16), line, order, cap)
    slot_grad = jnp.transpose(slot_grad, (0, 2, 1))
    held = jnp.sum((owners == lax.axis_index("dp")).astype(jnp.int32))
    occupied = (jnp.arange(cap) < held).astype(F32)[:, None, None]
    new_slots = adamw(master_slots, slot_one, slot_two, slot_grad, MATRIX_RATE)
    return (layer, grad_in) + new_vec + tuple(v * occupied for v in new_slots)


def solution(mesh):
    line = mesh.shape["dp"] // 2
    rows, slots = P("dp", None), P("dp", None, "mp")
    return jax.shard_map(
        functools.partial(on_device, line),
        mesh=mesh,
        in_specs=(rows, rows, P("dp", None, None), P(), P(), P(), P(), slots, slots, slots),
        out_specs=(rows, rows, P(), P(), P(), slots, slots, slots),
        check_vma=False,
    )
```

```python
import functools
import jax
import jax.numpy as jnp
from jax import lax
from jax.sharding import PartitionSpec as P
from jax.experimental import pallas as pl
from jax.experimental.pallas import tpu as pltpu

MESH = pl.DeviceIdType.MESH
BF16 = jnp.bfloat16
F32 = jnp.float32
LN_EPS = 1e-12
HDIM = 64
LEN = 512
NT = (((1,), (1,)), ((), ()))
NN = (((1,), (0,)), ((), ()))
TN = (((0,), (0,)), ((), ()))


def dg(left, right, dims):
    return lax.dot_general(left, right, dims, preferred_element_type=F32)


def flow_order(nmat):
    ratio = (nmat - 4) // 2
    return (0, 1, 2, 3) + tuple(p for k in range(ratio) for p in (4 + k, 4 + ratio + k))


def layer_norm(value, gain, shift):
    center = value - jnp.mean(value, axis=-1, keepdims=True)
    inverse = lax.rsqrt(jnp.mean(center * center, axis=-1, keepdims=True) + LN_EPS)
    normed = center * inverse
    return normed * gain + shift, normed, inverse


def gelu(value):
    return 0.5 * value * (1.0 + lax.erf(value * 2.0 ** (-0.5)))


def place():
    dp, mp = lax.axis_index("dp"), lax.axis_index("mp")
    return dp // 2, dp % 2, mp // 2, mp % 2


def device(z, y, x, c):
    return (z * 2 + y, x * 2 + c)


def greet(line):
    z, y, x, c = place()
    bar = pltpu.get_barrier_semaphore()
    for who in (device(z, 1 - y, x, c), device(z, y, 1 - x, c), device(z, y, x, 1 - c)):
        pl.semaphore_signal(bar, inc=1, device_id=who, device_id_type=MESH)

    @pl.when(z > 0)
    def _():
        pl.semaphore_signal(bar, inc=1, device_id=device(z - 1, y, x, c), device_id_type=MESH)

    @pl.when(z < line - 1)
    def _():
        pl.semaphore_signal(bar, inc=1, device_id=device(z + 1, y, x, c), device_id_type=MESH)

    peers = 3 + jnp.where(z > 0, 1, 0) + jnp.where(z < line - 1, 1, 0)
    pl.semaphore_wait(bar, peers.astype(jnp.int32))


def rcopy(src, dst, send, recv, who):
    return pltpu.make_async_remote_copy(
        src_ref=src, dst_ref=dst, send_sem=send, recv_sem=recv, device_id=who, device_id_type=MESH
    )


def forward_kernel(line, nmat, cap, owners, slots_in, hidden, vecs, out, layer, k_ref, v_ref,
                   full, slots, ys, stage, fr, fl, hid, q_ref, ctx, y1, low, acc, zo, idx,
                   hid_sem, slot_send, slot_recv, sr, rl, sl, rr, xs, xr, ysd, yr, ds, dr, cs, cr, loc):
    share = slots.shape[1]
    quarter = share // 2
    half = quarter // 2
    nchunk = 2 * nmat
    z, y, x, c = place()
    me = 2 * x + c
    over = 2 * (1 - x) + c
    to_y, to_x, to_c = device(z, 1 - y, x, c), device(z, y, 1 - x, c), device(z, y, x, 1 - c)
    greet(line)
    ratio = (nmat - 4) // 2
    order = flow_order(nmat)
    own_rows = q_ref.shape[0]
    hid_copy = pltpu.make_async_copy(
        hidden.at[pl.ds(pl.multiple_of(me * own_rows, 16), own_rows)], hid, hid_sem)
    hid_copy.start()

    def slot_copy(s):
        return rcopy(
            slots.at[s, pl.ds(pl.multiple_of((1 - y) * quarter, 16), quarter), :],
            ys[s].at[y], slot_send.at[s], slot_recv.at[s], to_y)

    for s in range(cap):
        slots[s] = slots_in[s].astype(BF16)
        slot_copy(s).start()
        ys[s][y] = slots[s, pl.ds(pl.multiple_of(y * quarter, 16), quarter), :]
    for j, p in enumerate(order):
        mine = owners[p]
        place_of = jnp.int32(0)
        for q in range(p):
            place_of += jnp.where(owners[q] == mine, 1, 0).astype(jnp.int32)
        zo[j] = mine // 2
        idx[j] = (mine % 2) * cap + jnp.minimum(place_of, cap - 1)

    def rows(block, yy, h):
        return pl.ds(pl.multiple_of(block * share + yy * quarter + h * half, 16), half)

    def own(r):
        at = pl.ds(pl.multiple_of((r % 2) * half, 16), half)
        slot, half_of = idx[r // 2] % cap, idx[r // 2] // cap
        stage[...] = ys[0][half_of, at, :]
        for s in range(1, cap):
            @pl.when(r // 2 >= s)
            def _():
                stage[...] = jnp.where(slot == s, ys[s][half_of, at, :], stage[...])

        return stage[...]

    def right(r):
        return rcopy(fr.at[r], fr.at[r], sr.at[r], rl.at[r], device(z + 1, y, x, c))

    def left(r):
        return rcopy(fl.at[r], fl.at[r], sl.at[r], rr.at[r], device(z - 1, y, x, c))

    def x_copy(f):
        at = full.at[f // 2, rows(me, y, f % 2), :]
        return rcopy(at, at, xs.at[f], xr.at[f], to_x)

    def x_came(f):
        at = full.at[f // 2, rows(over, y, f % 2), :]
        return rcopy(at, at, xs.at[f], xr.at[f], to_x)

    def y_copy(f):
        at = full.at[f // 2, rows(me, y, f % 2), :]
        return rcopy(at, at, ysd.at[f], yr.at[f], to_y)

    def y_came(f):
        at = full.at[f // 2, rows(me, 1 - y, f % 2), :]
        return rcopy(at, at, ysd.at[f], yr.at[f], to_y)

    def diag_x(f):
        at = full.at[f // 2, rows(me, 1 - y, f % 2), :]
        return rcopy(at, at, ds.at[f], dr.at[f], to_x)

    def diag_y(f):
        at = full.at[f // 2, rows(over, y, f % 2), :]
        return rcopy(at, at, ds.at[f], dr.at[f], to_y)

    def diag_came(f):
        at = full.at[f // 2, rows(over, 1 - y, f % 2), :]
        return rcopy(at, at, ds.at[f], dr.at[f], to_x)

    def core_copy(p, k):
        block = jnp.where(k == 0, me, over) if not isinstance(k, int) else (me, over)[k]
        at = full.at[p, pl.ds(pl.multiple_of(block * share, 16), share), :]
        return rcopy(at, at, cs.at[p, k], cr.at[p, k], to_c)

    def core_came(p, k):
        block = (2 * x + 1 - c, 2 * (1 - x) + 1 - c)[k]
        at = full.at[p, pl.ds(pl.multiple_of(block * share, 16), share), :]
        return rcopy(at, at, cs.at[p, k], cr.at[p, k], to_c)

    def keep(p):
        return pltpu.make_async_copy(full.at[p], out.at[p], loc.at[p])

    lag0 = 2 * (line - 1)
    lag1 = lag0 + 2
    lag2 = lag1 + 3
    lag3 = lag2 + 1

    def slot_came(s):
        rcopy(slots.at[s, pl.ds(pl.multiple_of((1 - y) * quarter, 16), quarter), :],
              ys[s].at[1 - y], slot_send.at[s], slot_recv.at[s], to_y).wait_recv()

    def tick(t):
        for s in range(cap):
            pl.when(t == 2 * s)(functools.partial(slot_came, s))

        r = t - 2 * z

        @pl.when((r >= 0) & (r < nchunk))
        def _():
            @pl.when(z == 0)
            def _():
                fr[r] = own(r)

            @pl.when(z > 0)
            def _():
                right(r).wait_recv()
                fr[r] = jnp.where(zo[r // 2] == z, own(r), fr[r])

            @pl.when(z < line - 1)
            def _():
                right(r).start()

        l = t - 2 * (line - 1 - z)

        @pl.when((l >= 0) & (l < nchunk))
        def _():
            @pl.when(z == line - 1)
            def _():
                fl[l] = own(l)

            @pl.when(z < line - 1)
            def _():
                left(l).wait_recv()
                fl[l] = jnp.where(zo[l // 2] == z, own(l), fl[l])

            @pl.when(z > 0)
            def _():
                left(l).start()

        f = t - lag0

        @pl.when((f >= 0) & (f < nchunk))
        def _():
            full[f // 2, rows(me, y, f % 2), :] = jnp.where(zo[f // 2] <= z, fr[f], fl[f])
            x_copy(f).start()
            y_copy(f).start()

        g = t - lag1

        @pl.when((g >= 0) & (g < nchunk))
        def _():
            x_came(g).wait_recv()
            y_came(g).wait_recv()

            @pl.when(g % 2 == 0)
            def _():
                diag_x(g).start()

            @pl.when(g % 2 == 1)
            def _():
                diag_y(g).start()

        e = t - lag2

        @pl.when((e >= 0) & (e < nchunk))
        def _():
            diag_came(e).wait_recv()

            @pl.when(e % 2 == 1)
            def _():
                for k in range(2):
                    core_copy(e // 2, k).start()

        w = t - lag3

        @pl.when((w >= 0) & (w < nchunk) & (w % 2 == 1))
        def _():
            for k in range(2):
                core_came(w // 2, k).wait_recv()
            keep(w // 2).start()

    ticks = nchunk + lag3
    first = lag3 + 6

    def ticking(start, count):
        def body(i, carry):
            tick(start + i)
            return carry

        lax.fori_loop(0, count, body, 0)

    ticking(0, first)
    hid_copy.wait()
    tile = min(512, own_rows)
    tiles = own_rows // tile

    def at_rows(i):
        return pl.ds(pl.multiple_of(i * tile, 16), tile)

    def project(i, carry):
        block = hid[at_rows(i), :]
        q_ref[at_rows(i), :] = (
            (dg(block, full[0], NT) + vecs[0:1, :]).astype(BF16) * jnp.asarray(HDIM ** -0.5, BF16))
        k_ref[at_rows(i), :] = dg(block, full[1], NT).astype(BF16)
        v_ref[at_rows(i), :] = (dg(block, full[2], NT) + vecs[1:2, :]).astype(BF16)
        return carry

    lax.fori_loop(0, tiles, project, 0)
    pairs = hid.shape[1] // (2 * HDIM)
    blocks = own_rows // LEN * pairs
    lane = lax.broadcasted_iota(jnp.int32, (LEN, 2 * HDIM), 1)
    left_half = lane < HDIM
    ones = jnp.ones((LEN, 2 * HDIM), BF16)

    def attend(i):
        at = pl.ds(pl.multiple_of((i // pairs) * LEN, 16), LEN)
        lanes = pl.ds(pl.multiple_of((i % pairs) * (2 * HDIM), 2 * HDIM), 2 * HDIM)
        q_blk, k_blk = q_ref[at, lanes], k_ref[at, lanes]
        v_blk = jnp.concatenate([v_ref[at, lanes], ones], axis=1)
        mixed = []
        for h in range(2):
            q_one = jnp.where(left_half if h == 0 else ~left_half, q_blk, jnp.zeros_like(q_blk))
            scores = dg(q_one, k_blk, NT)
            raised = jnp.exp(scores - jnp.max(scores, axis=-1, keepdims=True)).astype(BF16)
            both = dg(raised, v_blk, NN)
            mixed.append(both[:, :2 * HDIM] / both[:, 2 * HDIM:])
        ctx[at, lanes] = jnp.where(left_half, mixed[0], mixed[1]).astype(BF16)

    def attend_step(i, carry):
        tick(first + i)
        attend(i)
        return carry

    lax.fori_loop(0, blocks, attend_step, 0)
    after = first + blocks
    ticking(after, max(0, ticks - after - 2 * tiles * 2))
    after = max(after, ticks - 2 * tiles * 2)

    def mix(i, carry):
        h1 = hid[at_rows(i), :].astype(F32) + dg(ctx[at_rows(i), :], full[3], NN) + vecs[2:3, :]
        value = layer_norm(h1, vecs[4 + ratio:5 + ratio, :], vecs[5 + ratio:6 + ratio, :])[0]
        y1[at_rows(i), :] = value
        low[at_rows(i), :] = value.astype(BF16)
        acc[at_rows(i), :] = value + vecs[3 + ratio:4 + ratio, :]
        return carry

    lax.fori_loop(0, tiles, mix, 0)

    def feed(i, carry):
        k, at = i // tiles, at_rows(i % tiles)

        @pl.when(after + i < ticks)
        def _():
            tick(after + i)

        up = dg(low[at, :], full[4 + 2 * k], NT) + vecs[pl.ds(3 + k, 1), :]
        acc[at, :] = acc[at, :] + dg(gelu(up).astype(BF16), full[5 + 2 * k], NN)
        return carry

    lax.fori_loop(0, ratio * tiles, feed, 0)

    def close(i, carry):
        layer[at_rows(i), :] = layer_norm(
            acc[at_rows(i), :], vecs[6 + ratio:7 + ratio, :], vecs[7 + ratio:8 + ratio, :])[0].astype(BF16)
        return carry

    lax.fori_loop(0, tiles, close, 0)

    def finish(r, carry):
        @pl.when(z < line - 1)
        def _():
            right(r).wait_send()

        @pl.when(z > 0)
        def _():
            left(r).wait_send()

        x_copy(r).wait_send()
        y_copy(r).wait_send()
        diag_came(r).wait_send()
        return carry

    lax.fori_loop(0, nchunk, finish, 0)

    def last(p, carry):
        for k in range(2):
            core_copy(p, k).wait_send()
        keep(p).wait()
        return carry

    lax.fori_loop(0, nmat, last, 0)
    for s in range(cap):
        slot_copy(s).wait_send()


def forward(owners, slots, hidden, vecs, line):
    cap, share, width = slots.shape
    nmat = owners.shape[0]
    own_rows = hidden.shape[0] // 4
    quarter, half = share // 2, share // 4
    n = 2 * nmat
    dma = pltpu.SemaphoreType.DMA
    vmem = pl.BlockSpec(memory_space=pltpu.VMEM)
    hbm = pl.BlockSpec(memory_space=pl.ANY)
    rows = jax.ShapeDtypeStruct((own_rows, width), BF16)
    return pl.pallas_call(
        functools.partial(forward_kernel, line, nmat, cap),
        out_shape=(jax.ShapeDtypeStruct((nmat, 4 * share, width), BF16), rows, rows, rows),
        in_specs=[pl.BlockSpec(memory_space=pltpu.SMEM), vmem, hbm, vmem],
        out_specs=(hbm, vmem, vmem, vmem),
        scratch_shapes=[
            pltpu.VMEM((nmat, 4 * share, width), BF16),
            pltpu.VMEM((cap, share, width), BF16),
            [pltpu.VMEM((2, quarter, width), BF16)] * cap,
            pltpu.VMEM((half, width), BF16),
            pltpu.VMEM((n, half, width), BF16),
            pltpu.VMEM((n, half, width), BF16),
            pltpu.VMEM((own_rows, width), BF16),
            pltpu.VMEM((own_rows, width), BF16),
            pltpu.VMEM((own_rows, width), BF16),
            pltpu.VMEM((own_rows, width), F32),
            pltpu.VMEM((own_rows, width), BF16),
            pltpu.VMEM((own_rows, width), F32),
            pltpu.SMEM((nmat,), jnp.int32),
            pltpu.SMEM((nmat,), jnp.int32),
            dma(()), dma((cap,)), dma((cap,)),
        ] + [dma((n,))] * 10 + [dma((nmat, 2)), dma((nmat, 2)), dma((nmat,))],
        name="forward",
        compiler_params=pltpu.CompilerParams(
            collective_id=1, has_side_effects=True, vmem_limit_bytes=58 * 1024 * 1024),
    )(owners, slots, hidden, vecs)


def reduce_kernel(line, order, cap, owners, grads, out, cin, hold, yo, yi, fr, fl, to, do, di,
                  who, pick, cs, cr, ysd, yr, sr, rl, sl, rr, dsem):
    nmat = len(order)
    share = grads.shape[1] // 2
    quarter = share // 2
    f32, bf16 = jnp.float32, jnp.bfloat16
    z, y, x, c = place()
    to_y, to_c = device(z, 1 - y, x, c), device(z, y, x, 1 - c)
    greet(line)

    for s in range(2 * cap):
        pick[s] = 0
    for j, p in enumerate(order):
        mine = owners[p]
        place_of = jnp.int32(0)
        for q in range(p):
            place_of += jnp.where(owners[q] == mine, 1, 0).astype(jnp.int32)
        who[j] = mine // 2
        slot = (mine % 2) * cap + jnp.minimum(place_of, cap - 1)
        for s in range(2 * cap):
            pick[s] = jnp.where((mine // 2 == z) & (slot == s), j, pick[s])

    def rows(start, size):
        return pl.ds(pl.multiple_of(start, 16), size)

    def core_copy(j):
        return rcopy(grads.at[j, rows((1 - c) * share, share), :], cin.at[j], cs.at[j], cr.at[j], to_c)

    def y_copy(j):
        return rcopy(yo.at[j], yi.at[j], ysd.at[j], yr.at[j], to_y)

    def right(j):
        return rcopy(to.at[0, j], fr.at[j], sr.at[j], rl.at[j], device(z + 1, y, x, c))

    def left(j):
        return rcopy(to.at[1, j], fl.at[j], sl.at[j], rr.at[j], device(z - 1, y, x, c))

    def stage0(j):
        core_copy(j).start()

    def stage1(j):
        core_copy(j).wait_recv()
        for part in range(2):
            at = y if part == 0 else 1 - y
            total = (grads[j, rows(c * share + at * quarter, quarter), :].astype(f32)
                     + cin[j, rows(at * quarter, quarter), :].astype(f32))
            if part == 0:
                hold[j] = total
            else:
                yo[j] = total.astype(bf16)
        y_copy(j).start()

    def stage2(j):
        y_copy(j).wait_recv()
        hold[j] = hold[j] + yi[j].astype(f32)

    def flow_right(j):
        @pl.when(z == 0)
        def _():
            to[0, j] = hold[j].astype(bf16)

        @pl.when(z > 0)
        def _():
            right(j).wait_recv()
            to[0, j] = (hold[j] + fr[j].astype(f32)).astype(bf16)

        @pl.when(z < line - 1)
        def _():
            right(j).start()

    def flow_left(j):
        @pl.when(z == line - 1)
        def _():
            to[1, j] = hold[j].astype(bf16)

        @pl.when(z < line - 1)
        def _():
            left(j).wait_recv()
            to[1, j] = (hold[j] + fl[j].astype(f32)).astype(bf16)

        @pl.when(z > 0)
        def _():
            left(j).start()

    def total(j):
        value = hold[j]
        value = value + jnp.where(z > 0, fr[j].astype(f32), 0.0)
        return value + jnp.where(z < line - 1, fl[j].astype(f32), 0.0)

    def ranged(j, do_it):
        pl.when((j >= 0) & (j < nmat))(functools.partial(do_it, j))

    def tick(t):
        ranged(t, stage0)
        ranged(t - 1, stage1)
        ranged(t - 3, stage2)
        ranged(t - 4 - 2 * z, flow_right)
        ranged(t - 4 - 2 * (line - 1 - z), flow_left)

    def body(t, carry):
        tick(t)
        return carry

    lax.fori_loop(0, nmat + 4 + 2 * (line - 1), body, 0)

    for s in range(cap):
        do[s] = total(pick[(1 - y) * cap + s]).astype(bf16)
    deliver = rcopy(do, di, dsem.at[0], dsem.at[1], to_y)
    deliver.start()
    for s in range(cap):
        out[s, rows(y * quarter, quarter), :] = total(pick[y * cap + s])
    deliver.wait_recv()
    for s in range(cap):
        out[s, rows((1 - y) * quarter, quarter), :] = di[s].astype(f32)
    deliver.wait_send()

    def finish(j, carry):
        core_copy(j).wait_send()
        y_copy(j).wait_send()

        @pl.when(z < line - 1)
        def _():
            right(j).wait_send()

        @pl.when(z > 0)
        def _():
            left(j).wait_send()

        return carry

    lax.fori_loop(0, nmat, finish, 0)


def reduce_grads(owners, grads, line, order, cap):
    nmat, both, width = grads.shape
    share = both // 2
    quarter = share // 2
    bf16, f32 = jnp.bfloat16, jnp.float32
    dma = pltpu.SemaphoreType.DMA
    return pl.pallas_call(
        functools.partial(reduce_kernel, line, order, cap),
        out_shape=jax.ShapeDtypeStruct((cap, share, width), f32),
        in_specs=[pl.BlockSpec(memory_space=pltpu.SMEM), pl.BlockSpec(memory_space=pltpu.VMEM)],
        out_specs=pl.BlockSpec(memory_space=pltpu.VMEM),
        scratch_shapes=[
            pltpu.VMEM((nmat, share, width), bf16),
            pltpu.VMEM((nmat, quarter, width), f32),
            pltpu.VMEM((nmat, quarter, width), bf16),
            pltpu.VMEM((nmat, quarter, width), bf16),
            pltpu.VMEM((nmat, quarter, width), bf16),
            pltpu.VMEM((nmat, quarter, width), bf16),
            pltpu.VMEM((2, nmat, quarter, width), bf16),
            pltpu.VMEM((cap, quarter, width), bf16),
            pltpu.VMEM((cap, quarter, width), bf16),
            pltpu.SMEM((nmat,), jnp.int32),
            pltpu.SMEM((2 * cap,), jnp.int32),
        ] + [dma((nmat,))] * 8 + [dma((2,))],
        name="reduce_grads",
        compiler_params=pltpu.CompilerParams(
            collective_id=2, has_side_effects=True, vmem_limit_bytes=56 * 1024 * 1024),
    )(owners, grads)


STEP = 10
SPAN_ROWS = 96
MATRIX_RATE = 0.03
VECTOR_RATE = 0.25
BETA_ONE = 0.5
BETA_TWO = 0.5
DECAY = 0.01
ADAM_EPS = 1e-08


def norm_back(grad, normed, inverse, gain):
    scaled = grad * gain
    first = jnp.mean(scaled, axis=-1, keepdims=True)
    second = jnp.mean(scaled * normed, axis=-1, keepdims=True)
    return inverse * (scaled - first - normed * second)


def gelu_slope(value):
    cdf = 0.5 * (1.0 + lax.erf(value * 2.0 ** (-0.5)))
    pdf = jnp.exp(-0.5 * value * value) * (2.0 * jnp.pi) ** (-0.5)
    return cdf + value * pdf


def adamw(weight, moment_one, moment_two, grad, step_rate):
    new_one = BETA_ONE * moment_one + (1.0 - BETA_ONE) * grad
    new_two = BETA_TWO * moment_two + (1.0 - BETA_TWO) * grad * grad
    corr_one = 1.0 - BETA_ONE**STEP
    corr_two = 1.0 - BETA_TWO**STEP
    direction = new_one / corr_one / (jnp.sqrt(new_two / corr_two) + ADAM_EPS)
    return (weight - step_rate * (direction + DECAY * weight), new_one, new_two)


def dot(eq, a, b):
    return jnp.einsum(eq, a, b, preferred_element_type=F32)


def on_device(line, hidden_in, incoming, spans, owners, vectors, vec_one, vec_two, master_slots, slot_one, slot_two):
    cap, width, share = master_slots.shape
    nmat = owners.shape[0]
    ratio = (nmat - 4) // 2
    scale = HDIM ** (-0.5)
    heads = width // HDIM
    rank_mp = lax.axis_index("mp")
    rx, rc = rank_mp // 2, rank_mp % 2
    tokens = hidden_in.shape[0]
    own = tokens // 4
    nseq = own // LEN
    b_up = vectors[3:3 + ratio].reshape(4, ratio, share).transpose(1, 0, 2).reshape(ratio, width)
    b_q, b_v, b_o, b_down = vectors[0], vectors[1], vectors[2], vectors[3 + ratio]
    gain_one, shift_one, gain_two, shift_two = (vectors[4 + ratio + i] for i in range(4))

    def split(v):
        return v.reshape(-1, LEN, heads, HDIM)

    def attend(block):
        q_blk, k_blk, v_blk = block
        scores = dot("qhd,khd->hqk", q_blk, k_blk) * scale
        probs = jax.nn.softmax(scores, axis=-1)
        return dot("hqk,khd->qhd", probs.astype(BF16), v_blk).astype(BF16)

    vecs = jnp.concatenate([vectors[:3], b_up, vectors[3 + ratio:]], axis=0)
    flow, layer, k_own, v_own = forward(owners, jnp.transpose(master_slots, (0, 2, 1)), hidden_in, vecs, line)
    layer = lax.all_gather(layer, "mp", axis=0, tiled=True)
    where = flow_order(nmat)
    pieces = [flow[where.index(p)] for p in range(nmat)]
    wq, wk, wv, wo = pieces[:4]

    def ours(v):
        v = v.reshape((2, 2, v.shape[0] // 4) + v.shape[1:])
        v = lax.dynamic_index_in_dim(v, rc, 1, keepdims=False)
        return v.reshape((-1,) + v.shape[2:])
    hid = ours(hidden_in)
    inc = ours(incoming)
    spn = ours(spans)
    position = jnp.arange(LEN, dtype=jnp.int32)
    starts = spn[:, :, 0][:, :, None]
    ends = starts + spn[:, :, 1][:, :, None]
    covered = jnp.any((position >= starts) & (position < ends), axis=1)
    rank = jnp.cumsum(covered.astype(jnp.int32), axis=1) - 1
    pick = ((rank[:, None, :] == jnp.arange(SPAN_ROWS)[None, :, None]) & covered[:, None, :]).astype(BF16)
    hid_s = hid.reshape(-1, LEN, width)
    ns = hid_s.shape[0]
    hm = dot("sit,std->sid", pick, hid_s).astype(BF16).reshape(-1, width)
    gm = dot("sit,std->sid", pick, inc.reshape(-1, LEN, width)).reshape(-1, width)
    q = (dot("td,sd->ts", hm, wq) + b_q).astype(BF16)
    k = dot("td,sd->ts", hid, wk).astype(BF16)
    v = (dot("td,sd->ts", hid, wv) + b_v).astype(BF16)
    q_s, k_s, v_s = q.reshape(ns, SPAN_ROWS, heads, HDIM), split(k), split(v)
    probs = jax.nn.softmax(dot("sqhd,skhd->shqk", q_s, k_s) * scale, axis=-1)
    pr = probs.astype(BF16)
    ctx = dot("shqk,skhd->sqhd", pr, v_s).astype(BF16).reshape(-1, width)
    y1, n1, i1 = layer_norm(hm.astype(F32) + dot("ts,so->to", ctx, wo) + b_o, gain_one, shift_one)
    low = y1.astype(BF16)
    second = y1 + b_down
    acts, ups = [], []
    for i in range(ratio):
        up = dot("td,fd->tf", low, pieces[4 + i]) + b_up[i]
        act = jax.nn.gelu(up, approximate=False).astype(BF16)
        second = second + dot("tf,fo->to", act, pieces[4 + ratio + i])
        ups.append(up)
        acts.append(act)
    _, n2, i2 = layer_norm(second, gain_two, shift_two)
    grad_g2 = jnp.sum(gm * n2, axis=0)
    grad_e2 = jnp.sum(gm, axis=0)
    dh2 = norm_back(gm, n2, i2, gain_two)
    df = dh2.astype(BF16)
    grad_b2 = jnp.sum(df.astype(F32), axis=0)

    def half(v):
        return lax.dynamic_slice_in_dim(v, rx * 2 * share, 2 * share, 1)
    grads = [None] * nmat
    dy1 = dh2
    b_rows = []
    for i in range(ratio):
        du = (dot("to,fo->tf", df, pieces[4 + ratio + i]) * gelu_slope(ups[i])).astype(BF16)
        dy1 = dy1 + dot("tf,fd->td", du, pieces[4 + i])
        b_rows.append(jnp.sum(du.astype(F32), axis=0))
        grads[4 + i] = dot("tf,td->fd", half(du), low)
        grads[4 + ratio + i] = dot("tf,to->fo", half(acts[i]), df)
    grad_b1 = jnp.stack(b_rows).reshape(ratio, 4, share).transpose(1, 0, 2).reshape(ratio, width)
    grad_g1 = jnp.sum(dy1 * n1, axis=0)
    grad_e1 = jnp.sum(dy1, axis=0)
    dh1 = norm_back(dy1, n1, i1, gain_one)
    da = dh1.astype(BF16)
    grad_bo = jnp.sum(da.astype(F32), axis=0)
    grads[3] = dot("ts,to->so", half(ctx), da)
    dctx = dot("to,so->ts", da, wo).astype(BF16).reshape(ns, SPAN_ROWS, heads, HDIM)
    dp = dot("sqhd,skhd->shqk", dctx, v_s)
    ds = (probs * (dp - jnp.sum(probs * dp, axis=-1, keepdims=True))).astype(BF16)
    dq = (dot("shqk,skhd->sqhd", ds, k_s) * scale).astype(BF16).reshape(-1, width)
    dk = (dot("shqk,sqhd->skhd", ds, q_s) * scale).astype(BF16).reshape(-1, width)
    dv = dot("shqk,sqhd->skhd", pr, dctx).astype(BF16).reshape(-1, width)
    grads[0] = dot("ts,td->sd", half(dq), hm)
    grads[1] = dot("ts,td->sd", half(dk), hid)
    grads[2] = dot("ts,td->sd", half(dv), hid)
    grad_bq = jnp.sum(dq.astype(F32), axis=0)
    grad_bv = jnp.sum(dv.astype(F32), axis=0)
    back = (dh1 + dot("ts,sd->td", dq, wq)).astype(BF16).reshape(ns, SPAN_ROWS, width)
    dx = dot("ts,sd->td", dk, wk) + dot("ts,sd->td", dv, wv) + dot("sit,sid->std", pick, back).reshape(-1, width)
    dx = lax.dynamic_slice_in_dim(dx.astype(BF16), rx * own, own, 0)
    grad_in = lax.all_gather(dx, "mp", axis=0, tiled=True)

    vec_grad = jnp.concatenate([
        jnp.stack([grad_bq, grad_bv, grad_bo]), grad_b1,
        jnp.stack([grad_b2, grad_g1, grad_e1, grad_g2, grad_e2])], axis=0)
    vec_total = lax.psum(vec_grad, ("dp", "mp")) * 0.5
    new_vec = adamw(vectors, vec_one, vec_two, vec_total, VECTOR_RATE)

    order = tuple(p for i in range(ratio) for p in (4 + ratio + i, 4 + i)) + (3, 0, 1, 2)
    slot_grad = reduce_grads(owners, jnp.stack([grads[p] for p in order]).astype(BF16), line, order, cap)
    slot_grad = jnp.transpose(slot_grad, (0, 2, 1))
    held = jnp.sum((owners == lax.axis_index("dp")).astype(jnp.int32))
    occupied = (jnp.arange(cap) < held).astype(F32)[:, None, None]
    new_slots = adamw(master_slots, slot_one, slot_two, slot_grad, MATRIX_RATE)
    return (layer, grad_in) + new_vec + tuple(v * occupied for v in new_slots)


def solution(mesh):
    line = mesh.shape["dp"] // 2
    rows, slots = P("dp", None), P("dp", None, "mp")
    return jax.shard_map(
        functools.partial(on_device, line),
        mesh=mesh,
        in_specs=(rows, rows, P("dp", None, None), P(), P(), P(), P(), slots, slots, slots),
        out_specs=(rows, rows, P(), P(), P(), slots, slots, slots),
        check_vma=False,
    )
```

```python
import functools
import jax
import jax.numpy as jnp
from jax import lax
from jax.sharding import PartitionSpec as P
from jax.experimental import pallas as pl
from jax.experimental.pallas import tpu as pltpu

MESH = pl.DeviceIdType.MESH
BF16 = jnp.bfloat16
F32 = jnp.float32
LN_EPS = 1e-12
HDIM = 64
LEN = 512
NT = (((1,), (1,)), ((), ()))
NN = (((1,), (0,)), ((), ()))
TN = (((0,), (0,)), ((), ()))


def dg(left, right, dims):
    return lax.dot_general(left, right, dims, preferred_element_type=F32)


def flow_order(nmat):
    ratio = (nmat - 4) // 2
    return (0, 1, 2, 3) + tuple(p for k in range(ratio) for p in (4 + k, 4 + ratio + k))


def layer_norm(value, gain, shift):
    center = value - jnp.mean(value, axis=-1, keepdims=True)
    inverse = lax.rsqrt(jnp.mean(center * center, axis=-1, keepdims=True) + LN_EPS)
    normed = center * inverse
    return normed * gain + shift, normed, inverse


def gelu(value):
    return 0.5 * value * (1.0 + lax.erf(value * 2.0 ** (-0.5)))


def place():
    dp, mp = lax.axis_index("dp"), lax.axis_index("mp")
    return dp // 2, dp % 2, mp // 2, mp % 2


def device(z, y, x, c):
    return (z * 2 + y, x * 2 + c)


def greet(line):
    z, y, x, c = place()
    bar = pltpu.get_barrier_semaphore()
    for who in (device(z, 1 - y, x, c), device(z, y, 1 - x, c), device(z, y, x, 1 - c)):
        pl.semaphore_signal(bar, inc=1, device_id=who, device_id_type=MESH)

    @pl.when(z > 0)
    def _():
        pl.semaphore_signal(bar, inc=1, device_id=device(z - 1, y, x, c), device_id_type=MESH)

    @pl.when(z < line - 1)
    def _():
        pl.semaphore_signal(bar, inc=1, device_id=device(z + 1, y, x, c), device_id_type=MESH)

    peers = 3 + jnp.where(z > 0, 1, 0) + jnp.where(z < line - 1, 1, 0)
    pl.semaphore_wait(bar, peers.astype(jnp.int32))


def rcopy(src, dst, send, recv, who):
    return pltpu.make_async_remote_copy(
        src_ref=src, dst_ref=dst, send_sem=send, recv_sem=recv, device_id=who, device_id_type=MESH
    )


def forward_kernel(line, nmat, cap, owners, slots_in, hidden, vecs, out, layer, k_ref, v_ref,
                   full, slots, ys, stage, fr, fl, hid, q_ref, ctx, y1, low, acc, zo, idx,
                   hid_sem, slot_send, slot_recv, sr, rl, sl, rr, xs, xr, ysd, yr, ds, dr, cs, cr, loc):
    share = slots.shape[1]
    quarter = share // 2
    half = quarter // 2
    nchunk = 2 * nmat
    z, y, x, c = place()
    me = 2 * x + c
    over = 2 * (1 - x) + c
    to_y, to_x, to_c = device(z, 1 - y, x, c), device(z, y, 1 - x, c), device(z, y, x, 1 - c)
    greet(line)
    ratio = (nmat - 4) // 2
    order = flow_order(nmat)
    own_rows = q_ref.shape[0]
    hid_copy = pltpu.make_async_copy(
        hidden.at[pl.ds(pl.multiple_of(me * own_rows, 16), own_rows)], hid, hid_sem)
    hid_copy.start()

    def slot_copy(s):
        return rcopy(
            slots.at[s, pl.ds(pl.multiple_of((1 - y) * quarter, 16), quarter), :],
            ys[s].at[y], slot_send.at[s], slot_recv.at[s], to_y)

    for s in range(cap):
        slots[s] = slots_in[s].astype(BF16)
        slot_copy(s).start()
        ys[s][y] = slots[s, pl.ds(pl.multiple_of(y * quarter, 16), quarter), :]
    for j, p in enumerate(order):
        mine = owners[p]
        place_of = jnp.int32(0)
        for q in range(p):
            place_of += jnp.where(owners[q] == mine, 1, 0).astype(jnp.int32)
        zo[j] = mine // 2
        idx[j] = (mine % 2) * cap + jnp.minimum(place_of, cap - 1)

    def rows(block, yy, h):
        return pl.ds(pl.multiple_of(block * share + yy * quarter + h * half, 16), half)

    def own(r):
        at = pl.ds(pl.multiple_of((r % 2) * half, 16), half)
        slot, half_of = idx[r // 2] % cap, idx[r // 2] // cap
        stage[...] = ys[0][half_of, at, :]
        for s in range(1, cap):
            @pl.when(r // 2 >= s)
            def _():
                stage[...] = jnp.where(slot == s, ys[s][half_of, at, :], stage[...])

        return stage[...]

    def right(r):
        return rcopy(fr.at[r], fr.at[r], sr.at[r], rl.at[r], device(z + 1, y, x, c))

    def left(r):
        return rcopy(fl.at[r], fl.at[r], sl.at[r], rr.at[r], device(z - 1, y, x, c))

    def x_copy(f):
        at = full.at[f // 2, rows(me, y, f % 2), :]
        return rcopy(at, at, xs.at[f], xr.at[f], to_x)

    def x_came(f):
        at = full.at[f // 2, rows(over, y, f % 2), :]
        return rcopy(at, at, xs.at[f], xr.at[f], to_x)

    def y_copy(f):
        at = full.at[f // 2, rows(me, y, f % 2), :]
        return rcopy(at, at, ysd.at[f], yr.at[f], to_y)

    def y_came(f):
        at = full.at[f // 2, rows(me, 1 - y, f % 2), :]
        return rcopy(at, at, ysd.at[f], yr.at[f], to_y)

    def diag_x(f):
        at = full.at[f // 2, rows(me, 1 - y, f % 2), :]
        return rcopy(at, at, ds.at[f], dr.at[f], to_x)

    def diag_y(f):
        at = full.at[f // 2, rows(over, y, f % 2), :]
        return rcopy(at, at, ds.at[f], dr.at[f], to_y)

    def diag_came(f):
        at = full.at[f // 2, rows(over, 1 - y, f % 2), :]
        return rcopy(at, at, ds.at[f], dr.at[f], to_x)

    def core_copy(p, k):
        block = jnp.where(k == 0, me, over) if not isinstance(k, int) else (me, over)[k]
        at = full.at[p, pl.ds(pl.multiple_of(block * share, 16), share), :]
        return rcopy(at, at, cs.at[p, k], cr.at[p, k], to_c)

    def core_came(p, k):
        block = (2 * x + 1 - c, 2 * (1 - x) + 1 - c)[k]
        at = full.at[p, pl.ds(pl.multiple_of(block * share, 16), share), :]
        return rcopy(at, at, cs.at[p, k], cr.at[p, k], to_c)

    def keep(p):
        return pltpu.make_async_copy(full.at[p], out.at[p], loc.at[p])

    lag0 = 2 * (line - 1)
    lag1 = lag0 + 2
    lag2 = lag1 + 3
    lag3 = lag2 + 1

    def slot_came(s):
        rcopy(slots.at[s, pl.ds(pl.multiple_of((1 - y) * quarter, 16), quarter), :],
              ys[s].at[1 - y], slot_send.at[s], slot_recv.at[s], to_y).wait_recv()

    def tick(t):
        for s in range(cap):
            pl.when(t == 2 * s)(functools.partial(slot_came, s))

        r = t - 2 * z

        @pl.when((r >= 0) & (r < nchunk))
        def _():
            @pl.when(z == 0)
            def _():
                fr[r] = own(r)

            @pl.when(z > 0)
            def _():
                right(r).wait_recv()
                fr[r] = jnp.where(zo[r // 2] == z, own(r), fr[r])

            @pl.when(z < line - 1)
            def _():
                right(r).start()

        l = t - 2 * (line - 1 - z)

        @pl.when((l >= 0) & (l < nchunk))
        def _():
            @pl.when(z == line - 1)
            def _():
                fl[l] = own(l)

            @pl.when(z < line - 1)
            def _():
                left(l).wait_recv()
                fl[l] = jnp.where(zo[l // 2] == z, own(l), fl[l])

            @pl.when(z > 0)
            def _():
                left(l).start()

        f = t - lag0

        @pl.when((f >= 0) & (f < nchunk))
        def _():
            full[f // 2, rows(me, y, f % 2), :] = jnp.where(zo[f // 2] <= z, fr[f], fl[f])
            x_copy(f).start()
            y_copy(f).start()

        g = t - lag1

        @pl.when((g >= 0) & (g < nchunk))
        def _():
            x_came(g).wait_recv()
            y_came(g).wait_recv()

            @pl.when(g % 2 == 0)
            def _():
                diag_x(g).start()

            @pl.when(g % 2 == 1)
            def _():
                diag_y(g).start()

        e = t - lag2

        @pl.when((e >= 0) & (e < nchunk))
        def _():
            diag_came(e).wait_recv()

            @pl.when(e % 2 == 1)
            def _():
                for k in range(2):
                    core_copy(e // 2, k).start()

        w = t - lag3

        @pl.when((w >= 0) & (w < nchunk) & (w % 2 == 1))
        def _():
            for k in range(2):
                core_came(w // 2, k).wait_recv()
            keep(w // 2).start()

    ticks = nchunk + lag3
    first = lag3 + 6

    def ticking(start, count):
        def body(i, carry):
            tick(start + i)
            return carry

        lax.fori_loop(0, count, body, 0)

    ticking(0, first)
    hid_copy.wait()
    tile = min(512, own_rows)
    tiles = own_rows // tile

    def at_rows(i):
        return pl.ds(pl.multiple_of(i * tile, 16), tile)

    def project(i, carry):
        block = hid[at_rows(i), :]
        q_ref[at_rows(i), :] = (
            (dg(block, full[0], NT) + vecs[0:1, :]).astype(BF16) * jnp.asarray(HDIM ** -0.5, BF16))
        k_ref[at_rows(i), :] = dg(block, full[1], NT).astype(BF16)
        v_ref[at_rows(i), :] = (dg(block, full[2], NT) + vecs[1:2, :]).astype(BF16)
        return carry

    lax.fori_loop(0, tiles, project, 0)
    pairs = hid.shape[1] // (2 * HDIM)
    blocks = own_rows // LEN * pairs
    lane = lax.broadcasted_iota(jnp.int32, (LEN, 2 * HDIM), 1)
    left_half = lane < HDIM
    ones = jnp.ones((LEN, 2 * HDIM), BF16)

    def attend(i):
        at = pl.ds(pl.multiple_of((i // pairs) * LEN, 16), LEN)
        lanes = pl.ds(pl.multiple_of((i % pairs) * (2 * HDIM), 2 * HDIM), 2 * HDIM)
        q_blk, k_blk = q_ref[at, lanes], k_ref[at, lanes]
        v_blk = jnp.concatenate([v_ref[at, lanes], ones], axis=1)
        mixed = []
        for h in range(2):
            q_one = jnp.where(left_half if h == 0 else ~left_half, q_blk, jnp.zeros_like(q_blk))
            scores = dg(q_one, k_blk, NT)
            raised = jnp.exp(scores - jnp.max(scores, axis=-1, keepdims=True)).astype(BF16)
            both = dg(raised, v_blk, NN)
            mixed.append(both[:, :2 * HDIM] / both[:, 2 * HDIM:])
        ctx[at, lanes] = jnp.where(left_half, mixed[0], mixed[1]).astype(BF16)

    def attend_step(i, carry):
        tick(first + i)
        attend(i)
        return carry

    lax.fori_loop(0, blocks, attend_step, 0)
    after = first + blocks
    ticking(after, max(0, ticks - after - 2 * tiles * 2))
    after = max(after, ticks - 2 * tiles * 2)

    def mix(i, carry):
        h1 = hid[at_rows(i), :].astype(F32) + dg(ctx[at_rows(i), :], full[3], NN) + vecs[2:3, :]
        value = layer_norm(h1, vecs[4 + ratio:5 + ratio, :], vecs[5 + ratio:6 + ratio, :])[0]
        y1[at_rows(i), :] = value
        low[at_rows(i), :] = value.astype(BF16)
        acc[at_rows(i), :] = value + vecs[3 + ratio:4 + ratio, :]
        return carry

    lax.fori_loop(0, tiles, mix, 0)

    def feed(i, carry):
        k, at = i // tiles, at_rows(i % tiles)

        @pl.when(after + i < ticks)
        def _():
            tick(after + i)

        up = dg(low[at, :], full[4 + 2 * k], NT) + vecs[pl.ds(3 + k, 1), :]
        acc[at, :] = acc[at, :] + dg(gelu(up).astype(BF16), full[5 + 2 * k], NN)
        return carry

    lax.fori_loop(0, ratio * tiles, feed, 0)

    def close(i, carry):
        layer[at_rows(i), :] = layer_norm(
            acc[at_rows(i), :], vecs[6 + ratio:7 + ratio, :], vecs[7 + ratio:8 + ratio, :])[0].astype(BF16)
        return carry

    lax.fori_loop(0, tiles, close, 0)

    def finish(r, carry):
        @pl.when(z < line - 1)
        def _():
            right(r).wait_send()

        @pl.when(z > 0)
        def _():
            left(r).wait_send()

        x_copy(r).wait_send()
        y_copy(r).wait_send()
        diag_came(r).wait_send()
        return carry

    lax.fori_loop(0, nchunk, finish, 0)

    def last(p, carry):
        for k in range(2):
            core_copy(p, k).wait_send()
        keep(p).wait()
        return carry

    lax.fori_loop(0, nmat, last, 0)
    for s in range(cap):
        slot_copy(s).wait_send()


def forward(owners, slots, hidden, vecs, line):
    cap, share, width = slots.shape
    nmat = owners.shape[0]
    own_rows = hidden.shape[0] // 4
    quarter, half = share // 2, share // 4
    n = 2 * nmat
    dma = pltpu.SemaphoreType.DMA
    vmem = pl.BlockSpec(memory_space=pltpu.VMEM)
    hbm = pl.BlockSpec(memory_space=pl.ANY)
    rows = jax.ShapeDtypeStruct((own_rows, width), BF16)
    return pl.pallas_call(
        functools.partial(forward_kernel, line, nmat, cap),
        out_shape=(jax.ShapeDtypeStruct((nmat, 4 * share, width), BF16), rows, rows, rows),
        in_specs=[pl.BlockSpec(memory_space=pltpu.SMEM), vmem, hbm, vmem],
        out_specs=(hbm, vmem, vmem, vmem),
        scratch_shapes=[
            pltpu.VMEM((nmat, 4 * share, width), BF16),
            pltpu.VMEM((cap, share, width), BF16),
            [pltpu.VMEM((2, quarter, width), BF16)] * cap,
            pltpu.VMEM((half, width), BF16),
            pltpu.VMEM((n, half, width), BF16),
            pltpu.VMEM((n, half, width), BF16),
            pltpu.VMEM((own_rows, width), BF16),
            pltpu.VMEM((own_rows, width), BF16),
            pltpu.VMEM((own_rows, width), BF16),
            pltpu.VMEM((own_rows, width), F32),
            pltpu.VMEM((own_rows, width), BF16),
            pltpu.VMEM((own_rows, width), F32),
            pltpu.SMEM((nmat,), jnp.int32),
            pltpu.SMEM((nmat,), jnp.int32),
            dma(()), dma((cap,)), dma((cap,)),
        ] + [dma((n,))] * 10 + [dma((nmat, 2)), dma((nmat, 2)), dma((nmat,))],
        name="forward",
        compiler_params=pltpu.CompilerParams(
            collective_id=1, has_side_effects=True, vmem_limit_bytes=58 * 1024 * 1024),
    )(owners, slots, hidden, vecs)


SPAN_ROWS = 96


def norm_back(grad, normed, inverse, gain):
    scaled = grad * gain
    first = jnp.mean(scaled, axis=-1, keepdims=True)
    second = jnp.mean(scaled * normed, axis=-1, keepdims=True)
    return inverse * (scaled - first - normed * second)


def column_sum(value):
    return jnp.sum(value, axis=0, keepdims=True)


def backward_kernel(line, nmat, cap, owners, spans, vecs, flow, hidden, incoming, layer, k_own, v_own,
                    sg, vec_out, lay, gin,
                    full, hid, k_ref, v_ref, pick, probs, hm, gm, qm, ctx, n1, inv1, low, acc,
                    slope, act, df, dq, gqkv, gvec, vin, vz,
                    cin, hold, yi, fr, fl, do, di, slot_pick,
                    w_sem, in_sem, lsem_s, lsem_r, gsem_s, gsem_r, loc_sem,
                    cs, cr, ysd, yr, sr, rl, sl, rr, dsem, vs, vr, vzs, vzr):
    ratio = (nmat - 4) // 2
    width = vecs.shape[1]
    share = cin.shape[1]
    quarter, half = share // 2, share // 4
    nchunk = 2 * nmat
    z, y, x, c = place()
    me, over = 2 * x + c, 2 * (1 - x) + c
    to_y, to_x, to_c = device(z, 1 - y, x, c), device(z, y, 1 - x, c), device(z, y, x, 1 - c)
    own_rows = layer.shape[0]
    nseq = 2 * own_rows // LEN
    per = own_rows // LEN
    greet(line)

    def rows(start, size):
        return pl.ds(pl.multiple_of(start, 16), size)

    def block_copy(src, dst, b, sem):
        return pltpu.make_async_copy(
            src.at[rows((2 * b + c) * own_rows, own_rows)], dst.at[pl.ds(b * own_rows, own_rows)], sem)

    loads = [block_copy(hidden, hid, b, in_sem.at[b]) for b in range(2)]
    loads += [block_copy(incoming, v_ref, b, in_sem.at[2 + b]) for b in range(2)]
    loads += [pltpu.make_async_copy(src, dst.at[rows(x * own_rows, own_rows)], in_sem.at[4 + i])
              for i, (src, dst) in enumerate(((k_own, k_ref), (v_own, v_ref)))]
    for copy in loads[:4]:
        copy.start()
    for j in range(nmat):
        pltpu.make_async_copy(flow.at[j], full.at[j], w_sem.at[j]).start()

    def lay_rows(b):
        return lay.at[rows(b * own_rows, own_rows)]

    lay_x = rcopy(layer, lay_rows(me), lsem_s.at[0], lsem_r.at[0], to_x)
    lay_x_came = rcopy(layer, lay_rows(over), lsem_s.at[0], lsem_r.at[0], to_x)
    lay_c = rcopy(layer, lay_rows(me), lsem_s.at[1], lsem_r.at[1], to_c)
    lay_c_came = rcopy(layer, lay_rows(2 * x + 1 - c), lsem_s.at[1], lsem_r.at[1], to_c)
    lay_d = rcopy(lay_rows(over), lay_rows(over), lsem_s.at[2], lsem_r.at[2], to_c)
    lay_d_came = rcopy(layer, lay_rows(2 * (1 - x) + 1 - c), lsem_s.at[2], lsem_r.at[2], to_c)
    lay_own = pltpu.make_async_copy(layer, lay_rows(me), loc_sem.at[0])
    lay_x.start()
    lay_c.start()
    lay_own.start()

    order = tuple(p for k in range(ratio) for p in (4 + ratio + k, 4 + k)) + (3, 0, 1, 2)
    for s in range(2 * cap):
        slot_pick[s] = 0
    for j, p in enumerate(order):
        mine = owners[p]
        place_of = jnp.int32(0)
        for q in range(p):
            place_of += jnp.where(owners[q] == mine, 1, 0).astype(jnp.int32)
        slot = (mine % 2) * cap + jnp.minimum(place_of, cap - 1)
        for s in range(2 * cap):
            slot_pick[s] = jnp.where((mine // 2 == z) & (slot == s), j, slot_pick[s])

    def core_copy(j, src):
        return rcopy(src.at[rows((1 - c) * share, share), :], cin.at[j], cs.at[j], cr.at[j], to_c)

    def grad_of(j):
        if isinstance(j, int) and j >= 2 * ratio + 1:
            return gqkv.at[j - 2 * ratio - 1]
        if isinstance(j, int) and j == 2 * ratio:
            return full.at[3]
        return full.at[4 + j + 1 - 2 * (j % 2), pl.ds(0, 2 * share), :]

    def part(at, h):
        return rows(at * quarter + h * half, half)

    def y_copy(r):
        return rcopy(cin.at[r // 2, part(1 - y, r % 2), :], yi.at[r], ysd.at[r], yr.at[r], to_y)

    def right(r):
        return rcopy(yi.at[r], fr.at[r], sr.at[r], rl.at[r], device(z + 1, y, x, c))

    def left(r):
        return rcopy(cin.at[r // 2, part(y, r % 2), :], fl.at[r], sl.at[r], rr.at[r], device(z - 1, y, x, c))

    def stage1(r):
        j, h = r // 2, r % 2

        @pl.when(h == 0)
        def _():
            core_copy(j, gqkv.at[0]).wait_recv()

        def add(src):
            for at in (1 - y, y):
                value = (src[rows(c * share + at * quarter + h * half, half), :].astype(F32)
                         + cin[j, part(at, h), :].astype(F32))
                if at is y:
                    hold[r] = value
                else:
                    cin[j, part(at, h), :] = value.astype(BF16)

        @pl.when(j < 2 * ratio)
        def _():
            add(full.at[4 + j + 1 - 2 * (j % 2)])

        @pl.when(j == 2 * ratio)
        def _():
            add(full.at[3])

        @pl.when(j > 2 * ratio)
        def _():
            add(gqkv.at[j - 2 * ratio - 1])

        y_copy(r).start()

    def stage2(r):
        y_copy(r).wait_recv()
        hold[r] = hold[r] + yi[r].astype(F32)

    def flow_right(r):
        @pl.when(z == 0)
        def _():
            yi[r] = hold[r].astype(BF16)

        @pl.when(z > 0)
        def _():
            right(r).wait_recv()
            yi[r] = (hold[r] + fr[r].astype(F32)).astype(BF16)

        @pl.when(z < line - 1)
        def _():
            right(r).start()

    def flow_left(r):
        at = part(y, r % 2)

        @pl.when(z == line - 1)
        def _():
            cin[r // 2, at, :] = hold[r].astype(BF16)

        @pl.when(z < line - 1)
        def _():
            left(r).wait_recv()
            cin[r // 2, at, :] = (hold[r] + fl[r].astype(F32)).astype(BF16)

        @pl.when(z > 0)
        def _():
            left(r).start()

    def ranged(r, do_it):
        pl.when((r >= 0) & (r < nchunk))(functools.partial(do_it, r))

    lag = 3
    ticks = nchunk + lag + 2 * (line - 1)

    def tick(t):
        ranged(t, stage1)
        ranged(t - 2, stage2)
        ranged(t - lag - 2 * z, flow_right)
        ranged(t - lag - 2 * (line - 1 - z), flow_left)

    def ticking(start, stop):
        def body(t, carry):
            tick(t)
            return carry

        lax.fori_loop(start, stop, body, 0)

    position = lax.broadcasted_iota(jnp.int32, (8, LEN), 1)
    upper = (lax.broadcasted_iota(jnp.int32, (LEN, LEN), 0)
             <= lax.broadcasted_iota(jnp.int32, (LEN, LEN), 1)).astype(F32).astype(BF16)
    row_of = lax.broadcasted_iota(jnp.int32, (SPAN_ROWS, LEN), 0).astype(F32)
    for copy in loads[:4]:
        copy.wait()

    def cover(s, carry):
        seq = (2 * (s // per) + c) * per + s % per
        seen = jnp.zeros((8, LEN), F32)
        for n in range(spans.shape[1]):
            start, size = spans[seq, n, 0], spans[seq, n, 1]
            seen = jnp.where((position >= start) & (position < start + size), 1.0, seen)
        rank = dg(seen.astype(BF16), upper, NN)
        chosen = jnp.where((rank[0:1, :] - 1.0 == row_of) & (seen[0:1, :] > 0.0), 1.0, 0.0).astype(BF16)
        pick[s] = chosen
        at, span = rows(s * LEN, LEN), rows(s * SPAN_ROWS, SPAN_ROWS)
        hm[span, :] = dg(chosen, hid[at, :], NN).astype(BF16)
        gm[span, :] = dg(chosen, v_ref[at, :], NN).astype(BF16)
        return carry

    lax.fori_loop(0, nseq, cover, 0)

    for copy in loads[4:]:
        copy.start()

    for j in range(3):
        pltpu.make_async_copy(flow.at[j], full.at[j], w_sem.at[j]).wait()
    for i in range(per):
        at = rows((1 - x) * own_rows + i * LEN, LEN)
        k_ref[at, :] = dg(hid[at, :], full[1], NT).astype(BF16)
        v_ref[at, :] = (dg(hid[at, :], full[2], NT) + vecs[1:2, :]).astype(BF16)
    qm[...] = (dg(hm[...], full[0], NT) + vecs[0:1, :]).astype(BF16)
    for copy in loads[4:]:
        copy.wait()
    pairs = width // (2 * HDIM)
    left_half = lax.broadcasted_iota(jnp.int32, (SPAN_ROWS, 2 * HDIM), 1) < HDIM
    scale = HDIM ** -0.5

    def stacked(value):
        zero = jnp.zeros_like(value)
        return jnp.concatenate([jnp.where(left_half, value, zero), jnp.where(left_half, zero, value)], axis=0)

    def merged(value):
        return jnp.where(left_half, value[:SPAN_ROWS], value[SPAN_ROWS:])

    def places(i):
        s, pair = i // pairs, i % pairs
        return (rows(s * LEN, LEN), rows(s * SPAN_ROWS, SPAN_ROWS),
                pl.ds(pl.multiple_of(pair * (2 * HDIM), 2 * HDIM), 2 * HDIM))

    def attend(i, carry):
        at, span, lanes = places(i)
        scores = dg(stacked(qm[span, lanes]), k_ref[at, lanes], NT) * scale
        raised = jnp.exp(scores - jnp.max(scores, axis=-1, keepdims=True))
        value = (raised / jnp.sum(raised, axis=-1, keepdims=True)).astype(BF16)
        probs[i] = value
        ctx[span, lanes] = merged(dg(value, v_ref[at, lanes], NN)).astype(BF16)
        return carry

    lax.fori_loop(0, nseq * pairs, attend, 0)
    for j in range(3, nmat):
        pltpu.make_async_copy(flow.at[j], full.at[j], w_sem.at[j]).wait()
    h1 = hm[...].astype(F32) + dg(ctx[...], full[3], NN) + vecs[2:3, :]
    first, normed, inverse = layer_norm(h1, vecs[4 + ratio:5 + ratio, :], vecs[5 + ratio:6 + ratio, :])
    n1[...] = normed
    inv1[...] = inverse
    low[...] = first.astype(BF16)
    acc[...] = first + vecs[3 + ratio:4 + ratio, :]

    def feed(k, carry):
        up = dg(low[...], full[4 + 2 * k], NT) + vecs[pl.ds(3 + k, 1), :]
        cdf = 0.5 * (1.0 + lax.erf(up * 2.0 ** (-0.5)))
        active = (up * cdf).astype(BF16)
        act[k] = active
        slope[k] = (cdf + up * (jnp.exp(-0.5 * up * up) * (2.0 * jnp.pi) ** (-0.5))).astype(BF16)
        acc[...] = acc[...] + dg(active, full[5 + 2 * k], NN)
        return carry

    lax.fori_loop(0, ratio, feed, 0)
    _, normed, inverse = layer_norm(acc[...], vecs[6 + ratio:7 + ratio, :], vecs[7 + ratio:8 + ratio, :])
    given = gm[...].astype(F32)
    gvec[6 + ratio:7 + ratio, :] = column_sum(given * normed)
    gvec[7 + ratio:8 + ratio, :] = column_sum(given)
    back = norm_back(given, normed, inverse, vecs[6 + ratio:7 + ratio, :])
    acc[...] = back
    df[...] = back.astype(BF16)
    gvec[3 + ratio:4 + ratio, :] = column_sum(back.astype(BF16).astype(F32))
    halves = pl.ds(pl.multiple_of(x * 2 * share, 128), 2 * share)

    def feed_back(k, carry):
        d_up = (dg(df[...], full[5 + 2 * k], NT) * slope[k].astype(F32)).astype(BF16)
        gvec[pl.ds(3 + k, 1), :] = column_sum(d_up.astype(F32))
        acc[...] = acc[...] + dg(d_up, full[4 + 2 * k], NN)
        act_k = act[k, :, halves]
        act[k] = d_up
        full[5 + 2 * k, pl.ds(0, 2 * share), :] = dg(act_k, df[...], TN).astype(BF16)
        core_copy(2 * k, full.at[5 + 2 * k]).start()
        full[4 + 2 * k, pl.ds(0, 2 * share), :] = dg(act[k, :, halves], low[...], TN).astype(BF16)
        core_copy(2 * k + 1, full.at[4 + 2 * k]).start()
        tick(k)
        return carry

    lax.fori_loop(0, ratio, feed_back, 0)
    done = ratio
    gvec[4 + ratio:5 + ratio, :] = column_sum(acc[...] * n1[...])
    gvec[5 + ratio:6 + ratio, :] = column_sum(acc[...])
    back = norm_back(acc[...], n1[...], inv1[...], vecs[4 + ratio:5 + ratio, :])
    acc[...] = back
    da = back.astype(BF16)
    gvec[2:3, :] = column_sum(da.astype(F32))
    df[...] = da
    low[...] = dg(da, full[3], NT).astype(BF16)
    full[3, pl.ds(0, 2 * share), :] = dg(ctx[:, halves], da, TN).astype(BF16)
    core_copy(2 * ratio, full.at[3]).start()
    tick(done)
    done += 1

    def attend_back(i, carry):
        at, span, lanes = places(i)
        d_two = stacked(low[span, lanes])
        given = probs[i]
        value = given.astype(F32)
        keys = k_ref[at, lanes]
        d_probs = dg(d_two, v_ref[at, lanes], NT)
        mean = jnp.sum(value * d_probs, axis=-1, keepdims=True)
        ds = (value * (d_probs - mean)).astype(BF16)
        dq[span, lanes] = (merged(dg(ds, keys, NN)) * scale).astype(BF16)
        k_ref[at, lanes] = (dg(ds, stacked(qm[span, lanes]), TN) * scale).astype(BF16)
        v_ref[at, lanes] = dg(given, d_two, TN).astype(BF16)
        return carry

    every = 3
    for i in range(0, nseq * pairs, every):
        lax.fori_loop(i, min(i + every, nseq * pairs), attend_back, 0)
        tick(done)
        done += 1
    gvec[0:1, :] = column_sum(dq[...].astype(F32))
    gqkv[0] = dg(dq[:, halves], hm[...], TN).astype(BF16)
    core_copy(2 * ratio + 1, gqkv.at[0]).start()
    for which, src in ((1, k_ref), (2, v_ref)):
        def some(i, carry, src=src):
            at = rows(i * LEN, LEN)
            return carry + dg(src[at, halves], hid[at, :], TN)

        gqkv[which] = lax.fori_loop(0, nseq, some, jnp.zeros((2 * share, width), F32)).astype(BF16)
        core_copy(2 * ratio + 1 + which, gqkv.at[which]).start()
        tick(done)
        done += 1

    def sum_v(i, carry):
        return carry + column_sum(v_ref[rows(i * LEN, LEN), :].astype(F32))

    gvec[1:2, :] = lax.fori_loop(0, nseq, sum_v, jnp.zeros((1, width), F32))

    def vec_copy(k, who_to):
        return rcopy(gvec, vin.at[k], vs.at[k], vr.at[k], who_to)

    vec_copy(0, to_c).start()
    qm[...] = (acc[...] + dg(dq[...], full[0], NN)).astype(BF16)
    vec_copy(0, to_c).wait()
    gvec[...] = gvec[...] + vin[0]
    vec_copy(1, to_y).start()

    def gin_rows(s, core):
        return gin.at[rows((2 * (s // per) + core) * own_rows + (s % per) * LEN, LEN)]

    def gin_copy(s):
        return rcopy(hid.at[rows(s * LEN, LEN)], gin_rows(s, c), gsem_s.at[s], gsem_r.at[s], to_c)

    def gin_came(s):
        return rcopy(hid.at[rows(s * LEN, LEN)], gin_rows(s, 1 - c), gsem_s.at[s], gsem_r.at[s], to_c)

    def gin_own(s):
        return pltpu.make_async_copy(hid.at[rows(s * LEN, LEN)], gin_rows(s, c), loc_sem.at[1 + s])

    base = done

    def spread(s, carry):
        at, span = rows(s * LEN, LEN), rows(s * SPAN_ROWS, SPAN_ROWS)
        total = dg(k_ref[at, :], full[1], NN) + dg(v_ref[at, :], full[2], NN) + dg(pick[s], qm[span, :], TN)
        hid[at, :] = total.astype(BF16)
        gin_copy(s).start()
        gin_own(s).start()
        tick(base + s)
        return carry

    lax.fori_loop(0, nseq, spread, 0)
    done = base + nseq
    vec_copy(1, to_y).wait()
    vz[z] = gvec[...] + vin[1]

    def vec_flow(step, send):
        def one(near, ok_send, ok_recv, direction, slot_out, slot_in):
            copy = rcopy(vz.at[slot_out], vz.at[slot_out], vzs.at[direction, step], vzr.at[slot_out], near)
            if send:
                pl.when(ok_send)(copy.start)
            else:
                came = rcopy(vz.at[slot_in], vz.at[slot_in], vzs.at[direction, step], vzr.at[slot_in], near)
                pl.when(ok_send)(copy.wait_send)
                pl.when(ok_recv)(came.wait_recv)

        one(device(jnp.minimum(z + 1, line - 1), y, x, c), (z < line - 1) & (z - step >= 0), z - step - 1 >= 0, 0,
            jnp.maximum(z - step, 0), jnp.maximum(z - step - 1, 0))
        one(device(jnp.maximum(z - 1, 0), y, x, c), (z > 0) & (z + step <= line - 1), z + step + 1 <= line - 1, 1,
            jnp.minimum(z + step, line - 1), jnp.minimum(z + step + 1, line - 1))

    for step in range(line - 1):
        vec_flow(step, True)
        if done < ticks:
            tick(done)
            done += 1
        vec_flow(step, False)
    ticking(done, ticks)
    total = vz[0]
    for k in range(1, line):
        total = total + vz[k]
    vec_out[...] = total

    def piece_total(j, h):
        r = 2 * j + h
        value = hold[r]
        value = value + jnp.where(z > 0, fr[r].astype(F32), 0.0)
        return value + jnp.where(z < line - 1, fl[r].astype(F32), 0.0)

    deliver = rcopy(do, di, dsem.at[0], dsem.at[1], to_y)
    for s in range(cap):
        for h in range(2):
            do[s, pl.ds(h * half, half), :] = piece_total(slot_pick[(1 - y) * cap + s], h).astype(BF16)
    deliver.start()
    for s in range(cap):
        for h in range(2):
            sg[s, part(y, h), :] = piece_total(slot_pick[y * cap + s], h)
    lay_x_came.wait_recv()
    lay_d.start()

    def finish(r, carry):
        y_copy(r).wait_send()

        @pl.when(z < line - 1)
        def _():
            right(r).wait_send()

        @pl.when(z > 0)
        def _():
            left(r).wait_send()

        return carry

    lax.fori_loop(0, nchunk, finish, 0)

    def last(j, carry):
        core_copy(j, gqkv.at[0]).wait_send()
        return carry

    lax.fori_loop(0, nmat, last, 0)
    for s in range(nseq):
        gin_copy(s).wait_send()
        gin_came(s).wait_recv()
        gin_own(s).wait()
    lay_x.wait_send()
    lay_c.wait_send()
    lay_c_came.wait_recv()
    lay_own.wait()
    lay_d.wait_send()
    lay_d_came.wait_recv()
    deliver.wait_recv()
    for s in range(cap):
        sg[s, rows((1 - y) * quarter, quarter), :] = di[s].astype(F32)
    deliver.wait_send()


def backward(owners, spans, vecs, flow, hidden, incoming, layer, k_own, v_own, line, cap):
    nmat, width, _ = flow.shape
    share = width // 4
    own_rows = layer.shape[0]
    both = 2 * own_rows
    nseq = both // LEN
    span_rows = nseq * SPAN_ROWS
    ratio = (nmat - 4) // 2
    quarter, half = share // 2, share // 4
    n = 2 * nmat
    pairs = width // (2 * HDIM)
    dma = pltpu.SemaphoreType.DMA
    vmem = pl.BlockSpec(memory_space=pltpu.VMEM)
    smem = pl.BlockSpec(memory_space=pltpu.SMEM)
    hbm = pl.BlockSpec(memory_space=pl.ANY)
    whole = jax.ShapeDtypeStruct(hidden.shape, BF16)

    def lows(*shape):
        return pltpu.VMEM(shape, BF16)

    def wide(*shape):
        return pltpu.VMEM(shape, F32)

    return pl.pallas_call(
        functools.partial(backward_kernel, line, nmat, cap),
        out_shape=(jax.ShapeDtypeStruct((cap, share, width), F32),
                   jax.ShapeDtypeStruct(vecs.shape, F32), whole, whole),
        in_specs=[smem, smem, vmem, hbm, hbm, hbm, hbm, hbm, hbm],
        out_specs=(vmem, vmem, hbm, hbm),
        scratch_shapes=[
            lows(nmat, width, width), lows(both, width), lows(both, width), lows(both, width),
            lows(nseq, SPAN_ROWS, LEN),
            lows(nseq * pairs, 2 * SPAN_ROWS, LEN),
            lows(span_rows, width), lows(span_rows, width), lows(span_rows, width), lows(span_rows, width),
            wide(span_rows, width), wide(span_rows, 1), lows(span_rows, width), wide(span_rows, width),
            lows(ratio, span_rows, width), lows(ratio, span_rows, width),
            lows(span_rows, width), lows(span_rows, width), lows(3, 2 * share, width),
            wide(*vecs.shape), wide(2, *vecs.shape), wide(line, *vecs.shape),
            lows(nmat, share, width), wide(n, half, width), lows(n, half, width), lows(n, half, width),
            lows(n, half, width), lows(cap, quarter, width), lows(cap, quarter, width),
            pltpu.SMEM((2 * cap,), jnp.int32),
            dma((nmat,)), dma((6,)), dma((3,)), dma((3,)), dma((nseq,)), dma((nseq,)), dma((1 + nseq,)),
            dma((nmat,)), dma((nmat,)),
        ] + [dma((n,))] * 6 + [dma((2,)), dma((2,)), dma((2,)), dma((2, line)), dma((line,))],
        name="backward",
        compiler_params=pltpu.CompilerParams(
            collective_id=2, has_side_effects=True, vmem_limit_bytes=62 * 1024 * 1024),
    )(owners, spans, vecs, flow, hidden, incoming, layer, k_own, v_own)


STEP = 10
MATRIX_RATE = 0.03
VECTOR_RATE = 0.25
BETA_ONE = 0.5
BETA_TWO = 0.5
DECAY = 0.01
ADAM_EPS = 1e-08


def adamw(weight, moment_one, moment_two, grad, step_rate):
    new_one = BETA_ONE * moment_one + (1.0 - BETA_ONE) * grad
    new_two = BETA_TWO * moment_two + (1.0 - BETA_TWO) * grad * grad
    corr_one = 1.0 - BETA_ONE**STEP
    corr_two = 1.0 - BETA_TWO**STEP
    direction = new_one / corr_one / (jnp.sqrt(new_two / corr_two) + ADAM_EPS)
    return (weight - step_rate * (direction + DECAY * weight), new_one, new_two)


def on_device(line, hidden_in, incoming, spans, owners, vectors, vec_one, vec_two, master_slots, slot_one, slot_two):
    cap, width, share = master_slots.shape
    nmat = owners.shape[0]
    ratio = (nmat - 4) // 2

    def regroup(value, first, second):
        rows = value[3:3 + ratio].reshape(first, second, share).transpose(1, 0, 2).reshape(ratio, width)
        return jnp.concatenate([value[:3], rows, value[3 + ratio:]], axis=0)

    vecs = regroup(vectors, 4, ratio)
    flow, layer, k_own, v_own = forward(owners, jnp.transpose(master_slots, (0, 2, 1)), hidden_in, vecs, line)
    slot_grad, vec_grad, layer_out, input_grad = backward(
        owners, spans, vecs, flow, hidden_in, incoming, layer, k_own, v_own, line, cap)
    new_vec = adamw(vectors, vec_one, vec_two, regroup(vec_grad, ratio, 4), VECTOR_RATE)
    slot_grad = jnp.transpose(slot_grad, (0, 2, 1))
    held = jnp.sum((owners == lax.axis_index("dp")).astype(jnp.int32))
    occupied = (jnp.arange(cap) < held).astype(F32)[:, None, None]
    new_slots = adamw(master_slots, slot_one, slot_two, slot_grad, MATRIX_RATE)
    return (layer_out, input_grad) + new_vec + tuple(v * occupied for v in new_slots)


def solution(mesh):
    line = mesh.shape["dp"] // 2
    rows, slots = P("dp", None), P("dp", None, "mp")
    return jax.shard_map(
        functools.partial(on_device, line),
        mesh=mesh,
        in_specs=(rows, rows, P("dp", None, None), P(), P(), P(), P(), slots, slots, slots),
        out_specs=(rows, rows, P(), P(), P(), slots, slots, slots),
        check_vma=False,
    )
```

```python
import functools
import jax
import jax.numpy as jnp
from jax import lax
from jax.sharding import PartitionSpec as P
from jax.experimental import pallas as pl
from jax.experimental.pallas import tpu as pltpu

MESH = pl.DeviceIdType.MESH
BF16 = jnp.bfloat16
F32 = jnp.float32
LN_EPS = 1e-12
HDIM = 64
LEN = 512
NT = (((1,), (1,)), ((), ()))
NN = (((1,), (0,)), ((), ()))
TN = (((0,), (0,)), ((), ()))


def dg(left, right, dims):
    return lax.dot_general(left, right, dims, preferred_element_type=F32)


def flow_order(nmat):
    ratio = (nmat - 4) // 2
    return (0, 1, 2, 3) + tuple(p for k in range(ratio) for p in (4 + k, 4 + ratio + k))


def layer_norm(value, gain, shift):
    center = value - jnp.mean(value, axis=-1, keepdims=True)
    inverse = lax.rsqrt(jnp.mean(center * center, axis=-1, keepdims=True) + LN_EPS)
    normed = center * inverse
    return normed * gain + shift, normed, inverse


def gelu(value):
    return 0.5 * value * (1.0 + lax.erf(value * 2.0 ** (-0.5)))


def place():
    dp, mp = lax.axis_index("dp"), lax.axis_index("mp")
    return dp // 2, dp % 2, mp // 2, mp % 2


def device(z, y, x, c):
    return (z * 2 + y, x * 2 + c)


def greet(line):
    z, y, x, c = place()
    bar = pltpu.get_barrier_semaphore()
    for who in (device(z, 1 - y, x, c), device(z, y, 1 - x, c), device(z, y, x, 1 - c)):
        pl.semaphore_signal(bar, inc=1, device_id=who, device_id_type=MESH)

    @pl.when(z > 0)
    def _():
        pl.semaphore_signal(bar, inc=1, device_id=device(z - 1, y, x, c), device_id_type=MESH)

    @pl.when(z < line - 1)
    def _():
        pl.semaphore_signal(bar, inc=1, device_id=device(z + 1, y, x, c), device_id_type=MESH)

    peers = 3 + jnp.where(z > 0, 1, 0) + jnp.where(z < line - 1, 1, 0)
    pl.semaphore_wait(bar, peers.astype(jnp.int32))


def rcopy(src, dst, send, recv, who):
    return pltpu.make_async_remote_copy(
        src_ref=src, dst_ref=dst, send_sem=send, recv_sem=recv, device_id=who, device_id_type=MESH
    )


SPAN_ROWS = 96


def rows(start, size):
    return pl.ds(pl.multiple_of(start, 16), size)


def column_sum(value):
    return jnp.sum(value, axis=0, keepdims=True)


def regroup(src, dst, ratio, share):
    dst[...] = src[...]
    for j in range(ratio):
        for k in range(ratio):
            dst[3 + k:4 + k, j * share:(j + 1) * share] = src[3 + j:4 + j, k * share:(k + 1) * share]


def norm_back(grad, normed, inverse, gain):
    scaled = grad * gain
    first = jnp.mean(scaled, axis=-1, keepdims=True)
    second = jnp.mean(scaled * normed, axis=-1, keepdims=True)
    return inverse * (scaled - first - normed * second)


def stacked(value, left_half):
    zero = jnp.zeros_like(value)
    return jnp.concatenate([jnp.where(left_half, value, zero), jnp.where(left_half, zero, value)], axis=0)


def merged(value, left_half):
    size = left_half.shape[0]
    return jnp.where(left_half, value[:size], value[size:])


def forward_kernel(line, nmat, cap, owners, spans, slots_in, hidden, incoming, vectors,
                   out, layer_out, k_out, v_out, pick_out, probs_out, hm_out, qm_out, ctx_out, low_out,
                   act_out, slope_out, n1_out, inv_out, df_out, dh_out, gvec,
                   vecs, full, slots, ys, stage, fr, fl, hid, q_ref, k_ref, v_ref, ctx, low, acc,
                   pick, probs, hm, gm, qm, act, slope, n1, inv1, df, zo, idx,
                   in_sem, out_sem, slot_send, slot_recv, sr, rl, sl, rr, xs, xr, ysd, yr, ds, dr, cs, cr, loc):
    share = slots.shape[1]
    quarter = share // 2
    half = quarter // 2
    nchunk = 2 * nmat
    z, y, x, c = place()
    me = 2 * x + c
    over = 2 * (1 - x) + c
    to_y, to_x, to_c = device(z, 1 - y, x, c), device(z, y, 1 - x, c), device(z, y, x, 1 - c)
    greet(line)
    ratio = (nmat - 4) // 2
    order = flow_order(nmat)
    own_rows = q_ref.shape[0]
    width = vecs.shape[1]
    regroup(vectors, vecs, ratio, share)
    per = own_rows // LEN
    nseq = 2 * per

    def block_copy(src, dst, b, sem):
        return pltpu.make_async_copy(
            src.at[rows((2 * b + c) * own_rows, own_rows)], dst.at[pl.ds(b * own_rows, own_rows)], sem)

    slot_loads = [pltpu.make_async_copy(slots_in.at[s], acc.at[pl.ds(s * share, share)], in_sem.at[4 + s])
                  for s in range(cap)]
    loads = [block_copy(hidden, hid, b, in_sem.at[b]) for b in range(2)]
    loads += [block_copy(incoming, v_ref, b, in_sem.at[2 + b]) for b in range(2)]
    for copy in slot_loads + loads:
        copy.start()

    def slot_copy(s):
        return rcopy(
            slots.at[s, pl.ds(pl.multiple_of((1 - y) * quarter, 16), quarter), :],
            ys[s].at[y], slot_send.at[s], slot_recv.at[s], to_y)

    for s in range(cap):
        slot_loads[s].wait()
        slots[s] = acc[pl.ds(s * share, share), :].astype(BF16)
        slot_copy(s).start()
        ys[s][y] = slots[s, pl.ds(pl.multiple_of(y * quarter, 16), quarter), :]
    for j, p in enumerate(order):
        mine = owners[p]
        place_of = jnp.int32(0)
        for q in range(p):
            place_of += jnp.where(owners[q] == mine, 1, 0).astype(jnp.int32)
        zo[j] = mine // 2
        idx[j] = (mine % 2) * cap + jnp.minimum(place_of, cap - 1)

    def piece_rows(block, yy, h):
        return pl.ds(pl.multiple_of(block * share + yy * quarter + h * half, 16), half)

    def own(r):
        at = pl.ds(pl.multiple_of((r % 2) * half, 16), half)
        slot, half_of = idx[r // 2] % cap, idx[r // 2] // cap
        stage[...] = ys[0][half_of, at, :]
        for s in range(1, cap):
            @pl.when(r // 2 >= s)
            def _():
                stage[...] = jnp.where(slot == s, ys[s][half_of, at, :], stage[...])

        return stage[...]

    def right(r):
        return rcopy(fr.at[r], fr.at[r], sr.at[r], rl.at[r], device(z + 1, y, x, c))

    def left(r):
        return rcopy(fl.at[r], fl.at[r], sl.at[r], rr.at[r], device(z - 1, y, x, c))

    def x_copy(f):
        at = full.at[f // 2, piece_rows(me, y, f % 2), :]
        return rcopy(at, at, xs.at[f], xr.at[f], to_x)

    def x_came(f):
        at = full.at[f // 2, piece_rows(over, y, f % 2), :]
        return rcopy(at, at, xs.at[f], xr.at[f], to_x)

    def y_copy(f):
        at = full.at[f // 2, piece_rows(me, y, f % 2), :]
        return rcopy(at, at, ysd.at[f], yr.at[f], to_y)

    def y_came(f):
        at = full.at[f // 2, piece_rows(me, 1 - y, f % 2), :]
        return rcopy(at, at, ysd.at[f], yr.at[f], to_y)

    def diag_x(f):
        at = full.at[f // 2, piece_rows(me, 1 - y, f % 2), :]
        return rcopy(at, at, ds.at[f], dr.at[f], to_x)

    def diag_y(f):
        at = full.at[f // 2, piece_rows(over, y, f % 2), :]
        return rcopy(at, at, ds.at[f], dr.at[f], to_y)

    def diag_came(f):
        at = full.at[f // 2, piece_rows(over, 1 - y, f % 2), :]
        return rcopy(at, at, ds.at[f], dr.at[f], to_x)

    def core_copy(p, k):
        block = jnp.where(k == 0, me, over) if not isinstance(k, int) else (me, over)[k]
        at = full.at[p, pl.ds(pl.multiple_of(block * share, 16), share), :]
        return rcopy(at, at, cs.at[p, k], cr.at[p, k], to_c)

    def core_came(p, k):
        block = (2 * x + 1 - c, 2 * (1 - x) + 1 - c)[k]
        at = full.at[p, pl.ds(pl.multiple_of(block * share, 16), share), :]
        return rcopy(at, at, cs.at[p, k], cr.at[p, k], to_c)

    def keep(p):
        return pltpu.make_async_copy(full.at[p], out.at[p], loc.at[p])

    lag0 = 2 * (line - 1)
    lag1 = lag0 + 3
    lag2 = lag1 + 3
    lag3 = lag2 + 1

    def slot_came(s):
        rcopy(slots.at[s, pl.ds(pl.multiple_of((1 - y) * quarter, 16), quarter), :],
              ys[s].at[1 - y], slot_send.at[s], slot_recv.at[s], to_y).wait_recv()

    def tick(t):
        for s in range(cap):
            pl.when(t == 2 * s)(functools.partial(slot_came, s))

        r = t - 2 * z

        @pl.when((r >= 0) & (r < nchunk))
        def _():
            @pl.when(z == 0)
            def _():
                fr[r] = own(r)

            @pl.when(z > 0)
            def _():
                right(r).wait_recv()
                fr[r] = jnp.where(zo[r // 2] == z, own(r), fr[r])

            @pl.when(z < line - 1)
            def _():
                right(r).start()

        l = t - 2 * (line - 1 - z)

        @pl.when((l >= 0) & (l < nchunk))
        def _():
            @pl.when(z == line - 1)
            def _():
                fl[l] = own(l)

            @pl.when(z < line - 1)
            def _():
                left(l).wait_recv()
                fl[l] = jnp.where(zo[l // 2] == z, own(l), fl[l])

            @pl.when(z > 0)
            def _():
                left(l).start()

        f = t - lag0

        @pl.when((f >= 0) & (f < nchunk))
        def _():
            full[f // 2, piece_rows(me, y, f % 2), :] = jnp.where(zo[f // 2] <= z, fr[f], fl[f])
            x_copy(f).start()
            y_copy(f).start()

        g = t - lag1

        @pl.when((g >= 0) & (g < nchunk))
        def _():
            x_came(g).wait_recv()
            y_came(g).wait_recv()

            @pl.when(g % 2 == 0)
            def _():
                diag_x(g).start()

            @pl.when(g % 2 == 1)
            def _():
                diag_y(g).start()

        e = t - lag2

        @pl.when((e >= 0) & (e < nchunk))
        def _():
            diag_came(e).wait_recv()

            @pl.when(e % 2 == 1)
            def _():
                for k in range(2):
                    core_copy(e // 2, k).start()

        w = t - lag3

        @pl.when((w >= 0) & (w < nchunk) & (w % 2 == 1))
        def _():
            for k in range(2):
                core_came(w // 2, k).wait_recv()
            keep(w // 2).start()

    ticks = nchunk + lag3

    def ticking(start, count):
        def body(i, carry):
            tick(start + i)
            return carry

        if count > 0:
            lax.fori_loop(0, count, body, 0)

    position = lax.broadcasted_iota(jnp.int32, (8, LEN), 1)
    row_of = lax.broadcasted_iota(jnp.int32, (SPAN_ROWS, LEN), 0).astype(F32)

    def cover(s, carry):
        seq = (2 * (s // per) + c) * per + s % per
        seen = jnp.zeros((8, LEN), F32)
        for n in range(spans.shape[2]):
            start, size = spans[0, seq, n], spans[1, seq, n]
            seen = jnp.where((position >= start) & (position < start + size), 1.0, seen)
        upper = (lax.broadcasted_iota(jnp.int32, (LEN, LEN), 0)
                 <= lax.broadcasted_iota(jnp.int32, (LEN, LEN), 1)).astype(F32).astype(BF16)
        rank = dg(seen.astype(BF16), upper, NN)
        chosen = jnp.where((rank[0:1, :] - 1.0 == row_of) & (seen[0:1, :] > 0.0), 1.0, 0.0).astype(BF16)
        pick[s] = chosen
        at, span = rows(s * LEN, LEN), rows(s * SPAN_ROWS, SPAN_ROWS)
        hm[span, :] = dg(chosen, hid[at, :], NN).astype(BF16)
        gm[span, :] = dg(chosen, v_ref[at, :], NN).astype(BF16)
        tick(nseq + s)
        return carry

    ticking(0, nseq)
    for copy in loads:
        copy.wait()
    lax.fori_loop(0, nseq, cover, 0)
    kept = []

    def keep_out(src, dst):
        copy = pltpu.make_async_copy(src, dst, out_sem.at[len(kept)])
        copy.start()
        kept.append(copy)

    keep_out(pick, pick_out)
    keep_out(hm, hm_out)

    now = lag3 + 2
    ticking(2 * nseq, now - 2 * nseq)
    for i in range(per):
        block = hid[rows(x * own_rows + i * LEN, LEN), :]
        q_ref[pl.ds(i * LEN, LEN), :] = (
            (dg(block, full[0], NT) + vecs[0:1, :]).astype(BF16) * jnp.asarray(HDIM ** -0.5, BF16))
    tick(now)
    qm[...] = (dg(hm[...], full[0], NT) + vecs[0:1, :]).astype(BF16)
    keep_out(qm, qm_out)
    tick(now + 1)
    now += 2

    def project_k(s, carry):
        at = rows(s * LEN, LEN)
        k_ref[at, :] = dg(hid[at, :], full[1], NT).astype(BF16)
        pl.when(s % 2 == 1)(lambda: tick(now_k + s // 2))
        return carry

    def project_v(s, carry):
        at = rows(s * LEN, LEN)
        v_ref[at, :] = (dg(hid[at, :], full[2], NT) + vecs[1:2, :]).astype(BF16)
        pl.when(s % 2 == 1)(lambda: tick(now_v + s // 2))
        return carry

    now_k = now
    lax.fori_loop(0, nseq, project_k, 0)
    keep_out(k_ref, k_out)
    now_v = now_k + nseq // 2
    lax.fori_loop(0, nseq, project_v, 0)
    keep_out(v_ref, v_out)
    now = now_v + nseq // 2

    pairs = width // (2 * HDIM)
    left_half = lax.broadcasted_iota(jnp.int32, (LEN, 2 * HDIM), 1) < HDIM
    ones = jnp.ones((LEN, 2 * HDIM), BF16)

    def lanes_of(pair):
        return pl.ds(pl.multiple_of(pair * (2 * HDIM), 2 * HDIM), 2 * HDIM)

    def attend(i):
        at, lanes = rows((i // pairs) * LEN, LEN), lanes_of(i % pairs)
        both = rows(x * own_rows + (i // pairs) * LEN, LEN)
        q_blk, k_blk = q_ref[at, lanes], k_ref[both, lanes]
        v_blk = jnp.concatenate([v_ref[both, lanes], ones], axis=1)
        mixed = []
        for h in range(2):
            q_one = jnp.where(left_half if h == 0 else ~left_half, q_blk, jnp.zeros_like(q_blk))
            scores = dg(q_one, k_blk, NT)
            raised = jnp.exp(scores - jnp.max(scores, axis=-1, keepdims=True)).astype(BF16)
            sums = dg(raised, v_blk, NN)
            mixed.append(sums[:, :2 * HDIM] / sums[:, 2 * HDIM:])
        ctx[at, lanes] = jnp.where(left_half, mixed[0], mixed[1]).astype(BF16)

    group = 3

    def attend_step(i, carry):
        for j in range(group):
            attend(i * group + j)
        tick(now + i)
        return carry

    count = per * pairs // group
    lax.fori_loop(0, count, attend_step, 0)
    now += count

    left_span = lax.broadcasted_iota(jnp.int32, (SPAN_ROWS, 2 * HDIM), 1) < HDIM
    scale = HDIM ** -0.5

    def attend_span(i):
        s, lanes = i // pairs, lanes_of(i % pairs)
        at, span = rows(s * LEN, LEN), rows(s * SPAN_ROWS, SPAN_ROWS)
        scores = dg(stacked(qm[span, lanes], left_span), k_ref[at, lanes], NT) * scale
        raised = jnp.exp(scores - jnp.max(scores, axis=-1, keepdims=True))
        value = (raised / jnp.sum(raised, axis=-1, keepdims=True)).astype(BF16)
        probs[i] = value
        ctx[rows(own_rows + s * SPAN_ROWS, SPAN_ROWS), lanes] = merged(
            dg(value, v_ref[at, lanes], NN), left_span).astype(BF16)

    span_group = pairs

    def span_step(i, carry):
        for j in range(span_group):
            attend_span(i * span_group + j)
        tick(now + i)
        return carry

    lax.fori_loop(0, nseq, span_step, 0)
    now += nseq
    keep_out(probs, probs_out)
    span_rows = nseq * SPAN_ROWS
    all_rows = own_rows + span_rows
    spanned = pl.ds(own_rows, span_rows)
    keep_out(ctx.at[spanned], ctx_out)

    def mix(residual, at):
        h1 = residual.astype(F32) + dg(ctx[at, :], full[3], NN) + vecs[2:3, :]
        value, normed, inverse = layer_norm(h1, vecs[4 + ratio:5 + ratio, :], vecs[5 + ratio:6 + ratio, :])
        low[at, :] = value.astype(BF16)
        acc[at, :] = value + vecs[3 + ratio:4 + ratio, :]
        return normed, inverse

    for i in range(per):
        mix(hid[rows(x * own_rows + i * LEN, LEN), :], pl.ds(i * LEN, LEN))
    normed, inverse = mix(hm[...], spanned)
    n1[...] = normed
    inv1[...] = jnp.broadcast_to(inverse, inv1.shape)
    keep_out(n1, n1_out)
    keep_out(inv1, inv_out)
    keep_out(low.at[spanned], low_out)
    tick(now)
    now += 1

    tile = all_rows // 2
    ready = [lag3 + 2 * (5 + 2 * k) + 2 for k in range(ratio)]
    for k in range(ratio):
        for i in range(2):
            if i == 0:
                ticking(now, max(0, ready[k] - now))
                now = max(now, ready[k])
            at = pl.ds(i * tile, tile)
            up = dg(low[at, :], full[4 + 2 * k], NT) + vecs[3 + k:4 + k, :]
            cdf = 0.5 * (1.0 + lax.erf(up * 2.0 ** (-0.5)))
            active = (up * cdf).astype(BF16)
            acc[at, :] = acc[at, :] + dg(active, full[5 + 2 * k], NN)
            if i == 1:
                up, cdf = up[tile - span_rows:], cdf[tile - span_rows:]
                act[k] = active[tile - span_rows:]
                slope[k] = (cdf + up * (jnp.exp(-0.5 * up * up) * (2.0 * jnp.pi) ** (-0.5))).astype(BF16)
            if now < ticks:
                tick(now)
                now += 1
    ticking(now, max(0, ticks - now))
    keep_out(act, act_out)
    keep_out(slope, slope_out)

    _, normed, inverse = layer_norm(
        acc[spanned, :], vecs[6 + ratio:7 + ratio, :], vecs[7 + ratio:8 + ratio, :])
    given = gm[...].astype(F32)
    gvec[...] = jnp.zeros_like(gvec)
    gvec[6 + ratio:7 + ratio, :] = column_sum(given * normed)
    gvec[7 + ratio:8 + ratio, :] = column_sum(given)
    back = norm_back(given, normed, inverse, vecs[6 + ratio:7 + ratio, :])
    df[...] = back.astype(BF16)
    gvec[3 + ratio:4 + ratio, :] = column_sum(back.astype(BF16).astype(F32))
    acc[spanned, :] = back
    keep_out(df, df_out)
    keep_out(acc.at[spanned], dh_out)
    for i in range(per):
        at = pl.ds(i * LEN, LEN)
        q_ref[at, :] = layer_norm(
            acc[at, :], vecs[6 + ratio:7 + ratio, :], vecs[7 + ratio:8 + ratio, :])[0].astype(BF16)
    keep_out(q_ref, layer_out)
    for copy in kept:
        copy.wait()

    def finish(r, carry):
        @pl.when(z < line - 1)
        def _():
            right(r).wait_send()

        @pl.when(z > 0)
        def _():
            left(r).wait_send()

        x_copy(r).wait_send()
        y_copy(r).wait_send()
        diag_came(r).wait_send()
        return carry

    lax.fori_loop(0, nchunk, finish, 0)

    def last(p, carry):
        for k in range(2):
            core_copy(p, k).wait_send()
        keep(p).wait()
        return carry

    lax.fori_loop(0, nmat, last, 0)
    for s in range(cap):
        slot_copy(s).wait_send()


def forward(owners, spans, slots, hidden, incoming, vecs, line):
    cap, share, width = slots.shape
    nmat = owners.shape[0]
    ratio = (nmat - 4) // 2
    own_rows = hidden.shape[0] // 4
    quarter, half = share // 2, share // 4
    n = 2 * nmat
    nseq = 2 * own_rows // LEN
    span_rows = nseq * SPAN_ROWS
    pairs = width // (2 * HDIM)
    dma = pltpu.SemaphoreType.DMA
    vmem = pl.BlockSpec(memory_space=pltpu.VMEM)
    smem = pl.BlockSpec(memory_space=pltpu.SMEM)
    hbm = pl.BlockSpec(memory_space=pl.ANY)

    def lows(*shape):
        return jax.ShapeDtypeStruct(shape, BF16)

    def wide(*shape):
        return jax.ShapeDtypeStruct(shape, F32)

    own, both, span = lows(own_rows, width), lows(2 * own_rows, width), lows(span_rows, width)
    outs = (lows(nmat, 4 * share, width), own, both, both, lows(nseq, SPAN_ROWS, LEN),
            lows(nseq * pairs, 2 * SPAN_ROWS, LEN), span, span, span, span,
            lows(ratio, span_rows, width), lows(ratio, span_rows, width),
            wide(span_rows, width), wide(span_rows, 128), span, wide(span_rows, width), wide(*vecs.shape))
    held = (outs[0], lows(cap, share, width)) + (lows(2, quarter, width),) * cap + (
        lows(half, width), lows(n, half, width), lows(n, half, width), both, own, both, both,
        lows(own_rows + span_rows, width), lows(own_rows + span_rows, width), wide(own_rows + span_rows, width),
        outs[4], outs[5], span, span, span, outs[10], outs[11], outs[12], outs[13], span)
    scratch = [pltpu.VMEM(h.shape, h.dtype) for h in held]
    scratch = [pltpu.VMEM(vecs.shape, F32)] + scratch[:2] + [scratch[2:2 + cap]] + scratch[2 + cap:]
    return pl.pallas_call(
        functools.partial(forward_kernel, line, nmat, cap),
        out_shape=outs,
        in_specs=[smem, smem, hbm, hbm, hbm, vmem],
        out_specs=(hbm,) * (len(outs) - 1) + (vmem,),
        scratch_shapes=scratch + [
            pltpu.SMEM((nmat,), jnp.int32), pltpu.SMEM((nmat,), jnp.int32),
            dma((4 + cap,)), dma((16,)), dma((cap,)), dma((cap,)),
        ] + [dma((n,))] * 10 + [dma((nmat, 2)), dma((nmat, 2)), dma((nmat,))],
        name="forward",
        compiler_params=pltpu.CompilerParams(
            collective_id=1, has_side_effects=True, vmem_limit_bytes=60 * 1024 * 1024),
    )(owners, spans, slots, hidden, incoming, vecs)


def backward_kernel(line, nmat, cap, owners, vectors, flow, hidden, layer, k_in, v_in, pick_in, probs_in,
                    hm_in, qm_in, ctx_in, low_in, act_in, slope_in, n1_in, inv_in, df_in, dh_in, gvec_in,
                    sg, vec_out, lay, gin,
                    vecs, full, hid, k_ref, v_ref, pick, probs, hm, qm, ctx, low, act, slope, n1, inv1, df, acc,
                    dq, gqkv, gvec, vin, vz, cin, hold, yi, fr, fl, do, di, slot_pick, far_pick, far_at,
                    w_sem, act_sem, in_sem, lsem_s, lsem_r, gsem_s, gsem_r, loc_sem,
                    cs, cr, ysd, yr, sr, rl, sl, rr, dss, dsr, vs, vr, vzs, vzr):
    ratio = (nmat - 4) // 2
    width = vecs.shape[1]
    share = cin.shape[1]
    quarter, half = share // 2, share // 4
    nchunk = 2 * nmat
    z, y, x, c = place()
    me, over = 2 * x + c, 2 * (1 - x) + c
    to_y, to_x, to_c = device(z, 1 - y, x, c), device(z, y, 1 - x, c), device(z, y, x, 1 - c)
    own_rows = layer.shape[0]
    nseq = 2 * own_rows // LEN
    per = own_rows // LEN
    greet(line)
    regroup(vectors, vecs, ratio, share)

    def load(src, dst, sem):
        return pltpu.make_async_copy(src, dst, in_sem.at[sem])

    def weight(j):
        return pltpu.make_async_copy(flow.at[j], full.at[j], w_sem.at[j])

    def block_copy(b):
        return load(hidden.at[rows((2 * b + c) * own_rows, own_rows)],
                    hid.at[pl.ds(b * own_rows, own_rows)], 14 + b)

    first_loads = [load(src, dst, i) for i, (src, dst) in enumerate(((df_in, df), (low_in, low), (dh_in, acc)))]
    next_loads = [load(src, dst, 5 + i) for i, (src, dst) in enumerate(
        ((n1_in, n1), (inv_in, inv1), (ctx_in, ctx)))]
    late_loads = [load(src, dst, 8 + i) for i, (src, dst) in enumerate(
        ((probs_in, probs), (k_in, k_ref), (v_in, v_ref), (qm_in, qm), (hm_in, hm), (pick_in, pick)))]
    late_loads += [block_copy(b) for b in range(2)]
    def chunk_loads(k):
        return [weight(5 + 2 * k), pltpu.make_async_copy(slope_in.at[k], slope.at[k], act_sem.at[0, k]),
                weight(4 + 2 * k), pltpu.make_async_copy(act_in.at[k], act.at[k], act_sem.at[1, k])]

    for copy in first_loads:
        copy.start()
    for k in range(ratio):
        for copy in chunk_loads(k):
            copy.start()

    def lay_rows(b):
        return lay.at[rows(b * own_rows, own_rows)]

    lay_x = rcopy(layer, lay_rows(me), lsem_s.at[0], lsem_r.at[0], to_x)
    lay_x_came = rcopy(layer, lay_rows(over), lsem_s.at[0], lsem_r.at[0], to_x)
    lay_c = rcopy(layer, lay_rows(me), lsem_s.at[1], lsem_r.at[1], to_c)
    lay_c_came = rcopy(layer, lay_rows(2 * x + 1 - c), lsem_s.at[1], lsem_r.at[1], to_c)
    lay_d = rcopy(lay_rows(over), lay_rows(over), lsem_s.at[2], lsem_r.at[2], to_c)
    lay_d_came = rcopy(layer, lay_rows(2 * (1 - x) + 1 - c), lsem_s.at[2], lsem_r.at[2], to_c)
    own_block = k_ref.at[pl.ds(0, own_rows)]
    lay_in = pltpu.make_async_copy(layer, own_block, loc_sem.at[1 + nseq])
    lay_own = pltpu.make_async_copy(own_block, lay_rows(me), loc_sem.at[0])
    lay_x.start()
    lay_c.start()

    order = tuple(p for k in range(ratio) for p in (4 + ratio + k, 4 + k)) + (3, 0, 1, 2)
    for s in range(2 * cap):
        slot_pick[s] = -1
        far_pick[s] = -1
        far_at[s] = 0
    for j, p in enumerate(order):
        mine = owners[p]
        place_of, later = jnp.int32(0), jnp.int32(0)
        for q in range(p):
            place_of += jnp.where(owners[q] == mine, 1, 0).astype(jnp.int32)
        for q in order[j + 1:]:
            later += jnp.where(owners[q] == mine, 1, 0).astype(jnp.int32)
        slot = (mine % 2) * cap + jnp.minimum(place_of, cap - 1)
        when = cap - 1 - jnp.minimum(later, cap - 1)
        for s in range(2 * cap):
            slot_pick[s] = jnp.where((mine // 2 == z) & (slot == s), j, slot_pick[s])
            far_at[s] = jnp.where((mine // 2 == z) & (slot == s), when, far_at[s])
            far_pick[s] = jnp.where((mine // 2 == z) & ((mine % 2) * cap + when == s), j, far_pick[s])

    def core_copy(j, src):
        return rcopy(src.at[rows((1 - c) * share, share), :], cin.at[j], cs.at[j], cr.at[j], to_c)

    def grad_of(j):
        if isinstance(j, int) and j >= 2 * ratio + 1:
            return gqkv.at[j - 2 * ratio - 1]
        if isinstance(j, int) and j == 2 * ratio:
            return full.at[3]
        return full.at[4 + j + 1 - 2 * (j % 2), pl.ds(0, 2 * share), :]

    def part(at, h):
        return rows(at * quarter + h * half, half)

    def y_copy(r):
        return rcopy(cin.at[r // 2, part(1 - y, r % 2), :], yi.at[r], ysd.at[r], yr.at[r], to_y)

    def right(r):
        return rcopy(yi.at[r], fr.at[r], sr.at[r], rl.at[r], device(z + 1, y, x, c))

    def left(r):
        return rcopy(cin.at[r // 2, part(y, r % 2), :], fl.at[r], sl.at[r], rr.at[r], device(z - 1, y, x, c))

    def stage1(r):
        j, h = r // 2, r % 2

        @pl.when(h == 0)
        def _():
            core_copy(j, gqkv.at[0]).wait_recv()

        def add(src):
            for at in (1 - y, y):
                value = (src[rows(c * share + at * quarter + h * half, half), :].astype(F32)
                         + cin[j, part(at, h), :].astype(F32))
                if at is y:
                    hold[r] = value
                else:
                    cin[j, part(at, h), :] = value.astype(BF16)

        @pl.when(j < 2 * ratio)
        def _():
            add(full.at[4 + j + 1 - 2 * (j % 2)])

        @pl.when(j == 2 * ratio)
        def _():
            add(full.at[3])

        @pl.when(j > 2 * ratio)
        def _():
            add(gqkv.at[j - 2 * ratio - 1])

        y_copy(r).start()

    def stage2(r):
        y_copy(r).wait_recv()
        hold[r] = hold[r] + yi[r].astype(F32)

    def flow_right(r):
        @pl.when(z == 0)
        def _():
            yi[r] = hold[r].astype(BF16)

        @pl.when(z > 0)
        def _():
            right(r).wait_recv()
            yi[r] = (hold[r] + fr[r].astype(F32)).astype(BF16)

        @pl.when(z < line - 1)
        def _():
            right(r).start()

    def flow_left(r):
        at = part(y, r % 2)

        @pl.when(z == line - 1)
        def _():
            cin[r // 2, at, :] = hold[r].astype(BF16)

        @pl.when(z < line - 1)
        def _():
            left(r).wait_recv()
            cin[r // 2, at, :] = (hold[r] + fl[r].astype(F32)).astype(BF16)

        @pl.when(z > 0)
        def _():
            left(r).start()

    def ranged(r, do_it):
        pl.when((r >= 0) & (r < nchunk))(functools.partial(do_it, r))

    lag, skew = 5, 3
    flown = lag + skew * (line - 1)
    ticks = nchunk + flown

    def piece_total(j, h):
        r = 2 * j + h
        value = hold[r]
        value = value + jnp.where(z > 0, fr[r].astype(F32), 0.0)
        return value + jnp.where(z < line - 1, fl[r].astype(F32), 0.0)

    def deliver(s):
        return rcopy(do.at[s], di.at[s], dss.at[s], dsr.at[s], to_y)

    def settle(j):
        for h in range(2):
            value = piece_total(j, h)
            for s in range(cap):
                sg[s, part(y, h), :] = jnp.where(slot_pick[y * cap + s] == j, value, sg[s, part(y, h), :])

                @pl.when(j <= nmat - cap + s)
                def _():
                    at = pl.ds(h * half, half)
                    do[s, at, :] = jnp.where(far_pick[(1 - y) * cap + s] == j, value.astype(BF16), do[s, at, :])

        for s in range(cap):
            pl.when(j == nmat - cap + s)(lambda s=s: deliver(s).start())

    def tick(t):
        ranged(t, stage1)
        ranged(t - 4, stage2)
        ranged(t - lag - skew * z, flow_right)
        ranged(t - lag - skew * (line - 1 - z), flow_left)
        late = t - flown
        pl.when((late >= 0) & (late < nchunk) & (late % 2 == 1))(lambda: settle(late // 2))

    def ticking(start, stop):
        def body(t, carry):
            tick(t)
            return carry

        lax.fori_loop(start, stop, body, 0)

    gvec[...] = gvec_in[...]
    sg[...] = jnp.zeros_like(sg)
    do[...] = jnp.zeros_like(do)
    for copy in first_loads:
        copy.wait()
    lay_in.start()
    halves = pl.ds(pl.multiple_of(x * 2 * share, 128), 2 * share)

    def feed_back(k, carry):
        for copy in chunk_loads(k):
            copy.wait()

        @pl.when(k == 0)
        def _():
            for j in (3, 0, 1, 2):
                weight(j).start()
            lay_in.wait()
            lay_own.start()
            lay_own.wait()
            for copy in next_loads + late_loads:
                copy.start()

        d_up = (dg(df[...], full[5 + 2 * k], NT) * slope[k].astype(F32)).astype(BF16)
        gvec[pl.ds(3 + k, 1), :] = column_sum(d_up.astype(F32))
        acc[...] = acc[...] + dg(d_up, full[4 + 2 * k], NN)
        act_k = act[k, :, halves]
        act[k] = d_up
        full[5 + 2 * k, pl.ds(0, 2 * share), :] = dg(act_k, df[...], TN).astype(BF16)
        core_copy(2 * k, full.at[5 + 2 * k]).start()
        full[4 + 2 * k, pl.ds(0, 2 * share), :] = dg(act[k, :, halves], low[...], TN).astype(BF16)
        core_copy(2 * k + 1, full.at[4 + 2 * k]).start()
        tick(2 * k)
        tick(2 * k + 1)
        return carry

    lax.fori_loop(0, ratio, feed_back, 0)
    done = 2 * ratio
    weight(3).wait()
    for copy in next_loads:
        copy.wait()
    gvec[4 + ratio:5 + ratio, :] = column_sum(acc[...] * n1[...])
    gvec[5 + ratio:6 + ratio, :] = column_sum(acc[...])
    back = norm_back(acc[...], n1[...], inv1[:, 0:1], vecs[4 + ratio:5 + ratio, :])
    acc[...] = back
    da = back.astype(BF16)
    gvec[2:3, :] = column_sum(da.astype(F32))
    df[...] = da
    low[...] = dg(da, full[3], NT).astype(BF16)
    full[3, pl.ds(0, 2 * share), :] = dg(ctx[:, halves], da, TN).astype(BF16)
    core_copy(2 * ratio, full.at[3]).start()
    ticking(done, done + 2)
    done += 2

    for copy in late_loads:
        copy.wait()
    pairs = width // (2 * HDIM)
    left_half = lax.broadcasted_iota(jnp.int32, (SPAN_ROWS, 2 * HDIM), 1) < HDIM
    scale = HDIM ** -0.5

    def attend_back(i):
        s, pair = i // pairs, i % pairs
        at, span = rows(s * LEN, LEN), rows(s * SPAN_ROWS, SPAN_ROWS)
        lanes = pl.ds(pl.multiple_of(pair * (2 * HDIM), 2 * HDIM), 2 * HDIM)
        d_two = stacked(low[span, lanes], left_half)
        given = probs[i]
        value = given.astype(F32)
        keys = k_ref[at, lanes]
        d_probs = dg(d_two, v_ref[at, lanes], NT)
        mean = jnp.sum(value * d_probs, axis=-1, keepdims=True)
        ds = (value * (d_probs - mean)).astype(BF16)
        dq[span, lanes] = (merged(dg(ds, keys, NN), left_half) * scale).astype(BF16)
        k_ref[at, lanes] = (dg(ds, stacked(qm[span, lanes], left_half), TN) * scale).astype(BF16)
        v_ref[at, lanes] = dg(given, d_two, TN).astype(BF16)

    base_back = done

    def back_step(i, carry):
        for j in range(pairs // 2):
            attend_back(i * (pairs // 2) + j)
        tick(base_back + i)
        return carry

    lax.fori_loop(0, 2 * nseq, back_step, 0)
    done += 2 * nseq
    gvec[0:1, :] = column_sum(dq[...].astype(F32))
    gqkv[0] = dg(dq[:, halves], hm[...], TN).astype(BF16)
    core_copy(2 * ratio + 1, gqkv.at[0]).start()
    for which, src in ((1, k_ref), (2, v_ref)):
        def some(i, carry, src=src):
            at = rows(i * LEN, LEN)
            return carry + dg(src[at, halves], hid[at, :], TN)

        gqkv[which] = lax.fori_loop(0, nseq, some, jnp.zeros((2 * share, width), F32)).astype(BF16)
        core_copy(2 * ratio + 1 + which, gqkv.at[which]).start()
        stop = min(2 * (2 * ratio + 2 + which), done + 3)
        ticking(done, stop)
        done = stop

    def sum_v(i, carry):
        return carry + column_sum(v_ref[rows(i * LEN, LEN), :].astype(F32))

    gvec[1:2, :] = lax.fori_loop(0, nseq, sum_v, jnp.zeros((1, width), F32))

    def vec_copy(k, who_to):
        return rcopy(gvec, vin.at[k], vs.at[k], vr.at[k], who_to)

    vec_copy(0, to_c).start()
    for j in range(3):
        weight(j).wait()
    qm[...] = (acc[...] + dg(dq[...], full[0], NN)).astype(BF16)
    def gin_rows(s, core):
        return gin.at[rows((2 * (s // per) + core) * own_rows + (s % per) * LEN, LEN)]

    def gin_copy(s):
        return rcopy(hid.at[rows(s * LEN, LEN)], gin_rows(s, c), gsem_s.at[s], gsem_r.at[s], to_c)

    def gin_came(s):
        return rcopy(hid.at[rows(s * LEN, LEN)], gin_rows(s, 1 - c), gsem_s.at[s], gsem_r.at[s], to_c)

    def gin_own(s):
        return pltpu.make_async_copy(hid.at[rows(s * LEN, LEN)], gin_rows(s, c), loc_sem.at[1 + s])

    def vec_flow(step, send):
        def one(near, ok_send, ok_recv, direction, slot_out, slot_in):
            copy = rcopy(vz.at[slot_out], vz.at[slot_out], vzs.at[direction, step], vzr.at[slot_out], near)
            if send:
                pl.when(ok_send)(copy.start)
            else:
                came = rcopy(vz.at[slot_in], vz.at[slot_in], vzs.at[direction, step], vzr.at[slot_in], near)
                pl.when(ok_send)(copy.wait_send)
                pl.when(ok_recv)(came.wait_recv)

        one(device(jnp.minimum(z + 1, line - 1), y, x, c), (z < line - 1) & (z - step >= 0), z - step - 1 >= 0, 0,
            jnp.maximum(z - step, 0), jnp.maximum(z - step - 1, 0))
        one(device(jnp.maximum(z - 1, 0), y, x, c), (z > 0) & (z + step <= line - 1), z + step + 1 <= line - 1, 1,
            jnp.minimum(z + step, line - 1), jnp.minimum(z + step + 1, line - 1))

    def vec_step(i):
        if i == 0:
            vec_copy(0, to_c).wait()
            gvec[...] = gvec[...] + vin[0]
            vec_copy(1, to_y).start()
        elif i == 1:
            vec_copy(1, to_y).wait()
            vz[z] = gvec[...] + vin[1]
        if 2 <= i <= line:
            vec_flow(i - 2, False)
        if 1 <= i <= line - 1:
            vec_flow(i - 1, True)

    for s in range(nseq):
        at, span = pl.ds(s * LEN, LEN), pl.ds(s * SPAN_ROWS, SPAN_ROWS)
        total = dg(k_ref[at, :], full[1], NN) + dg(v_ref[at, :], full[2], NN) + dg(pick[s], qm[span, :], TN)
        hid[at, :] = total.astype(BF16)
        gin_copy(s).start()
        gin_own(s).start()
        vec_step(s)
        stop = min(ticks, done + 2)
        ticking(done, stop)
        done = stop
    for i in range(nseq, line + 1):
        vec_step(i)
        stop = min(ticks, done + 1)
        ticking(done, stop)
        done = stop
    ticking(done, ticks)
    total = vz[0]
    for k in range(1, line):
        total = total + vz[k]
    gvec[...] = total
    regroup(gvec, vec_out, ratio, share)

    lay_x_came.wait_recv()
    lay_d.start()

    def finish(r, carry):
        y_copy(r).wait_send()

        @pl.when(z < line - 1)
        def _():
            right(r).wait_send()

        @pl.when(z > 0)
        def _():
            left(r).wait_send()

        return carry

    lax.fori_loop(0, nchunk, finish, 0)

    def last(j, carry):
        core_copy(j, gqkv.at[0]).wait_send()
        return carry

    lax.fori_loop(0, nmat, last, 0)
    for s in range(nseq):
        gin_copy(s).wait_send()
        gin_came(s).wait_recv()
        gin_own(s).wait()
    lay_x.wait_send()
    lay_c.wait_send()
    lay_c_came.wait_recv()
    lay_d.wait_send()
    lay_d_came.wait_recv()
    for s in range(cap):
        deliver(s).wait()
    for s in range(cap):
        sg[s, rows((1 - y) * quarter, quarter), :] = di[far_at[y * cap + s]].astype(F32)


def backward(owners, vecs, saved, hidden, line, cap):
    flow, layer, *kept, gvec = saved
    nmat, width, _ = flow.shape
    share = width // 4
    nseq = 2 * layer.shape[0] // LEN
    span_rows = nseq * SPAN_ROWS
    quarter, half = share // 2, share // 4
    n = 2 * nmat
    dma = pltpu.SemaphoreType.DMA
    vmem = pl.BlockSpec(memory_space=pltpu.VMEM)
    smem = pl.BlockSpec(memory_space=pltpu.SMEM)
    hbm = pl.BlockSpec(memory_space=pl.ANY)
    whole = jax.ShapeDtypeStruct(hidden.shape, BF16)

    def lows(*shape):
        return pltpu.VMEM(shape, BF16)

    def wide(*shape):
        return pltpu.VMEM(shape, F32)

    k, v, pick, probs, hm, qm, ctx, low, act, slope, n1, inv1, df, dh = (
        pltpu.VMEM(value.shape, value.dtype) for value in kept)
    return pl.pallas_call(
        functools.partial(backward_kernel, line, nmat, cap),
        out_shape=(jax.ShapeDtypeStruct((cap, share, width), F32),
                   jax.ShapeDtypeStruct(vecs.shape, F32), whole, whole),
        in_specs=[smem, vmem, hbm, hbm] + [hbm] * (1 + len(kept)) + [vmem],
        out_specs=(vmem, vmem, hbm, hbm),
        scratch_shapes=[
            wide(*vecs.shape), lows(nmat, width, width), lows(2 * layer.shape[0], width), k, v, pick, probs, hm, qm, ctx, low,
            act, slope, n1, inv1, df, dh,
            lows(span_rows, width), lows(3, 2 * share, width),
            wide(*vecs.shape), wide(2, *vecs.shape), wide(line, *vecs.shape),
            lows(nmat, share, width), wide(n, half, width), lows(n, half, width), lows(n, half, width),
            lows(n, half, width), lows(cap, quarter, width), lows(cap, quarter, width),
            pltpu.SMEM((2 * cap,), jnp.int32), pltpu.SMEM((2 * cap,), jnp.int32), pltpu.SMEM((2 * cap,), jnp.int32),
            dma((nmat,)), dma((2, (nmat - 4) // 2)), dma((16,)), dma((3,)), dma((3,)), dma((nseq,)), dma((nseq,)), dma((2 + nseq,)),
            dma((nmat,)), dma((nmat,)),
        ] + [dma((n,))] * 6 + [dma((cap,)), dma((cap,)), dma((2,)), dma((2,)), dma((2, line)), dma((line,))],
        name="backward",
        compiler_params=pltpu.CompilerParams(
            collective_id=2, has_side_effects=True, vmem_limit_bytes=60 * 1024 * 1024),
    )(owners, vecs, flow, hidden, layer, *kept, gvec)


STEP = 10
MATRIX_RATE = 0.03
VECTOR_RATE = 0.25
BETA_ONE = 0.5
BETA_TWO = 0.5
DECAY = 0.01
ADAM_EPS = 1e-08


def adamw(weight, moment_one, moment_two, grad, step_rate):
    new_one = BETA_ONE * moment_one + (1.0 - BETA_ONE) * grad
    new_two = BETA_TWO * moment_two + (1.0 - BETA_TWO) * grad * grad
    corr_one = 1.0 - BETA_ONE**STEP
    corr_two = 1.0 - BETA_TWO**STEP
    direction = new_one / corr_one / (jnp.sqrt(new_two / corr_two) + ADAM_EPS)
    return (weight - step_rate * (direction + DECAY * weight), new_one, new_two)


def on_device(line, hidden_in, incoming, spans, owners, vectors, vec_one, vec_two, master_slots, slot_one, slot_two):
    cap, width, share = master_slots.shape
    nmat = owners.shape[0]
    saved = forward(
        owners, jnp.transpose(spans, (2, 0, 1)), jnp.transpose(master_slots, (0, 2, 1)), hidden_in, incoming, vectors, line)
    slot_grad, vec_grad, layer_out, input_grad = backward(owners, vectors, saved, hidden_in, line, cap)
    new_vec = adamw(vectors, vec_one, vec_two, vec_grad, VECTOR_RATE)
    slot_grad = jnp.transpose(slot_grad, (0, 2, 1))
    held = jnp.sum((owners == lax.axis_index("dp")).astype(jnp.int32))
    occupied = (jnp.arange(cap) < held).astype(F32)[:, None, None]
    new_slots = adamw(master_slots, slot_one, slot_two, slot_grad, MATRIX_RATE)
    return (layer_out, input_grad) + new_vec + tuple(v * occupied for v in new_slots)


def solution(mesh):
    line = mesh.shape["dp"] // 2
    rows, slots = P("dp", None), P("dp", None, "mp")
    return jax.shard_map(
        functools.partial(on_device, line),
        mesh=mesh,
        in_specs=(rows, rows, P("dp", None, None), P(), P(), P(), P(), slots, slots, slots),
        out_specs=(rows, rows, P(), P(), P(), slots, slots, slots),
        check_vma=False,
    )
```

```python
import functools
import jax
import jax.numpy as jnp
from jax import lax
from jax.sharding import PartitionSpec as P
from jax.experimental import pallas as pl
from jax.experimental.pallas import tpu as pltpu

MESH = pl.DeviceIdType.MESH
BF16 = jnp.bfloat16
F32 = jnp.float32
LN_EPS = 1e-12
HDIM = 64
LEN = 512
NT = (((1,), (1,)), ((), ()))
NN = (((1,), (0,)), ((), ()))
TN = (((0,), (0,)), ((), ()))


def dg(left, right, dims):
    return lax.dot_general(left, right, dims, preferred_element_type=F32)


def flow_order(nmat):
    ratio = (nmat - 4) // 2
    return (0, 1, 2, 3) + tuple(p for k in range(ratio) for p in (4 + k, 4 + ratio + k))


def layer_norm(value, gain, shift):
    center = value - jnp.mean(value, axis=-1, keepdims=True)
    inverse = lax.rsqrt(jnp.mean(center * center, axis=-1, keepdims=True) + LN_EPS)
    normed = center * inverse
    return normed * gain + shift, normed, inverse


def gelu(value):
    return 0.5 * value * (1.0 + lax.erf(value * 2.0 ** (-0.5)))


def place():
    dp, mp = lax.axis_index("dp"), lax.axis_index("mp")
    return dp // 2, dp % 2, mp // 2, mp % 2


def device(z, y, x, c):
    return (z * 2 + y, x * 2 + c)


def greet(line):
    z, y, x, c = place()
    bar = pltpu.get_barrier_semaphore()
    for who in (device(z, 1 - y, x, c), device(z, y, 1 - x, c), device(z, y, x, 1 - c)):
        pl.semaphore_signal(bar, inc=1, device_id=who, device_id_type=MESH)

    @pl.when(z > 0)
    def _():
        pl.semaphore_signal(bar, inc=1, device_id=device(z - 1, y, x, c), device_id_type=MESH)

    @pl.when(z < line - 1)
    def _():
        pl.semaphore_signal(bar, inc=1, device_id=device(z + 1, y, x, c), device_id_type=MESH)

    peers = 3 + jnp.where(z > 0, 1, 0) + jnp.where(z < line - 1, 1, 0)
    pl.semaphore_wait(bar, peers.astype(jnp.int32))


def rcopy(src, dst, send, recv, who):
    return pltpu.make_async_remote_copy(
        src_ref=src, dst_ref=dst, send_sem=send, recv_sem=recv, device_id=who, device_id_type=MESH
    )


SPAN_ROWS = 96


def rows(start, size):
    return pl.ds(pl.multiple_of(start, 16), size)


def column_sum(value):
    return jnp.sum(value, axis=0, keepdims=True)


def regroup(src, dst, ratio, share):
    dst[...] = src[...]
    for j in range(ratio):
        for k in range(ratio):
            dst[3 + k:4 + k, j * share:(j + 1) * share] = src[3 + j:4 + j, k * share:(k + 1) * share]


def norm_back(grad, normed, inverse, gain):
    scaled = grad * gain
    first = jnp.mean(scaled, axis=-1, keepdims=True)
    second = jnp.mean(scaled * normed, axis=-1, keepdims=True)
    return inverse * (scaled - first - normed * second)


def stacked(value, left_half):
    zero = jnp.zeros_like(value)
    return jnp.concatenate([jnp.where(left_half, value, zero), jnp.where(left_half, zero, value)], axis=0)


def merged(value, left_half):
    size = left_half.shape[0]
    return jnp.where(left_half, value[:size], value[size:])


def forward_kernel(line, nmat, cap, owners, spans, slots_in, hidden, incoming, vectors,
                   out, layer_out, k_out, v_out, pick_out, probs_out, hm_out, qm_out, ctx_out, low_out,
                   act_out, slope_out, n1_out, inv_out, df_out, dh_out, gvec,
                   vecs, full, slots, ys, stage, fr, fl, hid, q_ref, k_ref, v_ref, ctx, low, acc,
                   pick, probs, hm, gm, qm, act, slope, n1, inv1, df, zo, idx,
                   in_sem, out_sem, slot_send, slot_recv, sr, rl, sl, rr, xs, xr, ysd, yr, ds, dr, cs, cr, loc):
    share = slots.shape[1]
    quarter = share // 2
    half = quarter // 2
    nchunk = 2 * nmat
    z, y, x, c = place()
    me = 2 * x + c
    over = 2 * (1 - x) + c
    to_y, to_x, to_c = device(z, 1 - y, x, c), device(z, y, 1 - x, c), device(z, y, x, 1 - c)
    greet(line)
    ratio = (nmat - 4) // 2
    order = flow_order(nmat)
    own_rows = q_ref.shape[0]
    width = vecs.shape[1]
    regroup(vectors, vecs, ratio, share)
    per = own_rows // LEN
    nseq = 2 * per

    def block_copy(src, dst, b, sem):
        return pltpu.make_async_copy(
            src.at[rows((2 * b + c) * own_rows, own_rows)], dst.at[pl.ds(b * own_rows, own_rows)], sem)

    slot_loads = [pltpu.make_async_copy(slots_in.at[s], acc.at[pl.ds(s * share, share)], in_sem.at[4 + s])
                  for s in range(cap)]
    loads = [block_copy(hidden, hid, b, in_sem.at[b]) for b in range(2)]
    loads += [block_copy(incoming, v_ref, b, in_sem.at[2 + b]) for b in range(2)]
    for copy in slot_loads + loads:
        copy.start()

    def slot_copy(s):
        return rcopy(
            slots.at[s, pl.ds(pl.multiple_of((1 - y) * quarter, 16), quarter), :],
            ys[s].at[y], slot_send.at[s], slot_recv.at[s], to_y)

    for s in range(cap):
        slot_loads[s].wait()
        slots[s] = acc[pl.ds(s * share, share), :].astype(BF16)
        slot_copy(s).start()
        ys[s][y] = slots[s, pl.ds(pl.multiple_of(y * quarter, 16), quarter), :]
    for j, p in enumerate(order):
        mine = owners[p]
        place_of = jnp.int32(0)
        for q in range(p):
            place_of += jnp.where(owners[q] == mine, 1, 0).astype(jnp.int32)
        zo[j] = mine // 2
        idx[j] = (mine % 2) * cap + jnp.minimum(place_of, cap - 1)

    def piece_rows(block, yy, h):
        return pl.ds(pl.multiple_of(block * share + yy * quarter + h * half, 16), half)

    def own(r):
        at = pl.ds(pl.multiple_of((r % 2) * half, 16), half)
        slot, half_of = idx[r // 2] % cap, idx[r // 2] // cap
        stage[...] = ys[0][half_of, at, :]
        for s in range(1, cap):
            @pl.when(r // 2 >= s)
            def _():
                stage[...] = jnp.where(slot == s, ys[s][half_of, at, :], stage[...])

        return stage[...]

    def right(r):
        return rcopy(fr.at[r], fr.at[r], sr.at[r], rl.at[r], device(z + 1, y, x, c))

    def left(r):
        return rcopy(fl.at[r], fl.at[r], sl.at[r], rr.at[r], device(z - 1, y, x, c))

    def x_copy(f):
        at = full.at[f // 2, piece_rows(me, y, f % 2), :]
        return rcopy(at, at, xs.at[f], xr.at[f], to_x)

    def x_came(f):
        at = full.at[f // 2, piece_rows(over, y, f % 2), :]
        return rcopy(at, at, xs.at[f], xr.at[f], to_x)

    def y_copy(f):
        at = full.at[f // 2, piece_rows(me, y, f % 2), :]
        return rcopy(at, at, ysd.at[f], yr.at[f], to_y)

    def y_came(f):
        at = full.at[f // 2, piece_rows(me, 1 - y, f % 2), :]
        return rcopy(at, at, ysd.at[f], yr.at[f], to_y)

    def diag_x(f):
        at = full.at[f // 2, piece_rows(me, 1 - y, f % 2), :]
        return rcopy(at, at, ds.at[f], dr.at[f], to_x)

    def diag_y(f):
        at = full.at[f // 2, piece_rows(over, y, f % 2), :]
        return rcopy(at, at, ds.at[f], dr.at[f], to_y)

    def diag_came(f):
        at = full.at[f // 2, piece_rows(over, 1 - y, f % 2), :]
        return rcopy(at, at, ds.at[f], dr.at[f], to_x)

    def core_copy(p, k):
        block = jnp.where(k == 0, me, over) if not isinstance(k, int) else (me, over)[k]
        at = full.at[p, pl.ds(pl.multiple_of(block * share, 16), share), :]
        return rcopy(at, at, cs.at[p, k], cr.at[p, k], to_c)

    def core_came(p, k):
        block = (2 * x + 1 - c, 2 * (1 - x) + 1 - c)[k]
        at = full.at[p, pl.ds(pl.multiple_of(block * share, 16), share), :]
        return rcopy(at, at, cs.at[p, k], cr.at[p, k], to_c)

    def keep(p):
        return pltpu.make_async_copy(full.at[p], out.at[p], loc.at[p])

    lag0 = 2 * (line - 1)
    lag1 = lag0 + 3
    lag2 = lag1 + 3
    lag3 = lag2 + 1

    def slot_came(s):
        rcopy(slots.at[s, pl.ds(pl.multiple_of((1 - y) * quarter, 16), quarter), :],
              ys[s].at[1 - y], slot_send.at[s], slot_recv.at[s], to_y).wait_recv()

    def tick(t):
        for s in range(cap):
            pl.when(t == 2 * s)(functools.partial(slot_came, s))

        r = t - 2 * z

        @pl.when((r >= 0) & (r < nchunk))
        def _():
            @pl.when(z == 0)
            def _():
                fr[r] = own(r)

            @pl.when(z > 0)
            def _():
                right(r).wait_recv()
                fr[r] = jnp.where(zo[r // 2] == z, own(r), fr[r])

            @pl.when(z < line - 1)
            def _():
                right(r).start()

        l = t - 2 * (line - 1 - z)

        @pl.when((l >= 0) & (l < nchunk))
        def _():
            @pl.when(z == line - 1)
            def _():
                fl[l] = own(l)

            @pl.when(z < line - 1)
            def _():
                left(l).wait_recv()
                fl[l] = jnp.where(zo[l // 2] == z, own(l), fl[l])

            @pl.when(z > 0)
            def _():
                left(l).start()

        f = t - lag0

        @pl.when((f >= 0) & (f < nchunk))
        def _():
            full[f // 2, piece_rows(me, y, f % 2), :] = jnp.where(zo[f // 2] <= z, fr[f], fl[f])
            x_copy(f).start()
            y_copy(f).start()

        g = t - lag1

        @pl.when((g >= 0) & (g < nchunk))
        def _():
            x_came(g).wait_recv()
            y_came(g).wait_recv()

            @pl.when(g % 2 == 0)
            def _():
                diag_x(g).start()

            @pl.when(g % 2 == 1)
            def _():
                diag_y(g).start()

        e = t - lag2

        @pl.when((e >= 0) & (e < nchunk))
        def _():
            diag_came(e).wait_recv()

            @pl.when(e % 2 == 1)
            def _():
                for k in range(2):
                    core_copy(e // 2, k).start()

        w = t - lag3

        @pl.when((w >= 0) & (w < nchunk) & (w % 2 == 1))
        def _():
            for k in range(2):
                core_came(w // 2, k).wait_recv()
            keep(w // 2).start()

    ticks = nchunk + lag3

    def ticking(start, count):
        def body(i, carry):
            tick(start + i)
            return carry

        if count > 0:
            lax.fori_loop(0, count, body, 0)

    position = lax.broadcasted_iota(jnp.int32, (8, LEN), 1)
    row_of = lax.broadcasted_iota(jnp.int32, (SPAN_ROWS, LEN), 0).astype(F32)

    def cover(s, carry):
        seq = (2 * (s // per) + c) * per + s % per
        seen = jnp.zeros((8, LEN), F32)
        for n in range(spans.shape[2]):
            start, size = spans[0, seq, n], spans[1, seq, n]
            seen = jnp.where((position >= start) & (position < start + size), 1.0, seen)
        upper = (lax.broadcasted_iota(jnp.int32, (LEN, LEN), 0)
                 <= lax.broadcasted_iota(jnp.int32, (LEN, LEN), 1)).astype(F32).astype(BF16)
        rank = dg(seen.astype(BF16), upper, NN)
        chosen = jnp.where((rank[0:1, :] - 1.0 == row_of) & (seen[0:1, :] > 0.0), 1.0, 0.0).astype(BF16)
        pick[s] = chosen
        at, span = rows(s * LEN, LEN), rows(s * SPAN_ROWS, SPAN_ROWS)
        hm[span, :] = dg(chosen, hid[at, :], NN).astype(BF16)
        gm[span, :] = dg(chosen, v_ref[at, :], NN).astype(BF16)
        tick(nseq + s)
        return carry

    ticking(0, nseq)
    for copy in loads:
        copy.wait()
    lax.fori_loop(0, nseq, cover, 0)
    kept = []

    def keep_out(src, dst):
        copy = pltpu.make_async_copy(src, dst, out_sem.at[len(kept)])
        copy.start()
        kept.append(copy)

    keep_out(pick, pick_out)
    keep_out(hm, hm_out)

    now = lag3 + 2
    ticking(2 * nseq, now - 2 * nseq)
    for i in range(per):
        block = hid[rows(x * own_rows + i * LEN, LEN), :]
        q_ref[pl.ds(i * LEN, LEN), :] = (
            (dg(block, full[0], NT) + vecs[0:1, :]).astype(BF16) * jnp.asarray(HDIM ** -0.5, BF16))
    tick(now)
    qm[...] = (dg(hm[...], full[0], NT) + vecs[0:1, :]).astype(BF16)
    keep_out(qm, qm_out)
    tick(now + 1)
    now += 2

    def project_k(s, carry):
        at = rows(s * LEN, LEN)
        k_ref[at, :] = dg(hid[at, :], full[1], NT).astype(BF16)
        pl.when(s % 2 == 1)(lambda: tick(now_k + s // 2))
        return carry

    def project_v(s, carry):
        at = rows(s * LEN, LEN)
        v_ref[at, :] = (dg(hid[at, :], full[2], NT) + vecs[1:2, :]).astype(BF16)
        pl.when(s % 2 == 1)(lambda: tick(now_v + s // 2))
        return carry

    now_k = now
    lax.fori_loop(0, nseq, project_k, 0)
    keep_out(k_ref, k_out)
    now_v = now_k + nseq // 2
    lax.fori_loop(0, nseq, project_v, 0)
    keep_out(v_ref, v_out)
    now = now_v + nseq // 2

    pairs = width // (2 * HDIM)
    left_half = lax.broadcasted_iota(jnp.int32, (LEN, 2 * HDIM), 1) < HDIM
    ones = jnp.ones((LEN, 2 * HDIM), BF16)

    def lanes_of(pair):
        return pl.ds(pl.multiple_of(pair * (2 * HDIM), 2 * HDIM), 2 * HDIM)

    def attend(i):
        at, lanes = rows((i // pairs) * LEN, LEN), lanes_of(i % pairs)
        both = rows(x * own_rows + (i // pairs) * LEN, LEN)
        q_blk, k_blk = q_ref[at, lanes], k_ref[both, lanes]
        v_blk = jnp.concatenate([v_ref[both, lanes], ones], axis=1)
        mixed = []
        for h in range(2):
            q_one = jnp.where(left_half if h == 0 else ~left_half, q_blk, jnp.zeros_like(q_blk))
            scores = dg(q_one, k_blk, NT)
            raised = jnp.exp(scores - jnp.max(scores, axis=-1, keepdims=True)).astype(BF16)
            sums = dg(raised, v_blk, NN)
            mixed.append(sums[:, :2 * HDIM] / sums[:, 2 * HDIM:])
        ctx[at, lanes] = jnp.where(left_half, mixed[0], mixed[1]).astype(BF16)

    group = 3

    def attend_step(i, carry):
        for j in range(group):
            attend(i * group + j)
        tick(now + i)
        return carry

    count = per * pairs // group
    lax.fori_loop(0, count, attend_step, 0)
    now += count

    left_span = lax.broadcasted_iota(jnp.int32, (SPAN_ROWS, 2 * HDIM), 1) < HDIM
    scale = HDIM ** -0.5

    def attend_span(i):
        s, lanes = i // pairs, lanes_of(i % pairs)
        at, span = rows(s * LEN, LEN), rows(s * SPAN_ROWS, SPAN_ROWS)
        scores = dg(stacked(qm[span, lanes], left_span), k_ref[at, lanes], NT) * scale
        raised = jnp.exp(scores - jnp.max(scores, axis=-1, keepdims=True))
        value = (raised / jnp.sum(raised, axis=-1, keepdims=True)).astype(BF16)
        probs[i] = value
        ctx[rows(own_rows + s * SPAN_ROWS, SPAN_ROWS), lanes] = merged(
            dg(value, v_ref[at, lanes], NN), left_span).astype(BF16)

    span_group = pairs

    def span_step(i, carry):
        for j in range(span_group):
            attend_span(i * span_group + j)
        tick(now + i)
        return carry

    lax.fori_loop(0, nseq, span_step, 0)
    now += nseq
    keep_out(probs, probs_out)
    span_rows = nseq * SPAN_ROWS
    all_rows = own_rows + span_rows
    spanned = pl.ds(own_rows, span_rows)
    keep_out(ctx.at[spanned], ctx_out)

    def mix(residual, at):
        h1 = residual.astype(F32) + dg(ctx[at, :], full[3], NN) + vecs[2:3, :]
        value, normed, inverse = layer_norm(h1, vecs[4 + ratio:5 + ratio, :], vecs[5 + ratio:6 + ratio, :])
        low[at, :] = value.astype(BF16)
        acc[at, :] = value + vecs[3 + ratio:4 + ratio, :]
        return normed, inverse

    for i in range(per):
        mix(hid[rows(x * own_rows + i * LEN, LEN), :], pl.ds(i * LEN, LEN))
    normed, inverse = mix(hm[...], spanned)
    n1[...] = normed
    inv1[...] = jnp.broadcast_to(inverse, inv1.shape)
    keep_out(n1, n1_out)
    keep_out(inv1, inv_out)
    keep_out(low.at[spanned], low_out)
    tick(now)
    now += 1

    tile = all_rows // 2
    ready = [lag3 + 2 * (5 + 2 * k) + 2 for k in range(ratio)]
    for k in range(ratio):
        for i in range(2):
            if i == 0:
                ticking(now, max(0, ready[k] - now))
                now = max(now, ready[k])
            at = pl.ds(i * tile, tile)
            up = dg(low[at, :], full[4 + 2 * k], NT) + vecs[3 + k:4 + k, :]
            cdf = 0.5 * (1.0 + lax.erf(up * 2.0 ** (-0.5)))
            active = (up * cdf).astype(BF16)
            acc[at, :] = acc[at, :] + dg(active, full[5 + 2 * k], NN)
            if i == 1:
                up, cdf = up[tile - span_rows:], cdf[tile - span_rows:]
                act[k] = active[tile - span_rows:]
                slope[k] = (cdf + up * (jnp.exp(-0.5 * up * up) * (2.0 * jnp.pi) ** (-0.5))).astype(BF16)
            if i == 1:
                keep_out(act.at[k], act_out.at[k])
                keep_out(slope.at[k], slope_out.at[k])
            if now < ticks:
                tick(now)
                now += 1
    ticking(now, max(0, ticks - now))

    _, normed, inverse = layer_norm(
        acc[spanned, :], vecs[6 + ratio:7 + ratio, :], vecs[7 + ratio:8 + ratio, :])
    given = gm[...].astype(F32)
    gvec[...] = jnp.zeros_like(gvec)
    gvec[6 + ratio:7 + ratio, :] = column_sum(given * normed)
    gvec[7 + ratio:8 + ratio, :] = column_sum(given)
    back = norm_back(given, normed, inverse, vecs[6 + ratio:7 + ratio, :])
    df[...] = back.astype(BF16)
    gvec[3 + ratio:4 + ratio, :] = column_sum(back.astype(BF16).astype(F32))
    acc[spanned, :] = back
    keep_out(df, df_out)
    keep_out(acc.at[spanned], dh_out)
    for i in range(per):
        at = pl.ds(i * LEN, LEN)
        q_ref[at, :] = layer_norm(
            acc[at, :], vecs[6 + ratio:7 + ratio, :], vecs[7 + ratio:8 + ratio, :])[0].astype(BF16)
    keep_out(q_ref, layer_out)
    for copy in kept:
        copy.wait()

    def finish(r, carry):
        @pl.when(z < line - 1)
        def _():
            right(r).wait_send()

        @pl.when(z > 0)
        def _():
            left(r).wait_send()

        x_copy(r).wait_send()
        y_copy(r).wait_send()
        diag_came(r).wait_send()
        return carry

    lax.fori_loop(0, nchunk, finish, 0)

    def last(p, carry):
        for k in range(2):
            core_copy(p, k).wait_send()
        keep(p).wait()
        return carry

    lax.fori_loop(0, nmat, last, 0)
    for s in range(cap):
        slot_copy(s).wait_send()


def forward(owners, spans, slots, hidden, incoming, vecs, line):
    cap, share, width = slots.shape
    nmat = owners.shape[0]
    ratio = (nmat - 4) // 2
    own_rows = hidden.shape[0] // 4
    quarter, half = share // 2, share // 4
    n = 2 * nmat
    nseq = 2 * own_rows // LEN
    span_rows = nseq * SPAN_ROWS
    pairs = width // (2 * HDIM)
    dma = pltpu.SemaphoreType.DMA
    vmem = pl.BlockSpec(memory_space=pltpu.VMEM)
    smem = pl.BlockSpec(memory_space=pltpu.SMEM)
    hbm = pl.BlockSpec(memory_space=pl.ANY)

    def lows(*shape):
        return jax.ShapeDtypeStruct(shape, BF16)

    def wide(*shape):
        return jax.ShapeDtypeStruct(shape, F32)

    own, both, span = lows(own_rows, width), lows(2 * own_rows, width), lows(span_rows, width)
    outs = (lows(nmat, 4 * share, width), own, both, both, lows(nseq, SPAN_ROWS, LEN),
            lows(nseq * pairs, 2 * SPAN_ROWS, LEN), span, span, span, span,
            lows(ratio, span_rows, width), lows(ratio, span_rows, width),
            wide(span_rows, width), wide(span_rows, 128), span, wide(span_rows, width), wide(*vecs.shape))
    held = (outs[0], lows(cap, share, width)) + (lows(2, quarter, width),) * cap + (
        lows(half, width), lows(n, half, width), lows(n, half, width), both, own, both, both,
        lows(own_rows + span_rows, width), lows(own_rows + span_rows, width), wide(own_rows + span_rows, width),
        outs[4], outs[5], span, span, span, outs[10], outs[11], outs[12], outs[13], span)
    scratch = [pltpu.VMEM(h.shape, h.dtype) for h in held]
    scratch = [pltpu.VMEM(vecs.shape, F32)] + scratch[:2] + [scratch[2:2 + cap]] + scratch[2 + cap:]
    return pl.pallas_call(
        functools.partial(forward_kernel, line, nmat, cap),
        out_shape=outs,
        in_specs=[smem, smem, hbm, hbm, hbm, vmem],
        out_specs=(hbm,) * (len(outs) - 1) + (vmem,),
        scratch_shapes=scratch + [
            pltpu.SMEM((nmat,), jnp.int32), pltpu.SMEM((nmat,), jnp.int32),
            dma((4 + cap,)), dma((13 + 2 * ratio,)), dma((cap,)), dma((cap,)),
        ] + [dma((n,))] * 10 + [dma((nmat, 2)), dma((nmat, 2)), dma((nmat,))],
        name="forward",
        compiler_params=pltpu.CompilerParams(
            collective_id=1, has_side_effects=True, vmem_limit_bytes=60 * 1024 * 1024),
    )(owners, spans, slots, hidden, incoming, vecs)


def backward_kernel(line, nmat, cap, owners, vectors, flow, hidden, layer, k_in, v_in, pick_in, probs_in,
                    hm_in, qm_in, ctx_in, low_in, act_in, slope_in, n1_in, inv_in, df_in, dh_in, gvec_in,
                    sg, vec_out, lay, gin,
                    vecs, full, hid, k_ref, v_ref, pick, probs, hm, qm, ctx, low, act, slope, n1, inv1, df, acc,
                    dq, gqkv, gvec, vin, vz, cin, hold, yi, fr, fl, do, di, slot_pick, far_pick, far_at,
                    w_sem, act_sem, in_sem, lsem_s, lsem_r, gsem_s, gsem_r, loc_sem,
                    cs, cr, ysd, yr, sr, rl, sl, rr, dss, dsr, vs, vr, vzs, vzr):
    ratio = (nmat - 4) // 2
    width = vecs.shape[1]
    share = cin.shape[1]
    quarter, half = share // 2, share // 4
    nchunk = 2 * nmat
    z, y, x, c = place()
    me, over = 2 * x + c, 2 * (1 - x) + c
    to_y, to_x, to_c = device(z, 1 - y, x, c), device(z, y, 1 - x, c), device(z, y, x, 1 - c)
    own_rows = layer.shape[0]
    nseq = 2 * own_rows // LEN
    per = own_rows // LEN
    greet(line)
    regroup(vectors, vecs, ratio, share)

    def load(src, dst, sem):
        return pltpu.make_async_copy(src, dst, in_sem.at[sem])

    def weight(j):
        return pltpu.make_async_copy(flow.at[j], full.at[j], w_sem.at[j])

    def block_copy(b):
        return load(hidden.at[rows((2 * b + c) * own_rows, own_rows)],
                    hid.at[pl.ds(b * own_rows, own_rows)], 14 + b)

    first_loads = [load(src, dst, i) for i, (src, dst) in enumerate(((df_in, df), (low_in, low), (dh_in, acc)))]
    next_loads = [load(src, dst, 5 + i) for i, (src, dst) in enumerate(
        ((n1_in, n1), (inv_in, inv1), (ctx_in, ctx)))]
    late_loads = [load(src, dst, 8 + i) for i, (src, dst) in enumerate(
        ((probs_in, probs), (k_in, k_ref), (v_in, v_ref), (qm_in, qm), (hm_in, hm), (pick_in, pick)))]
    late_loads += [block_copy(b) for b in range(2)]
    def chunk_loads(k):
        return [weight(5 + 2 * k), pltpu.make_async_copy(slope_in.at[k], slope.at[k], act_sem.at[0, k]),
                weight(4 + 2 * k), pltpu.make_async_copy(act_in.at[k], act.at[k], act_sem.at[1, k])]

    for copy in first_loads:
        copy.start()
    for k in range(ratio):
        for copy in chunk_loads(k):
            copy.start()

    def lay_rows(b):
        return lay.at[rows(b * own_rows, own_rows)]

    lay_x = rcopy(layer, lay_rows(me), lsem_s.at[0], lsem_r.at[0], to_x)
    lay_x_came = rcopy(layer, lay_rows(over), lsem_s.at[0], lsem_r.at[0], to_x)
    lay_c = rcopy(layer, lay_rows(me), lsem_s.at[1], lsem_r.at[1], to_c)
    lay_c_came = rcopy(layer, lay_rows(2 * x + 1 - c), lsem_s.at[1], lsem_r.at[1], to_c)
    lay_d = rcopy(lay_rows(over), lay_rows(over), lsem_s.at[2], lsem_r.at[2], to_c)
    lay_d_came = rcopy(layer, lay_rows(2 * (1 - x) + 1 - c), lsem_s.at[2], lsem_r.at[2], to_c)
    own_block = k_ref.at[pl.ds(0, own_rows)]
    lay_in = pltpu.make_async_copy(layer, own_block, loc_sem.at[1 + nseq])
    lay_own = pltpu.make_async_copy(own_block, lay_rows(me), loc_sem.at[0])
    lay_x.start()
    lay_c.start()

    order = tuple(p for k in range(ratio) for p in (4 + ratio + k, 4 + k)) + (3, 0, 1, 2)
    for s in range(2 * cap):
        slot_pick[s] = -1
        far_pick[s] = -1
        far_at[s] = 0
    for j, p in enumerate(order):
        mine = owners[p]
        place_of, later = jnp.int32(0), jnp.int32(0)
        for q in range(p):
            place_of += jnp.where(owners[q] == mine, 1, 0).astype(jnp.int32)
        for q in order[j + 1:]:
            later += jnp.where(owners[q] == mine, 1, 0).astype(jnp.int32)
        slot = (mine % 2) * cap + jnp.minimum(place_of, cap - 1)
        when = cap - 1 - jnp.minimum(later, cap - 1)
        for s in range(2 * cap):
            slot_pick[s] = jnp.where((mine // 2 == z) & (slot == s), j, slot_pick[s])
            far_at[s] = jnp.where((mine // 2 == z) & (slot == s), when, far_at[s])
            far_pick[s] = jnp.where((mine // 2 == z) & ((mine % 2) * cap + when == s), j, far_pick[s])

    def core_copy(j, src):
        return rcopy(src.at[rows((1 - c) * share, share), :], cin.at[j], cs.at[j], cr.at[j], to_c)

    def grad_of(j):
        if isinstance(j, int) and j >= 2 * ratio + 1:
            return gqkv.at[j - 2 * ratio - 1]
        if isinstance(j, int) and j == 2 * ratio:
            return full.at[3]
        return full.at[4 + j + 1 - 2 * (j % 2), pl.ds(0, 2 * share), :]

    def part(at, h):
        return rows(at * quarter + h * half, half)

    def y_copy(r):
        return rcopy(cin.at[r // 2, part(1 - y, r % 2), :], yi.at[r], ysd.at[r], yr.at[r], to_y)

    def right(r):
        return rcopy(yi.at[r], fr.at[r], sr.at[r], rl.at[r], device(z + 1, y, x, c))

    def left(r):
        return rcopy(cin.at[r // 2, part(y, r % 2), :], fl.at[r], sl.at[r], rr.at[r], device(z - 1, y, x, c))

    def stage1(r):
        j, h = r // 2, r % 2

        @pl.when(h == 0)
        def _():
            core_copy(j, gqkv.at[0]).wait_recv()

        def add(src):
            for at in (1 - y, y):
                value = (src[rows(c * share + at * quarter + h * half, half), :].astype(F32)
                         + cin[j, part(at, h), :].astype(F32))
                if at is y:
                    hold[r] = value
                else:
                    cin[j, part(at, h), :] = value.astype(BF16)

        @pl.when(j < 2 * ratio)
        def _():
            add(full.at[4 + j + 1 - 2 * (j % 2)])

        @pl.when(j == 2 * ratio)
        def _():
            add(full.at[3])

        @pl.when(j > 2 * ratio)
        def _():
            add(gqkv.at[j - 2 * ratio - 1])

        y_copy(r).start()

    def stage2(r):
        y_copy(r).wait_recv()
        hold[r] = hold[r] + yi[r].astype(F32)

    def flow_right(r):
        @pl.when(z == 0)
        def _():
            yi[r] = hold[r].astype(BF16)

        @pl.when(z > 0)
        def _():
            right(r).wait_recv()
            yi[r] = (hold[r] + fr[r].astype(F32)).astype(BF16)

        @pl.when(z < line - 1)
        def _():
            right(r).start()

    def flow_left(r):
        at = part(y, r % 2)

        @pl.when(z == line - 1)
        def _():
            cin[r // 2, at, :] = hold[r].astype(BF16)

        @pl.when(z < line - 1)
        def _():
            left(r).wait_recv()
            cin[r // 2, at, :] = (hold[r] + fl[r].astype(F32)).astype(BF16)

        @pl.when(z > 0)
        def _():
            left(r).start()

    def ranged(r, do_it):
        pl.when((r >= 0) & (r < nchunk))(functools.partial(do_it, r))

    lag, skew = 5, 3
    flown = lag + skew * (line - 1)
    ticks = nchunk + flown

    def piece_total(j, h):
        r = 2 * j + h
        value = hold[r]
        value = value + jnp.where(z > 0, fr[r].astype(F32), 0.0)
        return value + jnp.where(z < line - 1, fl[r].astype(F32), 0.0)

    def deliver(s):
        return rcopy(do.at[s], di.at[s], dss.at[s], dsr.at[s], to_y)

    def settle(j):
        for h in range(2):
            value = piece_total(j, h)
            for s in range(cap):
                sg[s, part(y, h), :] = jnp.where(slot_pick[y * cap + s] == j, value, sg[s, part(y, h), :])

                @pl.when(j <= nmat - cap + s)
                def _():
                    at = pl.ds(h * half, half)
                    do[s, at, :] = jnp.where(far_pick[(1 - y) * cap + s] == j, value.astype(BF16), do[s, at, :])

        for s in range(cap):
            pl.when(j == nmat - cap + s)(lambda s=s: deliver(s).start())

    def tick(t):
        ranged(t, stage1)
        ranged(t - 4, stage2)
        ranged(t - lag - skew * z, flow_right)
        ranged(t - lag - skew * (line - 1 - z), flow_left)
        late = t - flown
        pl.when((late >= 0) & (late < nchunk) & (late % 2 == 1))(lambda: settle(late // 2))

    def ticking(start, stop):
        def body(t, carry):
            tick(t)
            return carry

        lax.fori_loop(start, stop, body, 0)

    gvec[...] = gvec_in[...]
    sg[...] = jnp.zeros_like(sg)
    do[...] = jnp.zeros_like(do)
    for copy in first_loads:
        copy.wait()
    lay_in.start()
    halves = pl.ds(pl.multiple_of(x * 2 * share, 128), 2 * share)

    def feed_back(k, carry):
        for copy in chunk_loads(k):
            copy.wait()

        @pl.when(k == 0)
        def _():
            for j in (3, 0, 1, 2):
                weight(j).start()
            lay_in.wait()
            lay_own.start()
            lay_own.wait()
            for copy in next_loads + late_loads:
                copy.start()

        d_up = (dg(df[...], full[5 + 2 * k], NT) * slope[k].astype(F32)).astype(BF16)
        gvec[pl.ds(3 + k, 1), :] = column_sum(d_up.astype(F32))
        acc[...] = acc[...] + dg(d_up, full[4 + 2 * k], NN)
        act_k = act[k, :, halves]
        act[k] = d_up
        full[5 + 2 * k, pl.ds(0, 2 * share), :] = dg(act_k, df[...], TN).astype(BF16)
        core_copy(2 * k, full.at[5 + 2 * k]).start()
        full[4 + 2 * k, pl.ds(0, 2 * share), :] = dg(act[k, :, halves], low[...], TN).astype(BF16)
        core_copy(2 * k + 1, full.at[4 + 2 * k]).start()
        tick(2 * k)
        tick(2 * k + 1)
        return carry

    lax.fori_loop(0, ratio, feed_back, 0)
    done = 2 * ratio
    weight(3).wait()
    for copy in next_loads:
        copy.wait()
    gvec[4 + ratio:5 + ratio, :] = column_sum(acc[...] * n1[...])
    gvec[5 + ratio:6 + ratio, :] = column_sum(acc[...])
    back = norm_back(acc[...], n1[...], inv1[:, 0:1], vecs[4 + ratio:5 + ratio, :])
    acc[...] = back
    da = back.astype(BF16)
    gvec[2:3, :] = column_sum(da.astype(F32))
    df[...] = da
    low[...] = dg(da, full[3], NT).astype(BF16)
    full[3, pl.ds(0, 2 * share), :] = dg(ctx[:, halves], da, TN).astype(BF16)
    core_copy(2 * ratio, full.at[3]).start()
    ticking(done, done + 2)
    done += 2

    for copy in late_loads:
        copy.wait()
    pairs = width // (2 * HDIM)
    left_half = lax.broadcasted_iota(jnp.int32, (SPAN_ROWS, 2 * HDIM), 1) < HDIM
    scale = HDIM ** -0.5

    def attend_back(i):
        s, pair = i // pairs, i % pairs
        at, span = rows(s * LEN, LEN), rows(s * SPAN_ROWS, SPAN_ROWS)
        lanes = pl.ds(pl.multiple_of(pair * (2 * HDIM), 2 * HDIM), 2 * HDIM)
        d_two = stacked(low[span, lanes], left_half)
        given = probs[i]
        value = given.astype(F32)
        keys = k_ref[at, lanes]
        d_probs = dg(d_two, v_ref[at, lanes], NT)
        mean = jnp.sum(value * d_probs, axis=-1, keepdims=True)
        ds = (value * (d_probs - mean)).astype(BF16)
        dq[span, lanes] = (merged(dg(ds, keys, NN), left_half) * scale).astype(BF16)
        k_ref[at, lanes] = (dg(ds, stacked(qm[span, lanes], left_half), TN) * scale).astype(BF16)
        v_ref[at, lanes] = dg(given, d_two, TN).astype(BF16)

    base_back = done

    def back_step(i, carry):
        for j in range(pairs // 2):
            attend_back(i * (pairs // 2) + j)
        tick(base_back + i)
        return carry

    lax.fori_loop(0, 2 * nseq, back_step, 0)
    done += 2 * nseq
    gvec[0:1, :] = column_sum(dq[...].astype(F32))
    gqkv[0] = dg(dq[:, halves], hm[...], TN).astype(BF16)
    core_copy(2 * ratio + 1, gqkv.at[0]).start()
    for which, src in ((1, k_ref), (2, v_ref)):
        def some(i, carry, src=src):
            at = rows(i * LEN, LEN)
            return carry + dg(src[at, halves], hid[at, :], TN)

        gqkv[which] = lax.fori_loop(0, nseq, some, jnp.zeros((2 * share, width), F32)).astype(BF16)
        core_copy(2 * ratio + 1 + which, gqkv.at[which]).start()
        stop = min(2 * (2 * ratio + 2 + which), done + 3)
        ticking(done, stop)
        done = stop

    def sum_v(i, carry):
        return carry + column_sum(v_ref[rows(i * LEN, LEN), :].astype(F32))

    gvec[1:2, :] = lax.fori_loop(0, nseq, sum_v, jnp.zeros((1, width), F32))

    def vec_copy(k, who_to):
        return rcopy(gvec, vin.at[k], vs.at[k], vr.at[k], who_to)

    vec_copy(0, to_c).start()
    for j in range(3):
        weight(j).wait()
    qm[...] = (acc[...] + dg(dq[...], full[0], NN)).astype(BF16)
    def gin_rows(s, core):
        return gin.at[rows((2 * (s // per) + core) * own_rows + (s % per) * LEN, LEN)]

    def gin_copy(s):
        return rcopy(hid.at[rows(s * LEN, LEN)], gin_rows(s, c), gsem_s.at[s], gsem_r.at[s], to_c)

    def gin_came(s):
        return rcopy(hid.at[rows(s * LEN, LEN)], gin_rows(s, 1 - c), gsem_s.at[s], gsem_r.at[s], to_c)

    def gin_own(s):
        return pltpu.make_async_copy(hid.at[rows(s * LEN, LEN)], gin_rows(s, c), loc_sem.at[1 + s])

    def vec_flow(step, send):
        def one(near, ok_send, ok_recv, direction, slot_out, slot_in):
            copy = rcopy(vz.at[slot_out], vz.at[slot_out], vzs.at[direction, step], vzr.at[slot_out], near)
            if send:
                pl.when(ok_send)(copy.start)
            else:
                came = rcopy(vz.at[slot_in], vz.at[slot_in], vzs.at[direction, step], vzr.at[slot_in], near)
                pl.when(ok_send)(copy.wait_send)
                pl.when(ok_recv)(came.wait_recv)

        one(device(jnp.minimum(z + 1, line - 1), y, x, c), (z < line - 1) & (z - step >= 0), z - step - 1 >= 0, 0,
            jnp.maximum(z - step, 0), jnp.maximum(z - step - 1, 0))
        one(device(jnp.maximum(z - 1, 0), y, x, c), (z > 0) & (z + step <= line - 1), z + step + 1 <= line - 1, 1,
            jnp.minimum(z + step, line - 1), jnp.minimum(z + step + 1, line - 1))

    def vec_step(i):
        if i == 0:
            vec_copy(0, to_c).wait()
            gvec[...] = gvec[...] + vin[0]
            vec_copy(1, to_y).start()
        elif i == 1:
            vec_copy(1, to_y).wait()
            vz[z] = gvec[...] + vin[1]
        if 2 <= i <= line:
            vec_flow(i - 2, False)
        if 1 <= i <= line - 1:
            vec_flow(i - 1, True)

    for s in range(nseq):
        at, span = pl.ds(s * LEN, LEN), pl.ds(s * SPAN_ROWS, SPAN_ROWS)
        total = dg(k_ref[at, :], full[1], NN) + dg(v_ref[at, :], full[2], NN) + dg(pick[s], qm[span, :], TN)
        hid[at, :] = total.astype(BF16)
        gin_copy(s).start()
        gin_own(s).start()
        vec_step(s)
        stop = min(ticks, done + 2)
        ticking(done, stop)
        done = stop
    lay_x_came.wait_recv()
    lay_d.start()
    for i in range(nseq, line + 1):
        vec_step(i)
        stop = min(ticks, done + 1)
        ticking(done, stop)
        done = stop
    ticking(done, ticks)
    total = vz[0]
    for k in range(1, line):
        total = total + vz[k]
    gvec[...] = total
    regroup(gvec, vec_out, ratio, share)


    def finish(r, carry):
        y_copy(r).wait_send()

        @pl.when(z < line - 1)
        def _():
            right(r).wait_send()

        @pl.when(z > 0)
        def _():
            left(r).wait_send()

        return carry

    lax.fori_loop(0, nchunk, finish, 0)

    def last(j, carry):
        core_copy(j, gqkv.at[0]).wait_send()
        return carry

    lax.fori_loop(0, nmat, last, 0)
    for s in range(nseq):
        gin_copy(s).wait_send()
        gin_came(s).wait_recv()
        gin_own(s).wait()
    lay_x.wait_send()
    lay_c.wait_send()
    lay_c_came.wait_recv()
    lay_d.wait_send()
    lay_d_came.wait_recv()
    for s in range(cap):
        deliver(s).wait()
    for s in range(cap):
        sg[s, rows((1 - y) * quarter, quarter), :] = di[far_at[y * cap + s]].astype(F32)


def backward(owners, vecs, saved, hidden, line, cap):
    flow, layer, *kept, gvec = saved
    nmat, width, _ = flow.shape
    share = width // 4
    nseq = 2 * layer.shape[0] // LEN
    span_rows = nseq * SPAN_ROWS
    quarter, half = share // 2, share // 4
    n = 2 * nmat
    dma = pltpu.SemaphoreType.DMA
    vmem = pl.BlockSpec(memory_space=pltpu.VMEM)
    smem = pl.BlockSpec(memory_space=pltpu.SMEM)
    hbm = pl.BlockSpec(memory_space=pl.ANY)
    whole = jax.ShapeDtypeStruct(hidden.shape, BF16)

    def lows(*shape):
        return pltpu.VMEM(shape, BF16)

    def wide(*shape):
        return pltpu.VMEM(shape, F32)

    k, v, pick, probs, hm, qm, ctx, low, act, slope, n1, inv1, df, dh = (
        pltpu.VMEM(value.shape, value.dtype) for value in kept)
    return pl.pallas_call(
        functools.partial(backward_kernel, line, nmat, cap),
        out_shape=(jax.ShapeDtypeStruct((cap, share, width), F32),
                   jax.ShapeDtypeStruct(vecs.shape, F32), whole, whole),
        in_specs=[smem, vmem, hbm, hbm] + [hbm] * (1 + len(kept)) + [vmem],
        out_specs=(vmem, vmem, hbm, hbm),
        scratch_shapes=[
            wide(*vecs.shape), lows(nmat, width, width), lows(2 * layer.shape[0], width), k, v, pick, probs, hm, qm, ctx, low,
            act, slope, n1, inv1, df, dh,
            lows(span_rows, width), lows(3, 2 * share, width),
            wide(*vecs.shape), wide(2, *vecs.shape), wide(line, *vecs.shape),
            lows(nmat, share, width), wide(n, half, width), lows(n, half, width), lows(n, half, width),
            lows(n, half, width), lows(cap, quarter, width), lows(cap, quarter, width),
            pltpu.SMEM((2 * cap,), jnp.int32), pltpu.SMEM((2 * cap,), jnp.int32), pltpu.SMEM((2 * cap,), jnp.int32),
            dma((nmat,)), dma((2, (nmat - 4) // 2)), dma((16,)), dma((3,)), dma((3,)), dma((nseq,)), dma((nseq,)), dma((2 + nseq,)),
            dma((nmat,)), dma((nmat,)),
        ] + [dma((n,))] * 6 + [dma((cap,)), dma((cap,)), dma((2,)), dma((2,)), dma((2, line)), dma((line,))],
        name="backward",
        compiler_params=pltpu.CompilerParams(
            collective_id=2, has_side_effects=True, vmem_limit_bytes=60 * 1024 * 1024),
    )(owners, vecs, flow, hidden, layer, *kept, gvec)


STEP = 10
MATRIX_RATE = 0.03
VECTOR_RATE = 0.25
BETA_ONE = 0.5
BETA_TWO = 0.5
DECAY = 0.01
ADAM_EPS = 1e-08


def adamw(weight, moment_one, moment_two, grad, step_rate):
    new_one = BETA_ONE * moment_one + (1.0 - BETA_ONE) * grad
    new_two = BETA_TWO * moment_two + (1.0 - BETA_TWO) * grad * grad
    corr_one = 1.0 - BETA_ONE**STEP
    corr_two = 1.0 - BETA_TWO**STEP
    direction = new_one / corr_one / (jnp.sqrt(new_two / corr_two) + ADAM_EPS)
    return (weight - step_rate * (direction + DECAY * weight), new_one, new_two)


def on_device(line, hidden_in, incoming, spans, owners, vectors, vec_one, vec_two, master_slots, slot_one, slot_two):
    cap, width, share = master_slots.shape
    nmat = owners.shape[0]
    saved = forward(
        owners, jnp.transpose(spans, (2, 0, 1)), jnp.transpose(master_slots, (0, 2, 1)), hidden_in, incoming, vectors, line)
    slot_grad, vec_grad, layer_out, input_grad = backward(owners, vectors, saved, hidden_in, line, cap)
    new_vec = adamw(vectors, vec_one, vec_two, vec_grad, VECTOR_RATE)
    slot_grad = jnp.transpose(slot_grad, (0, 2, 1))
    held = jnp.sum((owners == lax.axis_index("dp")).astype(jnp.int32))
    occupied = (jnp.arange(cap) < held).astype(F32)[:, None, None]
    new_slots = adamw(master_slots, slot_one, slot_two, slot_grad, MATRIX_RATE)
    return (layer_out, input_grad) + new_vec + tuple(v * occupied for v in new_slots)


def solution(mesh):
    line = mesh.shape["dp"] // 2
    rows, slots = P("dp", None), P("dp", None, "mp")
    return jax.shard_map(
        functools.partial(on_device, line),
        mesh=mesh,
        in_specs=(rows, rows, P("dp", None, None), P(), P(), P(), P(), slots, slots, slots),
        out_specs=(rows, rows, P(), P(), P(), slots, slots, slots),
        check_vma=False,
    )
```
